32 devices in a mesh: shard: 8 (over y, x, core), tile: 4 (over z).
Axes of the slice: x: 2, y: 2, z: 4, core: 2. Of those that a mesh axis runs over, the one named last changes fastest.
Arguments:
- embeddings: float32 [32768, 768], P(('shard', 'tile')), may hold values from -12 to 12
- cluster_ids: int32 [32768], P(('shard', 'tile')), may hold values from 0 to 127, as said below
Outputs:
- soft_max_sim: float32 [32768], P(('shard', 'tile'))
The draws below stay inside these ranges and needn't reach their ends.
Inputs may be any that keep to these rules, and one draw needn't show every extreme that they name: `cluster_ids`: cluster c is owned by group c // 16. Each device holds at most 256 rows of one group's clusters; in every draw, for each tile index, some group gets exactly 256 rows from every device of that tile index.
All inputs are finite; a program needn't handle non-finite values.
Results may differ from the reference program's by a relative error of at most 0.00053.
Values may be sent and summed in bfloat16 or wider, within the bound.
No kernel may reach another device: no remote copies, remote signals or barrier semaphores. Data moves between devices by JAX's collectives and lax.ppermute only.
A program may use at most 64 MiB of HBM per device.

```python
import math
import jax
import jax.numpy as jnp
from jax import lax

D = 768
ROW_DEV = 1024
KG = 16
CAP = 256
N_SHARD = 8
N_TILE = 4


def cluster_draw(key):
    devices = N_SHARD * N_TILE
    base_key = jax.random.fold_in(key, 11)
    first_key, second_key, third_key, fourth_key = jax.random.split(base_key, 4)
    full_owner = jax.random.randint(first_key, (N_TILE,), 0, N_SHARD)
    device_full = jnp.tile(full_owner, N_SHARD)
    slot_total = N_SHARD * CAP
    shuffled = jax.vmap(lambda single: jax.random.permutation(single, slot_total))(jax.random.split(second_key, devices))
    slot_owner = shuffled // CAP
    is_full = (slot_owner == device_full[:, None]).astype(jnp.int32)
    arranged = jnp.argsort(is_full, axis=1, stable=True)
    others = jnp.take_along_axis(slot_owner, arranged, axis=1)[:, :ROW_DEV - CAP]
    owners = jnp.concatenate([jnp.broadcast_to(device_full[:, None], (devices, CAP)), others], axis=1)
    mixing = jax.vmap(lambda single: jax.random.permutation(single, ROW_DEV))(jax.random.split(third_key, devices))
    owners = jnp.take_along_axis(owners, mixing, axis=1)
    local = jax.random.randint(fourth_key, (devices, ROW_DEV), 0, KG)
    return (owners * KG + local).reshape(devices * ROW_DEV).astype(jnp.int32)


def draw_cluster_ids(key, part):
    return cluster_draw(key)


def draw_embeddings(key, part):
    labels = cluster_draw(key)
    total = labels.shape[0]
    own_key = jax.random.fold_in(key, 23)
    coin_key = jax.random.fold_in(own_key, 0)
    base_key = jax.random.fold_in(own_key, 1)
    noise_key = jax.random.fold_in(own_key, 4)
    relative_key = jax.random.fold_in(own_key, 5)
    stretch_key = jax.random.fold_in(own_key, 6)
    order = jnp.argsort(labels, stable=True).astype(jnp.int32)
    position = jnp.arange(total, dtype=jnp.int32)
    sorted_labels = labels[order]
    previous_same = jnp.concatenate([jnp.zeros((1,), bool), sorted_labels[1:] == sorted_labels[:-1]])
    coin = jax.random.randint(coin_key, (total,), 0, 4) == 0
    copy_sorted = previous_same & (position % 2 == 1) & coin
    predecessor = order[jnp.maximum(position - 1, 0)]
    source_sorted = jnp.where(copy_sorted, predecessor, order)
    is_copy = jnp.zeros((total,), bool).at[order].set(copy_sorted)
    source = jnp.zeros((total,), jnp.int32).at[order].set(source_sorted)
    base = jax.random.truncated_normal(base_key, -6.0, 6.0, (total, D), jnp.float32)
    noise = jax.random.normal(noise_key, (total, D), jnp.float32)
    relative = jnp.exp(jax.random.uniform(relative_key, (total, 1), jnp.float32, math.log(0.03), math.log(0.5)))
    stretch = jnp.exp(jax.random.uniform(stretch_key, (total, 1), jnp.float32, math.log(0.5), math.log(2.0)))
    copied = stretch * (base[source] + relative * noise)
    result = jnp.where(is_copy[:, None], copied, base)
    return jnp.clip(result, -12.0, 12.0).astype(jnp.float32)


def setup_inputs(seed: int = 0) -> dict:
    key_list = jax.random.split(jax.random.key(seed), 3)
    embeddings = draw_embeddings(jax.random.fold_in(key_list[2], 71), 0)
    cluster_ids = draw_cluster_ids(jax.random.fold_in(key_list[2], 71), 0)
    return {"embeddings": embeddings, "cluster_ids": cluster_ids}


sharpness = 30.0
epsilon = 1e-06

def unit_rows(embeddings):
    energy = lax.optimization_barrier(jnp.sum(embeddings * embeddings, axis=1, keepdims=True))
    return (embeddings * lax.rsqrt(energy + epsilon)).astype(jnp.bfloat16)

def reference(embeddings, cluster_ids):
    unit = unit_rows(embeddings).astype(jnp.float32)
    total_rows = unit.shape[0]
    owner = cluster_ids // KG
    group_slots = 2 * ROW_DEV * N_TILE
    order = jnp.argsort(owner, stable=True).astype(jnp.int32)
    counts = lax.optimization_barrier(jnp.sum((owner[:, None] == jnp.arange(N_SHARD, dtype=jnp.int32)[None, :]).astype(jnp.int32), axis=0))
    starts = (jnp.cumsum(counts) - counts).astype(jnp.int32)
    block = min(1024, group_slots)

    def one_group(group):
        place = jnp.arange(group_slots, dtype=jnp.int32)
        valid = place < counts[group]
        members = order[jnp.where(valid, starts[group] + place, 0)]
        labels = jnp.where(valid, cluster_ids[members], -1)
        vectors = unit[members]

        def left_block(index):
            lower = (index * block).astype(jnp.int32)
            rows_block = lax.dynamic_slice_in_dim(vectors, lower, block)
            labels_block = lax.dynamic_slice_in_dim(labels, lower, block)
            place_block = lower + jnp.arange(block, dtype=jnp.int32)
            scores = jnp.dot(rows_block, vectors.T, preferred_element_type=jnp.float32, precision=lax.Precision.HIGHEST)
            same = (labels_block[:, None] == labels[None, :]) & (labels_block[:, None] >= 0)
            same = same & (place_block[:, None] != place[None, :])
            return lax.optimization_barrier(jnp.sum(jnp.where(same, jnp.exp(sharpness * scores), 0.0), axis=1))
        totals = lax.map(left_block, jnp.arange(group_slots // block, dtype=jnp.int32)).reshape(group_slots)
        targets = jnp.where(valid, members, total_rows)
        return (totals, targets)
    totals, targets = lax.map(one_group, jnp.arange(N_SHARD, dtype=jnp.int32))
    placed = jnp.zeros((total_rows,), jnp.float32).at[targets.reshape(-1)].set(totals.reshape(-1), mode='drop')
    return jnp.log(1.0 + placed)
```

```python
import functools

import jax
import jax.numpy as jnp
from jax import lax
from jax.experimental import pallas as pl
from jax.experimental.pallas import tpu as pltpu
from jax.sharding import Mesh
from jax.sharding import PartitionSpec as P

KG = 16


sharpness = 30.0
epsilon = 1e-06

VMEM_BYTES = 48 * 1024 * 1024
LANES = 128
FLAG = LANES - 1


def unit_rows(embeddings):
    energy = jnp.sum(embeddings * embeddings, axis=1, keepdims=True)
    return (embeddings * lax.rsqrt(energy + epsilon)).astype(jnp.bfloat16)


def pair_sums(left, left_labels, left_place, right, right_labels, right_place):
    count = left.shape[0]
    block = min(512, count)
    blocks = count // block

    def step(column_total, items):
        rows_block, labels_block, place_block = items
        scores = lax.dot_general(
            rows_block, right, (((1,), (1,)), ((), ())), preferred_element_type=jnp.float32
        )
        same = (labels_block[:, None] == right_labels[None, :]) & (labels_block[:, None] >= 0)
        same = same & (place_block[:, None] < right_place[None, :])
        terms = jnp.where(same, jnp.exp(sharpness * scores), 0.0)
        return (column_total + jnp.sum(terms, axis=0), jnp.sum(terms, axis=1))

    column_total, row_totals = lax.scan(
        step,
        jnp.zeros((right.shape[0],), jnp.float32),
        (
            left.reshape(blocks, block, left.shape[1]),
            left_labels.reshape(blocks, block),
            left_place.reshape(blocks, block),
        ),
    )
    return (row_totals.reshape(count), column_total)


def add_into(vector, start, values):
    current = lax.dynamic_slice_in_dim(vector, start, values.shape[0])
    return lax.dynamic_update_slice_in_dim(vector, current + values, start, 0)


def general_plan(embeddings, cluster_ids):
    shard_axes = ("chip", "core")
    local_rows = embeddings.shape[0]
    shards = lax.axis_size("chip") * lax.axis_size("core")
    tiles = lax.axis_size("tile")
    capacity = 2 * local_rows // shards
    slot_count = shards * capacity
    unit = unit_rows(embeddings)
    owner = cluster_ids // KG
    onehot = (owner[:, None] == jnp.arange(shards, dtype=jnp.int32)[None, :]).astype(jnp.int32)
    ranks = jnp.sum((jnp.cumsum(onehot, axis=0) - 1) * onehot, axis=1)
    slots = owner * capacity + ranks
    outgoing = jnp.zeros((slot_count, unit.shape[1]), jnp.bfloat16).at[slots].set(unit)
    outgoing_labels = jnp.full((slot_count,), -1, jnp.int32).at[slots].set(cluster_ids)
    owned = lax.all_to_all(outgoing, shard_axes, split_axis=0, concat_axis=0, tiled=True)
    owned_labels = lax.all_to_all(
        outgoing_labels, shard_axes, split_axis=0, concat_axis=0, tiled=True
    )
    own_start = lax.axis_index("tile") * slot_count
    own_place = own_start + jnp.arange(slot_count, dtype=jnp.int32)
    group_size = tiles * slot_count
    piece_rows = lax.all_gather(owned, "tile", axis=0, tiled=True)
    piece_labels = lax.all_gather(owned_labels, "tile", axis=0, tiled=True)
    piece_place = jnp.arange(group_size, dtype=jnp.int32)
    row_sum, column_sum = pair_sums(
        owned, owned_labels, own_place, piece_rows, piece_labels, piece_place
    )
    group_total = add_into(column_sum, own_start, row_sum)
    own_totals = lax.psum_scatter(
        group_total.astype(jnp.bfloat16), "tile", scatter_dimension=0, tiled=True
    ).astype(jnp.float32)
    returned = lax.all_to_all(own_totals, shard_axes, split_axis=0, concat_axis=0, tiled=True)
    return jnp.log(1.0 + returned[slots])


def up(value, multiple):
    return -(-value // multiple) * multiple


def exact_dot(left, right):
    return jnp.dot(
        left, right, precision=lax.Precision.HIGHEST, preferred_element_type=jnp.float32
    )


def iota(shape, axis):
    return lax.broadcasted_iota(jnp.int32, shape, axis)


def pack_kernel(chips, labels, cap, emb_ref, ids_ref, out_ref, rank_ref, aug_ref):
    rows, width = emb_ref.shape
    bits = chips.bit_length() - 1
    chunk = 256
    for start in range(0, rows, chunk):
        x = emb_ref[start : start + chunk, :]
        energy = jnp.sum(x * x, axis=1, keepdims=True)
        aug_ref[start : start + chunk, :] = (x * lax.rsqrt(energy + epsilon)).astype(jnp.bfloat16)

    ids = ids_ref[...]
    chip = ids & (chips - 1)
    label = ids >> bits
    key = ((chip * labels + label) * rows + iota((1, rows), 1)).astype(jnp.float32)
    base = (chip * (labels * rows)).astype(jnp.float32)
    key_t = jnp.broadcast_to(key, (LANES, rows)).T
    ranks = []
    for start in range(0, rows, LANES):
        own = key[:, start : start + LANES]
        low = base[:, start : start + LANES]
        before = (key_t < own) & (key_t >= low)
        ranks.append(jnp.sum(jnp.where(before, 1.0, 0.0), axis=0, keepdims=True))
    rank = jnp.concatenate(ranks, axis=1)
    rank_ref[...] = rank
    over = jnp.max(jnp.where(rank >= cap - 1, 1.0, 0.0), axis=1, keepdims=True)
    slot = jnp.where(rank < cap - 1, chip * cap + rank.astype(jnp.int32), -1)

    in_chip = jnp.where(iota((LANES, rows), 0) == chip, 1.0, 0.0).astype(jnp.bfloat16)
    in_label = jnp.where(iota((LANES, rows), 0) == label, 1.0, 0.0).astype(jnp.bfloat16)
    counts = lax.dot_general(
        in_chip, in_label, (((1,), (1,)), ((), ())), preferred_element_type=jnp.float32
    )
    counts = jnp.where(iota((LANES, LANES), 1) == FLAG, over, counts)
    aug_ref[rows:, :] = jnp.zeros((LANES, width), jnp.bfloat16)
    aug_ref[rows:, 0:LANES] = counts.astype(jnp.bfloat16)
    place = iota((1, LANES), 1)
    head = jnp.where(place < chips, place * cap + cap - 1, -1)
    slot = jnp.concatenate([slot, head], axis=1)

    total = chips * cap
    step = 16 * max(d for d in range(1, 17) if (total // 16) % d == 0)
    for start in range(0, total, step):
        pick = jnp.where(iota((step, rows + LANES), 0) + start == slot, 1.0, 0.0)
        out_ref[start : start + step, :] = jnp.dot(
            pick.astype(jnp.bfloat16), aug_ref[...], preferred_element_type=jnp.float32
        ).astype(jnp.bfloat16)


def sort_kernel(chips, labels, cap, rows_ref, out_ref, place_ref, ends_ref):
    total = rows_ref.shape[0]
    space = out_ref.shape[0]
    spot = iota((LANES, total), 1)
    block = iota((LANES, total), 0)
    head = jnp.where(spot == block * cap + cap - 1, 1.0, 0.0).astype(jnp.bfloat16)
    counts = jnp.dot(head, rows_ref[:, 0:LANES], preferred_element_type=jnp.float32)
    flag = jnp.max(counts[:, FLAG:], axis=0, keepdims=True)

    counts_t = counts.T
    lower = jnp.where(iota((LANES, LANES), 0) < iota((LANES, LANES), 1), 1.0, 0.0)
    ahead = exact_dot(counts_t, lower)
    in_block = jnp.zeros((1, LANES), jnp.float32)
    begin = jnp.zeros((1, 1), jnp.float32)
    ends = jnp.zeros((1, LANES), jnp.float32)
    lane = iota((1, LANES), 1)
    table = []
    for label in range(labels):
        own = counts_t[label : label + 1, :]
        table.append(begin + ahead[label : label + 1, :] - in_block)
        in_block = in_block + own
        table.append(in_block)
        begin = begin + jnp.sum(own, axis=1, keepdims=True)
        ends = jnp.where(lane == label, begin, ends)
    table.append((lane * cap).astype(jnp.float32))
    table.extend([jnp.zeros((1, LANES), jnp.float32)] * (up(len(table), 8) - len(table)))
    table = jnp.concatenate(table, axis=0)

    def positions(expand, rank_row):
        where = exact_dot(table, expand)
        rank = rank_row(where)
        place = jnp.full(rank.shape, -1.0, jnp.float32)
        for label in reversed(range(labels)):
            inside = rank < where[2 * label + 1 : 2 * label + 2, :]
            place = jnp.where(inside, where[2 * label : 2 * label + 1, :] + rank, place)
        return place

    spot_block = jnp.where((spot >= block * cap) & (spot < block * cap + cap), 1.0, 0.0)
    spot_row = iota((1, total), 1).astype(jnp.float32)
    place = positions(
        spot_block, lambda where: spot_row - where[2 * labels : 2 * labels + 1, :]
    ).astype(jnp.int32)

    lanes = place_ref.shape[1]
    rank_row = iota((1, lanes), 1).astype(jnp.float32)
    for index in range(chips):
        only = jnp.where(iota((LANES, lanes), 0) == index, 1.0, 0.0)
        place_ref[index : index + 1, :] = positions(only, lambda where: rank_row).astype(jnp.int32)

    flag = jnp.maximum(flag, jnp.where(begin > space, 1.0, 0.0))
    ends = jnp.where(lane == FLAG, flag, ends)
    ends_ref[...] = jnp.broadcast_to(ends, ends_ref.shape).astype(jnp.int32)

    step = 256
    for start in range(0, space, step):
        pick = jnp.where(iota((step, total), 0) + start == place, 1.0, 0.0)
        out_ref[start : start + step, :] = jnp.dot(
            pick.astype(jnp.bfloat16), rows_ref[...], preferred_element_type=jnp.float32
        ).astype(jnp.bfloat16)


def score_kernel(labels, own_ends, other_ends, own_ref, other_ref, place_ref, out_ref, total_ref):
    space = own_ref.shape[0]
    tile = LANES

    def clamp(value):
        return jnp.clip(value, 0, space)

    def label_of(ends, place):
        found = jnp.zeros(place.shape, jnp.int32)
        for label in range(labels):
            found = found + jnp.where(place >= ends[0, label], 1, 0)
        return found

    def first_label(ends, place):
        found = jnp.int32(0)
        for label in range(labels):
            found = found + jnp.where(place >= ends[0, label], 1, 0)
        return found

    def begin_of(ends, label):
        return jnp.where(label > 0, ends[0, jnp.maximum(label - 1, 0)], 0)

    count = clamp(own_ends[0, labels - 1])

    def row_tile(index, carry):
        start = pl.multiple_of(index * tile, tile)
        left = own_ref[pl.ds(start, tile), :]
        left_place = start + iota((tile, tile), 0)
        left_label = label_of(own_ends, left_place)
        low = first_label(own_ends, start)
        high = first_label(own_ends, jnp.minimum(start + tile, count) - 1)
        low = jnp.minimum(low, labels - 1)
        high = jnp.minimum(high, labels - 1)

        def side(ends, right_ref, same_rows, acc):
            begin = clamp(begin_of(ends, low)) // tile
            end = (clamp(ends[0, high]) + tile - 1) // tile

            def column_tile(position, acc):
                offset = pl.multiple_of(position * tile, tile)
                right = right_ref[pl.ds(offset, tile), :]
                scores = lax.dot_general(
                    left, right, (((1,), (1,)), ((), ())), preferred_element_type=jnp.float32
                )
                right_place = offset + iota((1, tile), 1)
                right_label = label_of(ends, right_place)
                right_label = jnp.where(right_label < labels, right_label, -1)
                same = left_label == right_label
                if same_rows:
                    same = same & (left_place != right_place)
                return acc + jnp.where(same, jnp.exp(sharpness * scores), 0.0)

            return lax.fori_loop(begin, end, column_tile, acc)

        acc = jnp.zeros((tile, tile), jnp.float32)
        acc = side(own_ends, own_ref, True, acc)
        acc = side(other_ends, other_ref, False, acc)
        sums = jnp.sum(acc, axis=1, keepdims=True)
        total_ref[pl.ds(start, tile), :] = jnp.broadcast_to(sums, (tile, tile))
        return carry

    total_ref[...] = jnp.zeros(total_ref.shape, jnp.float32)
    lax.fori_loop(0, (count + tile - 1) // tile, row_tile, 0)

    flag = jnp.maximum(own_ends[0, FLAG], other_ends[0, FLAG]).astype(jnp.float32)
    lanes = out_ref.shape[1]
    row = iota((space, LANES), 0)
    for index in range(out_ref.shape[0]):
        for start in range(0, lanes, LANES):
            place = place_ref[index : index + 1, start : start + LANES]
            value = jnp.sum(
                jnp.where(row == place, total_ref[...], 0.0), axis=0, keepdims=True
            )
            if start + LANES == lanes:
                value = jnp.where(iota((1, LANES), 1) == FLAG, flag, value)
            out_ref[index : index + 1, start : start + LANES] = value


def unpack_kernel(chips, ret_ref, ids_ref, rank_ref, out_ref, flag_ref):
    rows = ids_ref.shape[1]
    lanes = ret_ref.shape[1]
    values = ret_ref[...]
    flag = jnp.max(values[:, lanes - 1 :], axis=0, keepdims=True)
    flag_ref[...] = jnp.broadcast_to(flag, flag_ref.shape).astype(jnp.int32)
    chip = ids_ref[...] & (chips - 1)
    rank = rank_ref[...].astype(jnp.int32)
    at_rank = jnp.where(iota((lanes, rows), 0) == rank, 1.0, 0.0)
    found = exact_dot(values, at_rank)
    total = jnp.sum(jnp.where(iota((chips, rows), 0) == chip, found, 0.0), axis=0, keepdims=True)
    out_ref[...] = jnp.log(1.0 + total)


def call(kernel, out_shape, **options):
    return pl.pallas_call(
        kernel,
        out_shape=out_shape,
        compiler_params=pltpu.CompilerParams(vmem_limit_bytes=VMEM_BYTES),
        **options,
    )


def body(embeddings, cluster_ids):
    rows, width = embeddings.shape
    chip_axes = ("chip", "tile")
    chips = lax.axis_size("chip") * lax.axis_size("tile")
    labels = KG * lax.axis_size("chip") * lax.axis_size("core") // chips
    mean = rows // chips
    cap = up(int(mean + 4.75 * mean**0.5) + 1, 8)
    lanes = up(cap + 1, LANES)
    space = rows + 256
    total = chips * cap
    vmem = pl.BlockSpec(memory_space=pltpu.VMEM)
    smem = pl.BlockSpec(memory_space=pltpu.SMEM)
    shape = jax.ShapeDtypeStruct

    ids_row = cluster_ids.reshape(1, rows)
    outgoing, rank = call(
        functools.partial(pack_kernel, chips, labels, cap),
        (shape((total, width), jnp.bfloat16), shape((1, rows), jnp.float32)),
        in_specs=[vmem, vmem],
        out_specs=(vmem, vmem),
        scratch_shapes=[pltpu.VMEM((rows + LANES, width), jnp.bfloat16)],
    )(embeddings, ids_row)
    arrived = lax.all_to_all(outgoing, chip_axes, split_axis=0, concat_axis=0, tiled=True)
    ordered, place, ends = call(
        functools.partial(sort_kernel, chips, labels, cap),
        (
            shape((space, width), jnp.bfloat16),
            shape((chips, lanes), jnp.int32),
            shape((8, LANES), jnp.int32),
        ),
        in_specs=[vmem],
        out_specs=(vmem, vmem, vmem),
    )(arrived)
    swap = [(0, 1), (1, 0)]
    other_ends = lax.ppermute(ends, "core", swap)
    other = lax.ppermute(ordered, "core", swap)
    totals = call(
        functools.partial(score_kernel, labels),
        shape((chips, lanes), jnp.float32),
        in_specs=[smem, smem, vmem, vmem, vmem],
        out_specs=vmem,
        scratch_shapes=[pltpu.VMEM((space, LANES), jnp.float32)],
    )(ends, other_ends, ordered, other, place)
    returned = lax.all_to_all(totals, chip_axes, split_axis=0, concat_axis=0, tiled=True)
    result, flag = call(
        functools.partial(unpack_kernel, chips),
        (shape((1, rows), jnp.float32), shape((8, LANES), jnp.int32)),
        in_specs=[vmem, vmem, vmem],
        out_specs=(vmem, vmem),
    )(returned, ids_row, rank)
    return lax.cond(
        flag[0, 0] > 0,
        lambda: general_plan(embeddings, cluster_ids),
        lambda: result.reshape(rows),
    )


def solution(mesh):
    shards = mesh.shape["shard"]
    tiles = mesh.shape["tile"]
    split = Mesh(mesh.devices.reshape(shards // 2, 2, tiles), ("chip", "core", "tile"))
    rows = ("chip", "core", "tile")
    return jax.shard_map(
        body, mesh=split, in_specs=(P(rows, None), P(rows)), out_specs=P(rows), check_vma=False
    )
```

```python
import functools

import jax
import jax.numpy as jnp
from jax import lax
from jax.experimental import pallas as pl
from jax.experimental.pallas import tpu as pltpu
from jax.sharding import Mesh
from jax.sharding import PartitionSpec as P

KG = 16


sharpness = 30.0
epsilon = 1e-06

VMEM_BYTES = 48 * 1024 * 1024
LANES = 128
FLAG = LANES - 1
ALIGN = 16
STEP = 32
LEFT = 192
RIGHT = 384


def unit_rows(embeddings):
    energy = jnp.sum(embeddings * embeddings, axis=1, keepdims=True)
    return (embeddings * lax.rsqrt(energy + epsilon)).astype(jnp.bfloat16)


def row_sums(left, left_labels, right, right_labels, same_rows):
    count = left.shape[0]
    block = min(512, count)
    blocks = count // block

    def step(start, items):
        rows_block, labels_block = items
        scores = lax.dot_general(
            rows_block, right, (((1,), (1,)), ((), ())), preferred_element_type=jnp.float32
        )
        same = (labels_block[:, None] == right_labels[None, :]) & (labels_block[:, None] >= 0)
        itself = (start + jnp.arange(block))[:, None] == jnp.arange(count)[None, :]
        same = same & ~(itself & same_rows)
        terms = jnp.where(same, jnp.exp(sharpness * scores), 0.0)
        return (start + block, jnp.sum(terms, axis=1))

    _, totals = lax.scan(
        step,
        jnp.int32(0),
        (left.reshape(blocks, block, left.shape[1]), left_labels.reshape(blocks, block)),
    )
    return totals.reshape(count)


def general_plan(embeddings, cluster_ids):
    shard_axes = ("chip", "core")
    local_rows = embeddings.shape[0]
    shards = lax.axis_size("chip") * lax.axis_size("core")
    tiles = lax.axis_size("tile")
    capacity = 2 * local_rows // shards
    slot_count = shards * capacity
    unit = unit_rows(embeddings)
    owner = cluster_ids // KG
    onehot = (owner[:, None] == jnp.arange(shards, dtype=jnp.int32)[None, :]).astype(jnp.int32)
    ranks = jnp.sum((jnp.cumsum(onehot, axis=0) - 1) * onehot, axis=1)
    slots = owner * capacity + ranks
    outgoing = jnp.zeros((slot_count, unit.shape[1]), jnp.bfloat16).at[slots].set(unit)
    outgoing_labels = jnp.full((slot_count,), -1, jnp.int32).at[slots].set(cluster_ids)
    owned = lax.all_to_all(outgoing, shard_axes, split_axis=0, concat_axis=0, tiled=True)
    owned_labels = lax.all_to_all(
        outgoing_labels, shard_axes, split_axis=0, concat_axis=0, tiled=True
    )
    around = [(tile, (tile + 1) % tiles) for tile in range(tiles)]

    def visit(step, state):
        totals, rows, labels = state
        totals = totals + row_sums(owned, owned_labels, rows, labels, step == 0)
        return (totals, lax.ppermute(rows, "tile", around), lax.ppermute(labels, "tile", around))

    totals, _, _ = lax.fori_loop(
        0, tiles, visit, (jnp.zeros((slot_count,), jnp.float32), owned, owned_labels)
    )
    returned = lax.all_to_all(totals, shard_axes, split_axis=0, concat_axis=0, tiled=True)
    return jnp.log(1.0 + returned[slots])


def up(value, multiple):
    return -(-value // multiple) * multiple


def room(mean):
    return int(mean + 4.75 * mean**0.5) + 1


def iota(shape, axis):
    return lax.broadcasted_iota(jnp.int32, shape, axis)


def exact_dot(left, right):
    return jnp.dot(
        left, right, precision=lax.Precision.HIGHEST, preferred_element_type=jnp.float32
    )


def pick_rows(places, start, count, rows):
    pick = jnp.where(iota((count, places.shape[1]), 0) + start == places, 1.0, 0.0)
    return jnp.dot(pick.astype(jnp.bfloat16), rows, preferred_element_type=jnp.float32).astype(
        jnp.bfloat16
    )


def pack_kernel(size, emb_ref, ids_ref, *refs):
    *out_refs, rank_ref, aug_ref = refs
    rows, width = emb_ref.shape
    chips, labels, cap = size["chips"], size["labels"], size["cap"]
    across, tiles = size["across"], size["tiles"]
    chunk = 256
    for start in range(0, rows, chunk):
        x = emb_ref[start : start + chunk, :]
        energy = jnp.sum(x * x, axis=1, keepdims=True)
        aug_ref[start : start + chunk, :] = (x * lax.rsqrt(energy + epsilon)).astype(jnp.bfloat16)

    ids = ids_ref[...]
    label = ids >> (chips.bit_length() - 1)
    shift = ((ids & (tiles - 1)) - lax.axis_index("tile")) & (tiles - 1)
    side = ((ids & (chips - 1)) >> (tiles.bit_length() - 1)) ^ lax.axis_index("chip")
    block = shift * across + side
    key = ((block * labels + label) * rows + iota((1, rows), 1)).astype(jnp.float32)
    base = (block * (labels * rows)).astype(jnp.float32)
    key_t = jnp.broadcast_to(key, (LANES, rows)).T
    ranks = []
    for start in range(0, rows, LANES):
        own = key[:, start : start + LANES]
        low = base[:, start : start + LANES]
        before = (key_t < own) & (key_t >= low)
        ranks.append(jnp.sum(jnp.where(before, 1.0, 0.0), axis=0, keepdims=True))
    rank = jnp.concatenate(ranks, axis=1)
    rank_ref[...] = rank
    over = jnp.max(jnp.where(rank >= cap - 1, 1.0, 0.0), axis=1, keepdims=True)
    slot = jnp.where(rank < cap - 1, block * cap + rank.astype(jnp.int32), -1)

    in_block = jnp.where(iota((LANES, rows), 0) == block, 1.0, 0.0).astype(jnp.bfloat16)
    in_label = jnp.where(iota((LANES, rows), 0) == label, 1.0, 0.0).astype(jnp.bfloat16)
    counts = lax.dot_general(
        in_block, in_label, (((1,), (1,)), ((), ())), preferred_element_type=jnp.float32
    )
    counts = jnp.where(iota((LANES, LANES), 1) == FLAG, over, counts)
    aug_ref[rows:, :] = jnp.zeros((LANES, width), jnp.bfloat16)
    aug_ref[rows:, 0:LANES] = counts.astype(jnp.bfloat16)
    place = iota((1, LANES), 1)
    head = jnp.where(place < chips, place * cap + cap - 1, -1)
    slot = jnp.concatenate([slot, head], axis=1)
    aug = aug_ref[...]
    for index, out_ref in enumerate(out_refs):
        out_ref[...] = pick_rows(slot, index * cap, cap, aug)


def sort_kernel(size, *refs):
    across, labels, cap, space = size["across"], size["labels"], size["cap"], size["space"]
    block_refs, (out_ref, place_ref, counts_ref, rows_ref) = refs[:across], refs[across:]
    total = across * cap
    for index, ref in enumerate(block_refs):
        rows_ref[index * cap : (index + 1) * cap, :] = ref[...]
    rows = rows_ref[...]
    spot = iota((LANES, total), 1)
    block = iota((LANES, total), 0)
    head = jnp.where(spot == block * cap + cap - 1, 1.0, 0.0).astype(jnp.bfloat16)
    counts = jnp.dot(head, rows[:, 0:LANES], preferred_element_type=jnp.float32)
    flag = jnp.max(counts[:, FLAG:], axis=0, keepdims=True)

    counts_t = counts.T
    lower = jnp.where(iota((LANES, LANES), 0) < iota((LANES, LANES), 1), 1.0, 0.0)
    ahead = exact_dot(counts_t, lower)
    in_block = jnp.zeros((1, LANES), jnp.float32)
    found = jnp.zeros((1, LANES), jnp.float32)
    begin = jnp.zeros((1, 1), jnp.float32)
    lane = iota((1, LANES), 1)
    table = []
    for label in range(labels):
        own = counts_t[label : label + 1, :]
        table.append(begin + ahead[label : label + 1, :] - in_block)
        in_block = in_block + own
        table.append(in_block)
        count = jnp.sum(own, axis=1, keepdims=True)
        found = jnp.where(lane == label, count, found)
        begin = begin + jnp.floor((count + (ALIGN - 1)) * (1.0 / ALIGN)) * ALIGN
    flag = jnp.maximum(flag, jnp.where(begin > space, 1.0, 0.0))
    found = jnp.where(lane == FLAG, flag, found)
    counts_ref[...] = jnp.broadcast_to(found, counts_ref.shape).astype(jnp.int32)
    table.append((lane * cap).astype(jnp.float32))
    table.extend([jnp.zeros((1, LANES), jnp.float32)] * (up(len(table), 8) - len(table)))
    table = jnp.concatenate(table, axis=0)

    def places(expand, rank_row):
        where = exact_dot(table, expand)
        rank = rank_row(where)
        place = jnp.full(rank.shape, -1.0, jnp.float32)
        for label in reversed(range(labels)):
            inside = rank < where[2 * label + 1 : 2 * label + 2, :]
            place = jnp.where(inside, where[2 * label : 2 * label + 1, :] + rank, place)
        return place.astype(jnp.int32)

    spot_block = jnp.where((spot >= block * cap) & (spot < block * cap + cap), 1.0, 0.0)
    spot_row = iota((1, total), 1).astype(jnp.float32)
    place = places(spot_block, lambda where: spot_row - where[2 * labels : 2 * labels + 1, :])
    lanes = place_ref.shape[1]
    rank_row = iota((1, lanes), 1).astype(jnp.float32)
    for index in range(across):
        only = jnp.where(iota((LANES, lanes), 0) == index, 1.0, 0.0)
        place_ref[index : index + 1, :] = places(only, lambda where: rank_row)

    out_ref[space:, :] = jnp.zeros((STEP, out_ref.shape[1]), jnp.bfloat16)
    for start in range(0, space, ALIGN * 9):
        count = min(ALIGN * 9, space - start)
        out_ref[start : start + count, :] = pick_rows(place, start, count, rows)


def score_kernel(size, *refs):
    across, tiles, labels, space = size["across"], size["tiles"], size["labels"], size["space"]
    pieces = 2 * tiles
    counts_refs, piece_refs, place_refs = (
        refs[:pieces],
        refs[pieces : 2 * pieces],
        refs[2 * pieces : 2 * pieces + tiles],
    )
    out_ref, rows_ref, total_ref, back_ref = refs[2 * pieces + tiles :]
    lane = iota((1, LANES), 1)
    flag = jnp.int32(0)
    for ref in counts_refs:
        flag = jnp.maximum(flag, ref[0, FLAG])

    def aligned(count):
        return (count + (ALIGN - 1)) & -ALIGN

    counts, places, begins = [], [], []
    begin = jnp.int32(0)
    source = [jnp.int32(0)] * pieces
    for label in range(labels):
        begins.append(begin)
        counts.append([])
        places.append([])
        for index in range(pieces):
            free = space - source[index]
            count = jnp.clip(counts_refs[index][0, label], 0, free)
            counts[label].append(count)
            places[label].append((source[index], begin))
            src, dst = source[index], begin

            def move(step, carry, ref=piece_refs[index], src=src, dst=dst):
                rows = pl.ds(pl.multiple_of(src + step * STEP, ALIGN), STEP)
                to = pl.ds(pl.multiple_of(dst + step * STEP, ALIGN), STEP)
                rows_ref[to, :] = ref[rows, :]
                return carry

            move(0, 0)
            lax.fori_loop(1, (count + STEP - 1) // STEP, move, 0)
            source[index] = source[index] + aligned(count)
            begin = begin + aligned(count)

    for label in range(labels):
        first = begins[label]
        own_end = places[label][tiles][1]
        end = begins[label + 1] if label + 1 < labels else begin

        def window(row, column, label=label):
            left = rows_ref[pl.ds(pl.multiple_of(row, ALIGN), LEFT), :]
            right = rows_ref[pl.ds(pl.multiple_of(column, ALIGN), RIGHT), :]
            scores = lax.dot_general(
                left, right, (((1,), (1,)), ((), ())), preferred_element_type=jnp.float32
            )
            at = iota((1, RIGHT), 1) + column
            valid = at < 0
            for index in range(pieces):
                low = places[label][index][1]
                valid = valid | ((at >= low) & (at < low + counts[label][index]))
            at = jnp.where(valid, at, -1)
            itself = iota((LEFT, RIGHT), 0) + row
            counted = (at >= 0) & (at != itself)
            terms = jnp.where(counted, jnp.exp(sharpness * scores), 0.0)
            return jnp.sum(terms, axis=1, keepdims=True)

        def strip(row, first=first, end=end, window=window):
            sums = window(row, first)
            sums = lax.fori_loop(
                1,
                (end - first + RIGHT - 1) // RIGHT,
                lambda step, sums: sums + window(row, first + step * RIGHT),
                sums,
            )
            total_ref[pl.ds(pl.multiple_of(row, ALIGN), LEFT), :] = jnp.broadcast_to(
                sums, (LEFT, LANES)
            )

        def more(step, carry, first=first, strip=strip):
            strip(first + step * LEFT)
            return carry

        strip(first)
        lax.fori_loop(1, (own_end - first + LEFT - 1) // LEFT, more, 0)

    for index in range(tiles):
        for label in range(labels):
            src, dst = places[label][index][1], places[label][index][0]

            def back(step, carry, index=index, src=src, dst=dst):
                rows = pl.ds(pl.multiple_of(src + step * STEP, ALIGN), STEP)
                to = pl.ds(pl.multiple_of(dst + step * STEP, ALIGN), STEP)
                back_ref[index, to, :] = total_ref[rows, :]
                return carry

            back(0, 0)
            lax.fori_loop(1, (counts[label][index] + STEP - 1) // STEP, back, 0)

    lanes = out_ref.shape[1]
    row = iota((space, LANES), 0)
    chip, tile = lax.axis_index("chip"), lax.axis_index("tile")
    for shift in range(tiles):
        for side in range(across):
            home = (chip ^ side) * tiles + ((tile - shift) & (tiles - 1))
            for start in range(0, lanes, LANES):
                place = place_refs[shift][side : side + 1, start : start + LANES]
                value = jnp.sum(
                    jnp.where(row == place, back_ref[shift, 0:space, :], 0.0),
                    axis=0,
                    keepdims=True,
                )
                if start + LANES == lanes:
                    value = jnp.where(lane == FLAG, flag.astype(jnp.float32), value)
                out_ref[pl.ds(home, 1), start : start + LANES] = value


def unpack_kernel(chips, ret_ref, ids_ref, rank_ref, out_ref, flag_ref):
    rows = ids_ref.shape[1]
    lanes = ret_ref.shape[1]
    values = ret_ref[...]
    flag = jnp.max(values[:, lanes - 1 :], axis=0, keepdims=True)
    flag_ref[...] = jnp.broadcast_to(flag, flag_ref.shape).astype(jnp.int32)
    chip = ids_ref[...] & (chips - 1)
    rank = rank_ref[...].astype(jnp.int32)
    at_rank = jnp.where(iota((lanes, rows), 0) == rank, 1.0, 0.0)
    found = exact_dot(values, at_rank)
    total = jnp.sum(jnp.where(iota((chips, rows), 0) == chip, found, 0.0), axis=0, keepdims=True)
    out_ref[...] = jnp.log(1.0 + total)


def call(kernel, name, out_shape, inputs, scalars=0, **options):
    vmem = pl.BlockSpec(memory_space=pltpu.VMEM)
    smem = pl.BlockSpec(memory_space=pltpu.SMEM)
    return pl.pallas_call(
        kernel,
        out_shape=out_shape,
        in_specs=[smem] * scalars + [vmem] * (len(inputs) - scalars),
        out_specs=jax.tree.map(lambda _: vmem, out_shape),
        compiler_params=pltpu.CompilerParams(vmem_limit_bytes=VMEM_BYTES),
        name=name,
        **options,
    )(*inputs)


def body(embeddings, cluster_ids):
    rows, width = embeddings.shape
    across, tiles = lax.axis_size("chip"), lax.axis_size("tile")
    chips = across * tiles
    labels = KG * across * lax.axis_size("core") // chips
    cap = up(room(rows // chips) + 1, ALIGN)
    batch = rows // tiles
    space = up(room(batch) + labels * (ALIGN - 1) - labels * ALIGN // 4, ALIGN)
    size = dict(chips=chips, across=across, tiles=tiles, labels=labels, cap=cap, space=space)
    lanes = up(cap + 1, LANES)
    shape = jax.ShapeDtypeStruct

    ids_row = cluster_ids.reshape(1, rows)
    *blocks, rank = call(
        functools.partial(pack_kernel, size),
        "pack",
        [shape((cap, width), jnp.bfloat16)] * chips + [shape((1, rows), jnp.float32)],
        [embeddings, ids_row],
        scratch_shapes=[pltpu.VMEM((rows + LANES, width), jnp.bfloat16)],
    )
    own, other, own_counts, other_counts, places = [], [], [], [], []
    swap = [(0, 1), (1, 0)]
    for shift in range(tiles):
        arrived = []
        for side in range(across):
            block = blocks[shift * across + side]
            if shift or side:
                route = [
                    (a * tiles + z, (a ^ side) * tiles + (z + shift) % tiles)
                    for a in range(across)
                    for z in range(tiles)
                ]
                block = lax.ppermute(block, ("chip", "tile"), route)
            arrived.append(block)
        ordered, place, counts = call(
            functools.partial(sort_kernel, size),
            "sort",
            [
                shape((space + STEP, width), jnp.bfloat16),
                shape((across, lanes), jnp.int32),
                shape((8, LANES), jnp.int32),
            ],
            arrived,
            scratch_shapes=[pltpu.VMEM((across * cap, width), jnp.bfloat16)],
        )
        own.append(ordered)
        places.append(place)
        own_counts.append(counts)
        other_counts.append(lax.ppermute(counts, "core", swap))
        other.append(lax.ppermute(ordered, "core", swap))
    room_all = 2 * tiles * space + RIGHT
    totals = call(
        functools.partial(score_kernel, size),
        "score",
        shape((chips, lanes), jnp.float32),
        [*own_counts, *other_counts, *own, *other, *places],
        scalars=2 * tiles,
        scratch_shapes=[
            pltpu.VMEM((room_all, width), jnp.bfloat16),
            pltpu.VMEM((room_all, LANES), jnp.float32),
            pltpu.VMEM((tiles, space + STEP, LANES), jnp.float32),
        ],
    )
    returned = lax.all_to_all(totals, ("chip", "tile"), split_axis=0, concat_axis=0, tiled=True)
    result, flag = call(
        functools.partial(unpack_kernel, chips),
        "unpack",
        [shape((1, rows), jnp.float32), shape((8, LANES), jnp.int32)],
        [returned, ids_row, rank],
    )
    return lax.cond(
        flag[0, 0] > 0,
        lambda: general_plan(embeddings, cluster_ids),
        lambda: result.reshape(rows),
    )


def solution(mesh):
    shards = mesh.shape["shard"]
    tiles = mesh.shape["tile"]
    split = Mesh(mesh.devices.reshape(shards // 2, 2, tiles), ("chip", "core", "tile"))
    rows = ("chip", "core", "tile")
    return jax.shard_map(
        body, mesh=split, in_specs=(P(rows, None), P(rows)), out_specs=P(rows), check_vma=False
    )
```

```python
import functools
import math

import jax
import jax.numpy as jnp
from jax import lax
from jax.experimental import pallas as pl
from jax.experimental.pallas import tpu as pltpu
from jax.sharding import Mesh
from jax.sharding import PartitionSpec as P

KG = 16


sharpness = 30.0
epsilon = 1e-06

VMEM_BYTES = 48 * 1024 * 1024
LANES = 128
FLAG = LANES - 1
ALIGN = 16
STEP = 32
LEFT = 192
RIGHT = 384


def unit_rows(embeddings):
    energy = jnp.sum(embeddings * embeddings, axis=1, keepdims=True)
    return (embeddings * lax.rsqrt(energy + epsilon)).astype(jnp.bfloat16)


def row_sums(left, left_labels, right, right_labels, same_rows):
    count = left.shape[0]
    block = min(512, count)
    blocks = count // block

    def step(start, items):
        rows_block, labels_block = items
        scores = lax.dot_general(
            rows_block, right, (((1,), (1,)), ((), ())), preferred_element_type=jnp.float32
        )
        same = (labels_block[:, None] == right_labels[None, :]) & (labels_block[:, None] >= 0)
        itself = (start + jnp.arange(block))[:, None] == jnp.arange(count)[None, :]
        same = same & ~(itself & same_rows)
        terms = jnp.where(same, jnp.exp(sharpness * scores), 0.0)
        return (start + block, jnp.sum(terms, axis=1))

    _, totals = lax.scan(
        step,
        jnp.int32(0),
        (left.reshape(blocks, block, left.shape[1]), left_labels.reshape(blocks, block)),
    )
    return totals.reshape(count)


def general_plan(embeddings, cluster_ids):
    shard_axes = ("chip", "core")
    local_rows = embeddings.shape[0]
    shards = lax.axis_size("chip") * lax.axis_size("core")
    tiles = lax.axis_size("tile")
    capacity = 2 * local_rows // shards
    slot_count = shards * capacity
    unit = unit_rows(embeddings)
    owner = cluster_ids // KG
    onehot = (owner[:, None] == jnp.arange(shards, dtype=jnp.int32)[None, :]).astype(jnp.int32)
    ranks = jnp.sum((jnp.cumsum(onehot, axis=0) - 1) * onehot, axis=1)
    slots = owner * capacity + ranks
    outgoing = jnp.zeros((slot_count, unit.shape[1]), jnp.bfloat16).at[slots].set(unit)
    outgoing_labels = jnp.full((slot_count,), -1, jnp.int32).at[slots].set(cluster_ids)
    owned = lax.all_to_all(outgoing, shard_axes, split_axis=0, concat_axis=0, tiled=True)
    owned_labels = lax.all_to_all(
        outgoing_labels, shard_axes, split_axis=0, concat_axis=0, tiled=True
    )
    around = [(tile, (tile + 1) % tiles) for tile in range(tiles)]

    def visit(step, state):
        totals, rows, labels = state
        totals = totals + row_sums(owned, owned_labels, rows, labels, step == 0)
        return (totals, lax.ppermute(rows, "tile", around), lax.ppermute(labels, "tile", around))

    totals, _, _ = lax.fori_loop(
        0, tiles, visit, (jnp.zeros((slot_count,), jnp.float32), owned, owned_labels)
    )
    returned = lax.all_to_all(totals, shard_axes, split_axis=0, concat_axis=0, tiled=True)
    return jnp.log(1.0 + returned[slots])


def up(value, multiple):
    return -(-value // multiple) * multiple


def room(count, parts, sigmas):
    mean = count / parts
    return math.ceil(mean + sigmas * (mean * (1 - 1 / parts)) ** 0.5)


def iota(shape, axis):
    return lax.broadcasted_iota(jnp.int32, shape, axis)


def exact_dot(left, right):
    return jnp.dot(
        left, right, precision=lax.Precision.HIGHEST, preferred_element_type=jnp.float32
    )


def pick_rows(places, start, count, rows):
    pick = jnp.where(iota((count, places.shape[1]), 0) + start == places, 1.0, 0.0)
    return jnp.dot(pick.astype(jnp.bfloat16), rows, preferred_element_type=jnp.float32).astype(
        jnp.bfloat16
    )


def pack_kernel(size, emb_ref, ids_ref, *refs):
    *out_refs, rank_ref, aug_ref = refs
    rows, width = emb_ref.shape
    chips, labels, cap, pool = size["chips"], size["labels"], size["cap"], size["pool"]
    across, tiles = size["across"], size["tiles"]
    chunk = 256
    for start in range(0, rows, chunk):
        x = emb_ref[start : start + chunk, :]
        energy = jnp.sum(x * x, axis=1, keepdims=True)
        aug_ref[start : start + chunk, :] = (x * lax.rsqrt(energy + epsilon)).astype(jnp.bfloat16)

    ids = ids_ref[...]
    label = ids >> (chips.bit_length() - 1)
    shift = ((ids & (tiles - 1)) - lax.axis_index("tile")) & (tiles - 1)
    side = ((ids & (chips - 1)) >> (tiles.bit_length() - 1)) ^ lax.axis_index("chip")
    block = shift * across + side
    key = ((block * labels + label) * rows + iota((1, rows), 1)).astype(jnp.float32)
    base = (block * (labels * rows)).astype(jnp.float32)
    base_shift = (shift * (across * labels * rows)).astype(jnp.float32)
    key_t = jnp.broadcast_to(key, (LANES, rows)).T
    ranks, pooled = [], []
    for start in range(0, rows, LANES):
        here = slice(start, start + LANES)
        smaller = key_t < key[:, here]
        in_block = jnp.where(smaller & (key_t >= base[:, here]), 1.0, 0.0)
        in_shift = jnp.where(smaller & (key_t >= base_shift[:, here]), 1.0, 0.0)
        ranks.append(jnp.sum(in_block, axis=0, keepdims=True))
        pooled.append(jnp.sum(in_shift, axis=0, keepdims=True))
    rank = jnp.concatenate(ranks, axis=1)
    rank_ref[...] = rank
    pooled = jnp.concatenate(pooled, axis=1)
    full = (rank >= cap - 1) | ((shift > 0) & (pooled >= pool - across))
    over = jnp.max(jnp.where(full, 1.0, 0.0), axis=1, keepdims=True)
    place = jnp.where(shift > 0, pooled, side * cap + rank).astype(jnp.int32)
    place = jnp.where(full, -1, place)

    in_block = jnp.where(iota((LANES, rows), 0) == block, 1.0, 0.0).astype(jnp.bfloat16)
    in_label = jnp.where(iota((LANES, rows), 0) == label, 1.0, 0.0).astype(jnp.bfloat16)
    counts = lax.dot_general(
        in_block, in_label, (((1,), (1,)), ((), ())), preferred_element_type=jnp.float32
    )
    counts = jnp.where(iota((LANES, LANES), 1) == FLAG, over, counts)
    aug_ref[rows:, :] = jnp.zeros((LANES, width), jnp.bfloat16)
    aug_ref[rows:, 0:LANES] = counts.astype(jnp.bfloat16)
    lane = iota((1, LANES), 1)
    head_shift = jnp.where(lane < chips, lane >> (across.bit_length() - 1), -1)
    head_side = lane & (across - 1)
    head = jnp.where(head_shift > 0, pool - across + head_side, head_side * cap + cap - 1)
    shift = jnp.concatenate([shift, head_shift], axis=1)
    place = jnp.concatenate([place, head], axis=1)
    aug = aug_ref[...]
    for index in range(1, tiles):
        out_refs[across + index - 1][...] = pick_rows(
            jnp.where(shift == index, place, -1), 0, pool, aug
        )
    near = jnp.where(shift == 0, place, -1)
    for index in range(across):
        out_refs[index][...] = pick_rows(near, index * cap, cap, aug)


def regroup_kernel(size, pool_ref, *out_refs):
    across, cap, pool, labels = size["across"], size["cap"], size["pool"], size["labels"]
    rows = pool_ref[...]
    heads = rows[pool - 16 :, 0:LANES].astype(jnp.float32)
    heads = jnp.where(iota((16, LANES), 1) < labels, heads, 0.0)
    counts = jnp.sum(heads, axis=1, keepdims=True).astype(jnp.int32)
    spot = iota((1, pool), 1)
    place = jnp.full((1, pool), -1, jnp.int32)
    begin = jnp.zeros((1, 1), jnp.int32)
    for side in range(across):
        end = begin + counts[16 - across + side : 17 - across + side, :]
        place = jnp.where((spot >= begin) & (spot < end), spot - begin + side * cap, place)
        begin = end
    place = jnp.where(spot >= pool - across, (spot - (pool - across) + 1) * cap - 1, place)
    for side, out_ref in enumerate(out_refs):
        out_ref[...] = pick_rows(place, side * cap, cap, rows)


def sort_kernel(size, *refs):
    across, labels, cap, space = size["across"], size["labels"], size["cap"], size["space"]
    block_refs, (out_ref, place_ref, counts_ref, rows_ref) = refs[:across], refs[across:]
    held = up(cap, ALIGN)
    total = across * held
    for index, ref in enumerate(block_refs):
        if held > cap:
            start = (index + 1) * held - ALIGN
            rows_ref[start : start + ALIGN, :] = jnp.zeros((ALIGN, ref.shape[1]), jnp.bfloat16)
        rows_ref[index * held : index * held + cap, :] = ref[...]
    rows = rows_ref[...]
    spot = iota((LANES, total), 1)
    block = iota((LANES, total), 0)
    head = jnp.where(spot == block * held + cap - 1, 1.0, 0.0).astype(jnp.bfloat16)
    counts = jnp.dot(head, rows[:, 0:LANES], preferred_element_type=jnp.float32)
    flag = jnp.max(counts[:, FLAG:], axis=0, keepdims=True)

    counts_t = counts.T
    lower = jnp.where(iota((LANES, LANES), 0) < iota((LANES, LANES), 1), 1.0, 0.0)
    ahead = exact_dot(counts_t, lower)
    in_block = jnp.zeros((1, LANES), jnp.float32)
    found = jnp.zeros((1, LANES), jnp.float32)
    begin = jnp.zeros((1, 1), jnp.float32)
    lane = iota((1, LANES), 1)
    table = []
    for label in range(labels):
        own = counts_t[label : label + 1, :]
        table.append(begin + ahead[label : label + 1, :] - in_block)
        in_block = in_block + own
        table.append(in_block)
        count = jnp.sum(own, axis=1, keepdims=True)
        found = jnp.where(lane == label, count, found)
        begin = begin + jnp.floor((count + (ALIGN - 1)) * (1.0 / ALIGN)) * ALIGN
    flag = jnp.maximum(flag, jnp.where(begin > space, 1.0, 0.0))
    found = jnp.where(lane == FLAG, flag, found)
    counts_ref[...] = jnp.broadcast_to(found, counts_ref.shape).astype(jnp.int32)
    table.append((lane * held).astype(jnp.float32))
    table.extend([jnp.zeros((1, LANES), jnp.float32)] * (up(len(table), 8) - len(table)))
    table = jnp.concatenate(table, axis=0)

    def places(expand, rank_row):
        where = exact_dot(table, expand)
        rank = rank_row(where)
        place = jnp.full(rank.shape, -1.0, jnp.float32)
        for label in reversed(range(labels)):
            inside = rank < where[2 * label + 1 : 2 * label + 2, :]
            place = jnp.where(inside, where[2 * label : 2 * label + 1, :] + rank, place)
        return place.astype(jnp.int32)

    spot_block = jnp.where((spot >= block * held) & (spot < block * held + cap), 1.0, 0.0)
    spot_row = iota((1, total), 1).astype(jnp.float32)
    place = places(spot_block, lambda where: spot_row - where[2 * labels : 2 * labels + 1, :])
    lanes = place_ref.shape[1]
    rank_row = iota((1, lanes), 1).astype(jnp.float32)
    for index in range(across):
        only = jnp.where(iota((LANES, lanes), 0) == index, 1.0, 0.0)
        place_ref[index : index + 1, :] = places(only, lambda where: rank_row)

    out_ref[space:, :] = jnp.zeros((STEP, out_ref.shape[1]), jnp.bfloat16)
    for start in range(0, space, ALIGN * 9):
        count = min(ALIGN * 9, space - start)
        out_ref[start : start + count, :] = pick_rows(place, start, count, rows)


def score_kernel(size, *refs):
    across, tiles, labels, space = size["across"], size["tiles"], size["labels"], size["space"]
    pieces = 2 * tiles
    counts_refs, piece_refs, place_refs = (
        refs[:pieces],
        refs[pieces : 2 * pieces],
        refs[2 * pieces : 2 * pieces + tiles],
    )
    out_ref, rows_ref, total_ref, back_ref = refs[2 * pieces + tiles :]
    lane = iota((1, LANES), 1)
    flag = jnp.int32(0)
    for ref in counts_refs:
        flag = jnp.maximum(flag, ref[0, FLAG])

    def aligned(count):
        return (count + (ALIGN - 1)) & -ALIGN

    counts, places, begins = [], [], []
    begin = jnp.int32(0)
    source = [jnp.int32(0)] * pieces
    for label in range(labels):
        begins.append(begin)
        counts.append([])
        places.append([])
        for index in range(pieces):
            free = space - source[index]
            count = jnp.clip(counts_refs[index][0, label], 0, free)
            counts[label].append(count)
            places[label].append((source[index], begin))
            src, dst = source[index], begin

            def move(step, carry, ref=piece_refs[index], src=src, dst=dst):
                rows = pl.ds(pl.multiple_of(src + step * STEP, ALIGN), STEP)
                to = pl.ds(pl.multiple_of(dst + step * STEP, ALIGN), STEP)
                rows_ref[to, :] = ref[rows, :]
                return carry

            move(0, 0)
            lax.fori_loop(1, (count + STEP - 1) // STEP, move, 0)
            source[index] = source[index] + aligned(count)
            begin = begin + aligned(count)

    for label in range(labels):
        first = begins[label]
        own_end = places[label][tiles][1]
        end = begins[label + 1] if label + 1 < labels else begin

        def window(row, column, label=label):
            left = rows_ref[pl.ds(pl.multiple_of(row, ALIGN), LEFT), :]
            right = rows_ref[pl.ds(pl.multiple_of(column, ALIGN), RIGHT), :]
            scores = lax.dot_general(
                left, right, (((1,), (1,)), ((), ())), preferred_element_type=jnp.float32
            )
            at = iota((1, RIGHT), 1) + column
            valid = at < 0
            for index in range(pieces):
                low = places[label][index][1]
                valid = valid | ((at >= low) & (at < low + counts[label][index]))
            at = jnp.where(valid, at, -1)
            itself = iota((LEFT, RIGHT), 0) + row
            counted = (at >= 0) & (at != itself)
            terms = jnp.where(counted, jnp.exp(sharpness * scores), 0.0)
            return jnp.sum(terms, axis=1, keepdims=True)

        def strip(row, first=first, end=end, window=window):
            sums = window(row, first)
            sums = lax.fori_loop(
                1,
                (end - first + RIGHT - 1) // RIGHT,
                lambda step, sums: sums + window(row, first + step * RIGHT),
                sums,
            )
            total_ref[pl.ds(pl.multiple_of(row, ALIGN), LEFT), :] = jnp.broadcast_to(
                sums, (LEFT, LANES)
            )

        def more(step, carry, first=first, strip=strip):
            strip(first + step * LEFT)
            return carry

        strip(first)
        lax.fori_loop(1, (own_end - first + LEFT - 1) // LEFT, more, 0)

    for index in range(tiles):
        for label in range(labels):
            src, dst = places[label][index][1], places[label][index][0]

            def back(step, carry, index=index, src=src, dst=dst):
                rows = pl.ds(pl.multiple_of(src + step * STEP, ALIGN), STEP)
                to = pl.ds(pl.multiple_of(dst + step * STEP, ALIGN), STEP)
                back_ref[index, to, :] = total_ref[rows, :]
                return carry

            back(0, 0)
            lax.fori_loop(1, (counts[label][index] + STEP - 1) // STEP, back, 0)

    lanes = out_ref.shape[1]
    row = iota((space, LANES), 0)
    chip, tile = lax.axis_index("chip"), lax.axis_index("tile")
    for shift in range(tiles):
        for side in range(across):
            home = (chip ^ side) * tiles + ((tile - shift) & (tiles - 1))
            for start in range(0, lanes, LANES):
                place = place_refs[shift][side : side + 1, start : start + LANES]
                value = jnp.sum(
                    jnp.where(row == place, back_ref[shift, 0:space, :], 0.0),
                    axis=0,
                    keepdims=True,
                )
                if start + LANES == lanes:
                    value = jnp.where(lane == FLAG, flag.astype(jnp.float32), value)
                out_ref[pl.ds(home, 1), start : start + LANES] = value


def unpack_kernel(chips, ret_ref, ids_ref, rank_ref, out_ref, flag_ref):
    rows = ids_ref.shape[1]
    lanes = ret_ref.shape[1]
    values = ret_ref[...]
    flag = jnp.max(values[:, lanes - 1 :], axis=0, keepdims=True)
    flag_ref[...] = jnp.broadcast_to(flag, flag_ref.shape).astype(jnp.int32)
    chip = ids_ref[...] & (chips - 1)
    rank = rank_ref[...].astype(jnp.int32)
    at_rank = jnp.where(iota((lanes, rows), 0) == rank, 1.0, 0.0)
    found = exact_dot(values, at_rank)
    total = jnp.sum(jnp.where(iota((chips, rows), 0) == chip, found, 0.0), axis=0, keepdims=True)
    out_ref[...] = jnp.log(1.0 + total)


def call(kernel, name, out_shape, inputs, scalars=0, **options):
    vmem = pl.BlockSpec(memory_space=pltpu.VMEM)
    smem = pl.BlockSpec(memory_space=pltpu.SMEM)
    return pl.pallas_call(
        kernel,
        out_shape=out_shape,
        in_specs=[smem] * scalars + [vmem] * (len(inputs) - scalars),
        out_specs=jax.tree.map(lambda _: vmem, out_shape),
        compiler_params=pltpu.CompilerParams(vmem_limit_bytes=VMEM_BYTES),
        name=name,
        **options,
    )(*inputs)


def body(embeddings, cluster_ids):
    rows, width = embeddings.shape
    across, tiles = lax.axis_size("chip"), lax.axis_size("tile")
    chips = across * tiles
    labels = KG * across * lax.axis_size("core") // chips
    cap = up(room(rows, chips, 5.0) + 1, 8)
    pool = up(room(rows, tiles, 4.25) + across, ALIGN)
    space = up(room(rows, tiles, 4.75) + labels * (ALIGN - 4), ALIGN)
    size = dict(
        chips=chips, across=across, tiles=tiles, labels=labels, cap=cap, pool=pool, space=space
    )
    lanes = up(cap + 1, LANES)
    shape = jax.ShapeDtypeStruct

    ids_row = cluster_ids.reshape(1, rows)
    *packed, rank = call(
        functools.partial(pack_kernel, size),
        "pack",
        [shape((cap, width), jnp.bfloat16)] * across
        + [shape((pool, width), jnp.bfloat16)] * (tiles - 1)
        + [shape((1, rows), jnp.float32)],
        [embeddings, ids_row],
        scratch_shapes=[pltpu.VMEM((rows + LANES, width), jnp.bfloat16)],
    )
    pools = {
        shift: lax.ppermute(
            packed[across + shift - 1], "tile", [(z, (z + shift) % tiles) for z in range(tiles)]
        )
        for shift in sorted(range(1, tiles), key=lambda shift: -min(shift, tiles - shift))
    }
    own, other, own_counts, other_counts, places = [], [], [], [], []
    swap = [(0, 1), (1, 0)]
    for shift in range(tiles):
        blocks = packed[:across]
        if shift:
            blocks = call(
                functools.partial(regroup_kernel, size),
                "regroup",
                [shape((cap, width), jnp.bfloat16)] * across,
                [pools[shift]],
            )
        arrived = [blocks[0]] + [
            lax.ppermute(blocks[side], "chip", [(a, a ^ side) for a in range(across)])
            for side in range(1, across)
        ]
        ordered, place, counts = call(
            functools.partial(sort_kernel, size),
            "sort",
            [
                shape((space + STEP, width), jnp.bfloat16),
                shape((across, lanes), jnp.int32),
                shape((8, LANES), jnp.int32),
            ],
            arrived,
            scratch_shapes=[pltpu.VMEM((across * up(cap, ALIGN), width), jnp.bfloat16)],
        )
        own.append(ordered)
        places.append(place)
        own_counts.append(counts)
        other_counts.append(lax.ppermute(counts, "core", swap))
        other.append(lax.ppermute(ordered, "core", swap))
    room_all = 2 * tiles * space + RIGHT
    totals = call(
        functools.partial(score_kernel, size),
        "score",
        shape((chips, lanes), jnp.float32),
        [*own_counts, *other_counts, *own, *other, *places],
        scalars=2 * tiles,
        scratch_shapes=[
            pltpu.VMEM((room_all, width), jnp.bfloat16),
            pltpu.VMEM((room_all, LANES), jnp.float32),
            pltpu.VMEM((tiles, space + STEP, LANES), jnp.float32),
        ],
    )
    returned = lax.all_to_all(totals, ("chip", "tile"), split_axis=0, concat_axis=0, tiled=True)
    result, flag = call(
        functools.partial(unpack_kernel, chips),
        "unpack",
        [shape((1, rows), jnp.float32), shape((8, LANES), jnp.int32)],
        [returned, ids_row, rank],
    )
    return lax.cond(
        flag[0, 0] > 0,
        lambda: general_plan(embeddings, cluster_ids),
        lambda: result.reshape(rows),
    )


def solution(mesh):
    shards = mesh.shape["shard"]
    tiles = mesh.shape["tile"]
    split = Mesh(mesh.devices.reshape(shards // 2, 2, tiles), ("chip", "core", "tile"))
    rows = ("chip", "core", "tile")
    return jax.shard_map(
        body, mesh=split, in_specs=(P(rows, None), P(rows)), out_specs=P(rows), check_vma=False
    )
```

```python
import functools
import math

import jax
import jax.numpy as jnp
from jax import lax
from jax.experimental import pallas as pl
from jax.experimental.pallas import tpu as pltpu
from jax.sharding import Mesh
from jax.sharding import PartitionSpec as P

KG = 16


sharpness = 30.0
epsilon = 1e-06

VMEM_BYTES = 48 * 1024 * 1024
LANES = 128
FLAG = LANES - 1
ALIGN = 16
STEP = 32
LEFT = 192
RIGHT = 384
PLACES = 1 << 16


def unit_rows(embeddings):
    energy = jnp.sum(embeddings * embeddings, axis=1, keepdims=True)
    return (embeddings * lax.rsqrt(energy + epsilon)).astype(jnp.bfloat16)


def row_sums(left, left_labels, right, right_labels, same_rows):
    count = left.shape[0]
    block = min(512, count)
    blocks = count // block

    def step(start, items):
        rows_block, labels_block = items
        scores = lax.dot_general(
            rows_block, right, (((1,), (1,)), ((), ())), preferred_element_type=jnp.float32
        )
        same = (labels_block[:, None] == right_labels[None, :]) & (labels_block[:, None] >= 0)
        itself = (start + jnp.arange(block))[:, None] == jnp.arange(count)[None, :]
        same = same & ~(itself & same_rows)
        terms = jnp.where(same, jnp.exp(sharpness * scores), 0.0)
        return (start + block, jnp.sum(terms, axis=1))

    _, totals = lax.scan(
        step,
        jnp.int32(0),
        (left.reshape(blocks, block, left.shape[1]), left_labels.reshape(blocks, block)),
    )
    return totals.reshape(count)


def general_plan(embeddings, cluster_ids):
    shard_axes = ("chip", "core")
    local_rows = embeddings.shape[0]
    shards = lax.axis_size("chip") * lax.axis_size("core")
    tiles = lax.axis_size("tile")
    capacity = 2 * local_rows // shards
    slot_count = shards * capacity
    unit = unit_rows(embeddings)
    owner = cluster_ids // KG
    onehot = (owner[:, None] == jnp.arange(shards, dtype=jnp.int32)[None, :]).astype(jnp.int32)
    ranks = jnp.sum((jnp.cumsum(onehot, axis=0) - 1) * onehot, axis=1)
    slots = owner * capacity + ranks
    outgoing = jnp.zeros((slot_count, unit.shape[1]), jnp.bfloat16).at[slots].set(unit)
    outgoing_labels = jnp.full((slot_count,), -1, jnp.int32).at[slots].set(cluster_ids)
    owned = lax.all_to_all(outgoing, shard_axes, split_axis=0, concat_axis=0, tiled=True)
    owned_labels = lax.all_to_all(
        outgoing_labels, shard_axes, split_axis=0, concat_axis=0, tiled=True
    )
    around = [(tile, (tile + 1) % tiles) for tile in range(tiles)]

    def visit(step, state):
        totals, rows, labels = state
        totals = totals + row_sums(owned, owned_labels, rows, labels, step == 0)
        return (totals, lax.ppermute(rows, "tile", around), lax.ppermute(labels, "tile", around))

    totals, _, _ = lax.fori_loop(
        0, tiles, visit, (jnp.zeros((slot_count,), jnp.float32), owned, owned_labels)
    )
    returned = lax.all_to_all(totals, shard_axes, split_axis=0, concat_axis=0, tiled=True)
    return jnp.log(1.0 + returned[slots])


def up(value, multiple):
    return -(-value // multiple) * multiple


def room(count, parts, sigmas):
    mean = count / parts
    return math.ceil(mean + sigmas * (mean * (1 - 1 / parts)) ** 0.5)


def iota(shape, axis):
    return lax.broadcasted_iota(jnp.int32, shape, axis)


def exact_dot(left, right):
    return jnp.dot(
        left, right, precision=lax.Precision.HIGHEST, preferred_element_type=jnp.float32
    )


def pick_rows(places, start, count, rows):
    pick = jnp.where(iota((count, places.shape[1]), 0) + start == places, 1.0, 0.0)
    return jnp.dot(pick.astype(jnp.bfloat16), rows, preferred_element_type=jnp.float32).astype(
        jnp.bfloat16
    )


def plan_kernel(size, emb_ref, ids_ref, pool_ref, aug_ref, place_ref, rank_ref):
    rows, width = emb_ref.shape
    chips, labels, cap, pool = size["chips"], size["labels"], size["cap"], size["pool"]
    across, tiles, direct = size["across"], size["tiles"], size["direct"]
    chunk = 256
    for start in range(0, rows, chunk):
        x = emb_ref[start : start + chunk, :]
        energy = jnp.sum(x * x, axis=1, keepdims=True)
        aug_ref[start : start + chunk, :] = (x * lax.rsqrt(energy + epsilon)).astype(jnp.bfloat16)

    ids = ids_ref[...]
    label = ids >> (chips.bit_length() - 1)
    shift = ((ids & (tiles - 1)) - lax.axis_index("tile")) & (tiles - 1)
    side = ((ids & (chips - 1)) >> (tiles.bit_length() - 1)) ^ lax.axis_index("chip")
    block = shift * across + side
    key = ((block * labels + label) * rows + iota((1, rows), 1)).astype(jnp.float32)
    base = (block * (labels * rows)).astype(jnp.float32)
    base_shift = (shift * (across * labels * rows)).astype(jnp.float32)
    key_t = jnp.broadcast_to(key, (LANES, rows)).T
    ranks, pooled = [], []
    for start in range(0, rows, LANES):
        here = slice(start, start + LANES)
        smaller = key_t < key[:, here]
        in_block = jnp.where(smaller & (key_t >= base[:, here]), 1.0, 0.0)
        in_shift = jnp.where(smaller & (key_t >= base_shift[:, here]), 1.0, 0.0)
        ranks.append(jnp.sum(in_block, axis=0, keepdims=True))
        pooled.append(jnp.sum(in_shift, axis=0, keepdims=True))
    rank = jnp.concatenate(ranks, axis=1)
    rank_ref[...] = rank
    pooled = jnp.concatenate(pooled, axis=1)

    def apart(shift):
        return (shift == 0) | (shift == direct)

    full = (rank >= cap - 1) | (~apart(shift) & (pooled >= pool - across))
    over = jnp.max(jnp.where(full, 1.0, 0.0), axis=1, keepdims=True)
    place = jnp.where(apart(shift), side * cap + rank.astype(jnp.int32), pooled.astype(jnp.int32))
    place = jnp.where(full, -1, place)

    in_block = jnp.where(iota((LANES, rows), 0) == block, 1.0, 0.0).astype(jnp.bfloat16)
    in_label = jnp.where(iota((LANES, rows), 0) == label, 1.0, 0.0).astype(jnp.bfloat16)
    counts = lax.dot_general(
        in_block, in_label, (((1,), (1,)), ((), ())), preferred_element_type=jnp.float32
    )
    counts = jnp.where(iota((LANES, LANES), 1) == FLAG, over, counts)
    aug_ref[rows:, :] = jnp.zeros((LANES, width), jnp.bfloat16)
    aug_ref[rows:, 0:LANES] = counts.astype(jnp.bfloat16)
    lane = iota((1, LANES), 1)
    head_shift = jnp.where(lane < chips, lane >> (across.bit_length() - 1), -1)
    head_side = lane & (across - 1)
    head = jnp.where(
        apart(head_shift), head_side * cap + cap - 1, pool - across + head_side
    )
    shift = jnp.concatenate([shift, head_shift], axis=1)
    place = jnp.concatenate([place, head], axis=1)
    place = jnp.where(place >= 0, shift * PLACES + place, -1)
    place_ref[...] = place
    pool_ref[...] = pick_rows(place, size["first"] * PLACES, pool, aug_ref[...])


def pack_kernel(starts, aug_ref, place_ref, *out_refs):
    aug = aug_ref[...]
    place = place_ref[...]
    for start, out_ref in zip(starts, out_refs):
        out_ref[...] = pick_rows(place, start, out_ref.shape[0], aug)


def regroup_kernel(size, pool_ref, *out_refs):
    across, cap, pool, labels = size["across"], size["cap"], size["pool"], size["labels"]
    rows = pool_ref[...]
    heads = rows[pool - 16 :, 0:LANES].astype(jnp.float32)
    heads = jnp.where(iota((16, LANES), 1) < labels, heads, 0.0)
    counts = jnp.sum(heads, axis=1, keepdims=True).astype(jnp.int32)
    spot = iota((1, pool), 1)
    place = jnp.full((1, pool), -1, jnp.int32)
    begin = jnp.zeros((1, 1), jnp.int32)
    for side in range(across):
        end = begin + counts[16 - across + side : 17 - across + side, :]
        place = jnp.where((spot >= begin) & (spot < end), spot - begin + side * cap, place)
        begin = end
    place = jnp.where(spot >= pool - across, (spot - (pool - across) + 1) * cap - 1, place)
    for side, out_ref in enumerate(out_refs):
        out_ref[...] = pick_rows(place, side * cap, cap, rows)


def sort_kernel(size, *refs):
    across, labels, cap, space = size["across"], size["labels"], size["cap"], size["space"]
    block_refs, (out_ref, place_ref, counts_ref, rows_ref) = refs[:across], refs[across:]
    held = up(cap, ALIGN)
    total = across * held
    for index, ref in enumerate(block_refs):
        if held > cap:
            start = (index + 1) * held - ALIGN
            rows_ref[start : start + ALIGN, :] = jnp.zeros((ALIGN, ref.shape[1]), jnp.bfloat16)
        rows_ref[index * held : index * held + cap, :] = ref[...]
    rows = rows_ref[...]
    spot = iota((LANES, total), 1)
    block = iota((LANES, total), 0)
    head = jnp.where(spot == block * held + cap - 1, 1.0, 0.0).astype(jnp.bfloat16)
    counts = jnp.dot(head, rows[:, 0:LANES], preferred_element_type=jnp.float32)
    flag = jnp.max(counts[:, FLAG:], axis=0, keepdims=True)

    counts_t = counts.T
    lower = jnp.where(iota((LANES, LANES), 0) < iota((LANES, LANES), 1), 1.0, 0.0)
    ahead = exact_dot(counts_t, lower)
    in_block = jnp.zeros((1, LANES), jnp.float32)
    found = jnp.zeros((1, LANES), jnp.float32)
    begin = jnp.zeros((1, 1), jnp.float32)
    lane = iota((1, LANES), 1)
    table = []
    for label in range(labels):
        own = counts_t[label : label + 1, :]
        table.append(begin + ahead[label : label + 1, :] - in_block)
        in_block = in_block + own
        table.append(in_block)
        count = jnp.sum(own, axis=1, keepdims=True)
        found = jnp.where(lane == label, count, found)
        begin = begin + jnp.floor((count + (ALIGN - 1)) * (1.0 / ALIGN)) * ALIGN
    flag = jnp.maximum(flag, jnp.where(begin > space, 1.0, 0.0))
    found = jnp.where(lane == FLAG, flag, found)
    counts_ref[...] = jnp.broadcast_to(found, counts_ref.shape).astype(jnp.int32)
    table.append((lane * held).astype(jnp.float32))
    table.extend([jnp.zeros((1, LANES), jnp.float32)] * (up(len(table), 8) - len(table)))
    table = jnp.concatenate(table, axis=0)

    def places(expand, rank_row):
        where = exact_dot(table, expand)
        rank = rank_row(where)
        place = jnp.full(rank.shape, -1.0, jnp.float32)
        for label in reversed(range(labels)):
            inside = rank < where[2 * label + 1 : 2 * label + 2, :]
            place = jnp.where(inside, where[2 * label : 2 * label + 1, :] + rank, place)
        return place.astype(jnp.int32)

    spot_block = jnp.where((spot >= block * held) & (spot < block * held + cap), 1.0, 0.0)
    spot_row = iota((1, total), 1).astype(jnp.float32)
    place = places(spot_block, lambda where: spot_row - where[2 * labels : 2 * labels + 1, :])
    lanes = place_ref.shape[1]
    rank_row = iota((1, lanes), 1).astype(jnp.float32)
    for index in range(across):
        only = jnp.where(iota((LANES, lanes), 0) == index, 1.0, 0.0)
        place_ref[index : index + 1, :] = places(only, lambda where: rank_row)

    out_ref[space:, :] = jnp.zeros((STEP, out_ref.shape[1]), jnp.bfloat16)
    for start in range(0, space, ALIGN * 9):
        count = min(ALIGN * 9, space - start)
        out_ref[start : start + count, :] = pick_rows(place, start, count, rows)


def score_kernel(size, *refs):
    across, tiles, labels, space = size["across"], size["tiles"], size["labels"], size["space"]
    pieces = 2 * tiles
    counts_refs, piece_refs, place_refs = (
        refs[:pieces],
        refs[pieces : 2 * pieces],
        refs[2 * pieces : 2 * pieces + tiles],
    )
    out_ref, rows_ref, total_ref, back_ref = refs[2 * pieces + tiles :]
    lane = iota((1, LANES), 1)
    flag = jnp.int32(0)
    for ref in counts_refs:
        flag = jnp.maximum(flag, ref[0, FLAG])

    def aligned(count):
        return (count + (ALIGN - 1)) & -ALIGN

    counts, places, begins = [], [], []
    begin = jnp.int32(0)
    source = [jnp.int32(0)] * pieces
    for label in range(labels):
        begins.append(begin)
        counts.append([])
        places.append([])
        for index in range(pieces):
            free = space - source[index]
            count = jnp.clip(counts_refs[index][0, label], 0, free)
            counts[label].append(count)
            places[label].append((source[index], begin))
            src, dst = source[index], begin

            def move(step, carry, ref=piece_refs[index], src=src, dst=dst):
                rows = pl.ds(pl.multiple_of(src + step * STEP, ALIGN), STEP)
                to = pl.ds(pl.multiple_of(dst + step * STEP, ALIGN), STEP)
                rows_ref[to, :] = ref[rows, :]
                return carry

            move(0, 0)
            lax.fori_loop(1, (count + STEP - 1) // STEP, move, 0)
            source[index] = source[index] + aligned(count)
            begin = begin + aligned(count)

    for label in range(labels):
        first = begins[label]
        own_end = places[label][tiles][1]
        end = begins[label + 1] if label + 1 < labels else begin

        def window(row, column, label=label):
            left = rows_ref[pl.ds(pl.multiple_of(row, ALIGN), LEFT), :]
            right = rows_ref[pl.ds(pl.multiple_of(column, ALIGN), RIGHT), :]
            scores = lax.dot_general(
                left, right, (((1,), (1,)), ((), ())), preferred_element_type=jnp.float32
            )
            at = iota((1, RIGHT), 1) + column
            valid = at < 0
            for index in range(pieces):
                low = places[label][index][1]
                valid = valid | ((at >= low) & (at < low + counts[label][index]))
            at = jnp.where(valid, at, -1)
            itself = iota((LEFT, RIGHT), 0) + row
            counted = (at >= 0) & (at != itself)
            terms = jnp.where(counted, jnp.exp(sharpness * scores), 0.0)
            return jnp.sum(terms, axis=1, keepdims=True)

        def strip(row, first=first, end=end, window=window):
            sums = window(row, first)
            sums = lax.fori_loop(
                1,
                (end - first + RIGHT - 1) // RIGHT,
                lambda step, sums: sums + window(row, first + step * RIGHT),
                sums,
            )
            total_ref[pl.ds(pl.multiple_of(row, ALIGN), LEFT), :] = jnp.broadcast_to(
                sums, (LEFT, LANES)
            )

        def more(step, carry, first=first, strip=strip):
            strip(first + step * LEFT)
            return carry

        strip(first)
        lax.fori_loop(1, (own_end - first + LEFT - 1) // LEFT, more, 0)

    for index in range(tiles):
        for label in range(labels):
            src, dst = places[label][index][1], places[label][index][0]

            def back(step, carry, index=index, src=src, dst=dst):
                rows = pl.ds(pl.multiple_of(src + step * STEP, ALIGN), STEP)
                to = pl.ds(pl.multiple_of(dst + step * STEP, ALIGN), STEP)
                back_ref[index, to, :] = total_ref[rows, :]
                return carry

            back(0, 0)
            lax.fori_loop(1, (counts[label][index] + STEP - 1) // STEP, back, 0)

    lanes = out_ref.shape[1]
    row = iota((space, LANES), 0)
    chip, tile = lax.axis_index("chip"), lax.axis_index("tile")
    for shift in range(tiles):
        for side in range(across):
            home = (chip ^ side) * tiles + ((tile - shift) & (tiles - 1))
            for start in range(0, lanes, LANES):
                place = place_refs[shift][side : side + 1, start : start + LANES]
                value = jnp.sum(
                    jnp.where(row == place, back_ref[shift, 0:space, :], 0.0),
                    axis=0,
                    keepdims=True,
                )
                if start + LANES == lanes:
                    value = jnp.where(lane == FLAG, flag.astype(jnp.float32), value)
                out_ref[pl.ds(home, 1), start : start + LANES] = value


def unpack_kernel(chips, ret_ref, ids_ref, rank_ref, out_ref, flag_ref):
    rows = ids_ref.shape[1]
    lanes = ret_ref.shape[1]
    values = ret_ref[...]
    flag = jnp.max(values[:, lanes - 1 :], axis=0, keepdims=True)
    flag_ref[...] = jnp.broadcast_to(flag, flag_ref.shape).astype(jnp.int32)
    chip = ids_ref[...] & (chips - 1)
    rank = rank_ref[...].astype(jnp.int32)
    at_rank = jnp.where(iota((lanes, rows), 0) == rank, 1.0, 0.0)
    found = exact_dot(values, at_rank)
    total = jnp.sum(jnp.where(iota((chips, rows), 0) == chip, found, 0.0), axis=0, keepdims=True)
    out_ref[...] = jnp.log(1.0 + total)


def call(kernel, name, out_shape, inputs, scalars=0, **options):
    vmem = pl.BlockSpec(memory_space=pltpu.VMEM)
    smem = pl.BlockSpec(memory_space=pltpu.SMEM)
    return pl.pallas_call(
        kernel,
        out_shape=out_shape,
        in_specs=[smem] * scalars + [vmem] * (len(inputs) - scalars),
        out_specs=jax.tree.map(lambda _: vmem, out_shape),
        compiler_params=pltpu.CompilerParams(vmem_limit_bytes=VMEM_BYTES),
        name=name,
        **options,
    )(*inputs)


def body(embeddings, cluster_ids):
    rows, width = embeddings.shape
    across, tiles = lax.axis_size("chip"), lax.axis_size("tile")
    chips = across * tiles
    labels = KG * across * lax.axis_size("core") // chips
    cap = up(room(rows, chips, 5.0) + 1, 8)
    pool = up(room(rows, tiles, 4.25) + across, ALIGN)
    space = up(room(rows, tiles, 4.75) + labels * (ALIGN - 4), ALIGN)
    order = sorted(range(1, tiles), key=lambda shift: (-min(shift, tiles - shift), shift))
    direct = order[-1]
    size = dict(
        chips=chips, across=across, tiles=tiles, labels=labels, cap=cap, pool=pool, space=space,
        first=order[0], direct=direct,
    )
    lanes = up(cap + 1, LANES)
    shape = jax.ShapeDtypeStruct

    ids_row = cluster_ids.reshape(1, rows)
    first, aug, slots, rank = call(
        functools.partial(plan_kernel, size),
        "plan",
        [
            shape((pool, width), jnp.bfloat16),
            shape((rows + LANES, width), jnp.bfloat16),
            shape((1, rows + LANES), jnp.int32),
            shape((1, rows), jnp.float32),
        ],
        [embeddings, ids_row],
    )

    def pack(shift, count, step):
        return call(
            functools.partial(
                pack_kernel, [shift * PLACES + index * step for index in range(count)]
            ),
            "pack",
            [shape((step, width), jnp.bfloat16)] * count,
            [aug, slots],
        )

    def along(shift):
        return [(z, (z + shift) % tiles) for z in range(tiles)]

    def over(side):
        return [(a, a ^ side) for a in range(across)]

    near = pack(0, across, cap)
    pools, last = {}, None
    for shift in order[:-1]:
        pool_rows = first if shift == order[0] else pack(shift, 1, pool)[0]
        if last is not None:
            pool_rows, _ = lax.optimization_barrier((pool_rows, last))
        last = pools[shift] = lax.ppermute(pool_rows, "tile", along(shift))
    far = pack(direct, across, cap)
    if last is not None:
        *far, _ = lax.optimization_barrier((*far, last))

    own, other, own_counts, other_counts, places = [], [], [], [], []
    swap = [(0, 1), (1, 0)]
    for shift in range(tiles):
        if shift == direct:
            arrived = [
                lax.ppermute(
                    far[side],
                    ("chip", "tile"),
                    [(a * tiles + z, b * tiles + y) for a, b in over(side) for z, y in along(shift)],
                )
                for side in range(across)
            ]
        else:
            blocks = near
            if shift:
                blocks = call(
                    functools.partial(regroup_kernel, size),
                    "regroup",
                    [shape((cap, width), jnp.bfloat16)] * across,
                    [pools[shift]],
                )
            arrived = [blocks[0]] + [
                lax.ppermute(blocks[side], "chip", over(side)) for side in range(1, across)
            ]
        ordered, place, counts = call(
            functools.partial(sort_kernel, size),
            "sort",
            [
                shape((space + STEP, width), jnp.bfloat16),
                shape((across, lanes), jnp.int32),
                shape((8, LANES), jnp.int32),
            ],
            arrived,
            scratch_shapes=[pltpu.VMEM((across * up(cap, ALIGN), width), jnp.bfloat16)],
        )
        own.append(ordered)
        places.append(place)
        own_counts.append(counts)
        other_counts.append(lax.ppermute(counts, "core", swap))
        other.append(lax.ppermute(ordered, "core", swap))
    room_all = 2 * tiles * space + RIGHT
    totals = call(
        functools.partial(score_kernel, size),
        "score",
        shape((chips, lanes), jnp.float32),
        [*own_counts, *other_counts, *own, *other, *places],
        scalars=2 * tiles,
        scratch_shapes=[
            pltpu.VMEM((room_all, width), jnp.bfloat16),
            pltpu.VMEM((room_all, LANES), jnp.float32),
            pltpu.VMEM((tiles, space + STEP, LANES), jnp.float32),
        ],
    )
    returned = lax.all_to_all(totals, ("chip", "tile"), split_axis=0, concat_axis=0, tiled=True)
    result, flag = call(
        functools.partial(unpack_kernel, chips),
        "unpack",
        [shape((1, rows), jnp.float32), shape((8, LANES), jnp.int32)],
        [returned, ids_row, rank],
    )
    return lax.cond(
        flag[0, 0] > 0,
        lambda: general_plan(embeddings, cluster_ids),
        lambda: result.reshape(rows),
    )


def solution(mesh):
    shards = mesh.shape["shard"]
    tiles = mesh.shape["tile"]
    split = Mesh(mesh.devices.reshape(shards // 2, 2, tiles), ("chip", "core", "tile"))
    rows = ("chip", "core", "tile")
    return jax.shard_map(
        body, mesh=split, in_specs=(P(rows, None), P(rows)), out_specs=P(rows), check_vma=False
    )
```

```python
import functools
import math

import jax
import jax.numpy as jnp
from jax import lax
from jax.experimental import pallas as pl
from jax.experimental.pallas import tpu as pltpu
from jax.sharding import Mesh
from jax.sharding import PartitionSpec as P

KG = 16


sharpness = 30.0
epsilon = 1e-06

VMEM_BYTES = 48 * 1024 * 1024
LANES = 128
FLAG = LANES - 1
LOW = LANES // 2
ALIGN = 16
STEP = 32
LEFT = 192
RIGHT = 384
PLACES = 1 << 16


def unit_rows(embeddings):
    energy = jnp.sum(embeddings * embeddings, axis=1, keepdims=True)
    return (embeddings * lax.rsqrt(energy + epsilon)).astype(jnp.bfloat16)


def row_sums(left, left_labels, right, right_labels, same_rows):
    count = left.shape[0]
    block = min(512, count)
    blocks = count // block

    def step(start, items):
        rows_block, labels_block = items
        scores = lax.dot_general(
            rows_block, right, (((1,), (1,)), ((), ())), preferred_element_type=jnp.float32
        )
        same = (labels_block[:, None] == right_labels[None, :]) & (labels_block[:, None] >= 0)
        itself = (start + jnp.arange(block))[:, None] == jnp.arange(count)[None, :]
        same = same & ~(itself & same_rows)
        terms = jnp.where(same, jnp.exp(sharpness * scores), 0.0)
        return (start + block, jnp.sum(terms, axis=1))

    _, totals = lax.scan(
        step,
        jnp.int32(0),
        (left.reshape(blocks, block, left.shape[1]), left_labels.reshape(blocks, block)),
    )
    return totals.reshape(count)


def general_plan(embeddings, cluster_ids):
    shard_axes = ("chip", "core")
    local_rows = embeddings.shape[0]
    shards = lax.axis_size("chip") * lax.axis_size("core")
    tiles = lax.axis_size("tile")
    capacity = 2 * local_rows // shards
    slot_count = shards * capacity
    unit = unit_rows(embeddings)
    owner = cluster_ids // KG
    onehot = (owner[:, None] == jnp.arange(shards, dtype=jnp.int32)[None, :]).astype(jnp.int32)
    ranks = jnp.sum((jnp.cumsum(onehot, axis=0) - 1) * onehot, axis=1)
    slots = owner * capacity + ranks
    outgoing = jnp.zeros((slot_count, unit.shape[1]), jnp.bfloat16).at[slots].set(unit)
    outgoing_labels = jnp.full((slot_count,), -1, jnp.int32).at[slots].set(cluster_ids)
    owned = lax.all_to_all(outgoing, shard_axes, split_axis=0, concat_axis=0, tiled=True)
    owned_labels = lax.all_to_all(
        outgoing_labels, shard_axes, split_axis=0, concat_axis=0, tiled=True
    )
    around = [(tile, (tile + 1) % tiles) for tile in range(tiles)]

    def visit(step, state):
        totals, rows, labels = state
        totals = totals + row_sums(owned, owned_labels, rows, labels, step == 0)
        return (totals, lax.ppermute(rows, "tile", around), lax.ppermute(labels, "tile", around))

    totals, _, _ = lax.fori_loop(
        0, tiles, visit, (jnp.zeros((slot_count,), jnp.float32), owned, owned_labels)
    )
    returned = lax.all_to_all(totals, shard_axes, split_axis=0, concat_axis=0, tiled=True)
    return jnp.log(1.0 + returned[slots])


def up(value, multiple):
    return -(-value // multiple) * multiple


def room(count, parts, sigmas):
    mean = count / parts
    return math.ceil(mean + sigmas * (mean * (1 - 1 / parts)) ** 0.5)


def iota(shape, axis):
    return lax.broadcasted_iota(jnp.int32, shape, axis)


def exact_dot(left, right):
    return jnp.dot(
        left, right, precision=lax.Precision.HIGHEST, preferred_element_type=jnp.float32
    )


def pick_rows(places, start, count, rows):
    pick = jnp.where(iota((count, places.shape[1]), 0) + start == places, 1.0, 0.0)
    return jnp.dot(pick.astype(jnp.bfloat16), rows, preferred_element_type=jnp.float32).astype(
        jnp.bfloat16
    )


def plan_kernel(size, emb_ref, ids_ref, pool_ref, aug_ref, place_ref, rank_ref):
    rows, width = emb_ref.shape
    chips, labels, cap, pool = size["chips"], size["labels"], size["cap"], size["pool"]
    across, tiles = size["across"], size["tiles"]
    chunk = 256
    for start in range(0, rows, chunk):
        x = emb_ref[start : start + chunk, :]
        energy = jnp.sum(x * x, axis=1, keepdims=True)
        aug_ref[start : start + chunk, :] = (x * lax.rsqrt(energy + epsilon)).astype(jnp.bfloat16)

    ids = ids_ref[...]
    label = ids >> (chips.bit_length() - 1)
    shift = ((ids & (tiles - 1)) - lax.axis_index("tile")) & (tiles - 1)
    side = ((ids & (chips - 1)) >> (tiles.bit_length() - 1)) ^ lax.axis_index("chip")
    block = shift * across + side
    key = ((block * labels + label) * rows + iota((1, rows), 1)).astype(jnp.float32)
    base = (block * (labels * rows)).astype(jnp.float32)
    base_shift = (shift * (across * labels * rows)).astype(jnp.float32)
    key_t = jnp.broadcast_to(key, (LANES, rows)).T
    ranks, pooled = [], []
    for start in range(0, rows, LANES):
        here = slice(start, start + LANES)
        smaller = key_t < key[:, here]
        in_block = jnp.where(smaller & (key_t >= base[:, here]), 1.0, 0.0)
        in_shift = jnp.where(smaller & (key_t >= base_shift[:, here]), 1.0, 0.0)
        ranks.append(jnp.sum(in_block, axis=0, keepdims=True))
        pooled.append(jnp.sum(in_shift, axis=0, keepdims=True))
    rank = jnp.concatenate(ranks, axis=1)
    rank_ref[...] = rank
    pooled = jnp.concatenate(pooled, axis=1)

    def apart(shift):
        return shift != size["first"]

    full = (rank >= cap - 1) | (~apart(shift) & (pooled >= pool - across))
    over = jnp.max(jnp.where(full, 1.0, 0.0), axis=1, keepdims=True)
    place = jnp.where(apart(shift), side * cap + rank.astype(jnp.int32), pooled.astype(jnp.int32))
    place = jnp.where(full, -1, place)

    in_block = jnp.where(iota((LANES, rows), 0) == block, 1.0, 0.0).astype(jnp.bfloat16)
    in_label = jnp.where(iota((LANES, rows), 0) == label, 1.0, 0.0).astype(jnp.bfloat16)
    counts = lax.dot_general(
        in_block, in_label, (((1,), (1,)), ((), ())), preferred_element_type=jnp.float32
    )
    counts = jnp.where(iota((LANES, LANES), 1) == FLAG, over, counts)
    aug_ref[rows:, :] = jnp.zeros((LANES, width), jnp.bfloat16)
    aug_ref[rows:, 0:LANES] = counts.astype(jnp.bfloat16)
    lane = iota((1, LANES), 1)
    head_shift = jnp.where(lane < chips, lane >> (across.bit_length() - 1), -1)
    head_side = lane & (across - 1)
    head = jnp.where(
        apart(head_shift), head_side * cap + cap - 1, pool - across + head_side
    )
    shift = jnp.concatenate([shift, head_shift], axis=1)
    place = jnp.concatenate([place, head], axis=1)
    place = jnp.where(place >= 0, shift * PLACES + place, -1)
    place_ref[...] = place
    pool_ref[...] = pick_rows(place, size["first"] * PLACES, pool, aug_ref[...])


def pack_kernel(starts, aug_ref, place_ref, *out_refs):
    aug = aug_ref[...]
    place = place_ref[...]
    for start, out_ref in zip(starts, out_refs):
        out_ref[...] = pick_rows(place, start, out_ref.shape[0], aug)


def regroup_kernel(size, pool_ref, *out_refs):
    across, cap, pool, labels = size["across"], size["cap"], size["pool"], size["labels"]
    rows = pool_ref[...]
    heads = rows[pool - 16 :, 0:LANES].astype(jnp.float32)
    heads = jnp.where(iota((16, LANES), 1) < labels, heads, 0.0)
    counts = jnp.sum(heads, axis=1, keepdims=True).astype(jnp.int32)
    spot = iota((1, pool), 1)
    place = jnp.full((1, pool), -1, jnp.int32)
    begin = jnp.zeros((1, 1), jnp.int32)
    for side in range(across):
        end = begin + counts[16 - across + side : 17 - across + side, :]
        place = jnp.where((spot >= begin) & (spot < end), spot - begin + side * cap, place)
        begin = end
    place = jnp.where(spot >= pool - across, (spot - (pool - across) + 1) * cap - 1, place)
    for side, out_ref in enumerate(out_refs):
        out_ref[...] = pick_rows(place, side * cap, cap, rows)


def sort_kernel(size, *refs):
    across, labels, cap, space = size["across"], size["labels"], size["cap"], size["space"]
    block_refs, (out_ref, place_ref, rows_ref) = refs[:across], refs[across:]
    held = up(cap, ALIGN)
    total = across * held
    for index, ref in enumerate(block_refs):
        if held > cap:
            start = (index + 1) * held - ALIGN
            rows_ref[start : start + ALIGN, :] = jnp.zeros((ALIGN, ref.shape[1]), jnp.bfloat16)
        rows_ref[index * held : index * held + cap, :] = ref[...]
    rows = rows_ref[...]
    spot = iota((LANES, total), 1)
    block = iota((LANES, total), 0)
    head = jnp.where(spot == block * held + cap - 1, 1.0, 0.0).astype(jnp.bfloat16)
    counts = jnp.dot(head, rows[:, 0:LANES], preferred_element_type=jnp.float32)
    flag = jnp.max(counts[:, FLAG:], axis=0, keepdims=True)

    counts_t = counts.T
    lower = jnp.where(iota((LANES, LANES), 0) < iota((LANES, LANES), 1), 1.0, 0.0)
    ahead = exact_dot(counts_t, lower)
    in_block = jnp.zeros((1, LANES), jnp.float32)
    found = jnp.zeros((1, LANES), jnp.float32)
    begin = jnp.zeros((1, 1), jnp.float32)
    lane = iota((1, LANES), 1)
    table = []
    for label in range(labels):
        own = counts_t[label : label + 1, :]
        table.append(begin + ahead[label : label + 1, :] - in_block)
        in_block = in_block + own
        table.append(in_block)
        count = jnp.sum(own, axis=1, keepdims=True)
        high = jnp.floor(count * (1.0 / LANES))
        found = jnp.where(lane == label, high, found)
        found = jnp.where(lane == LOW + label, count - high * LANES, found)
        begin = begin + jnp.floor((count + (ALIGN - 1)) * (1.0 / ALIGN)) * ALIGN
    flag = jnp.maximum(flag, jnp.where(begin > space, 1.0, 0.0))
    found = jnp.where(lane == FLAG, flag, found)
    table.append((lane * held).astype(jnp.float32))
    table.extend([jnp.zeros((1, LANES), jnp.float32)] * (up(len(table), 8) - len(table)))
    table = jnp.concatenate(table, axis=0)

    def places(expand, rank_row):
        where = exact_dot(table, expand)
        rank = rank_row(where)
        place = jnp.full(rank.shape, -1.0, jnp.float32)
        for label in reversed(range(labels)):
            inside = rank < where[2 * label + 1 : 2 * label + 2, :]
            place = jnp.where(inside, where[2 * label : 2 * label + 1, :] + rank, place)
        return place.astype(jnp.int32)

    spot_block = jnp.where((spot >= block * held) & (spot < block * held + cap), 1.0, 0.0)
    spot_row = iota((1, total), 1).astype(jnp.float32)
    place = places(spot_block, lambda where: spot_row - where[2 * labels : 2 * labels + 1, :])
    lanes = place_ref.shape[1]
    rank_row = iota((1, lanes), 1).astype(jnp.float32)
    for index in range(across):
        only = jnp.where(iota((LANES, lanes), 0) == index, 1.0, 0.0)
        place_ref[index : index + 1, :] = places(only, lambda where: rank_row)

    out_ref[space:, :] = jnp.zeros((STEP, out_ref.shape[1]), jnp.bfloat16)
    out_ref[space : space + ALIGN, 0:LANES] = jnp.broadcast_to(found, (ALIGN, LANES)).astype(
        jnp.bfloat16
    )
    for start in range(0, space, ALIGN * 9):
        count = min(ALIGN * 9, space - start)
        out_ref[start : start + count, :] = pick_rows(place, start, count, rows)


def score_kernel(size, *refs):
    across, tiles, labels, space = size["across"], size["tiles"], size["labels"], size["space"]
    pieces = 2 * tiles
    piece_refs, place_refs = refs[:pieces], refs[pieces : pieces + tiles]
    out_ref, rows_ref, total_ref, back_ref, heads_ref, counts_ref, sem = refs[pieces + tiles :]
    lane = iota((1, LANES), 1)
    heads = [ref[space : space + ALIGN, 0:LANES].astype(jnp.float32)[0:1, :] for ref in piece_refs]
    heads_ref[...] = jnp.concatenate(heads, axis=0).astype(jnp.int32)
    copy = pltpu.make_async_copy(heads_ref, counts_ref, sem)
    copy.start()
    copy.wait()
    flag = jnp.int32(0)
    for index in range(pieces):
        flag = jnp.maximum(flag, counts_ref[index, FLAG])

    def aligned(count):
        return (count + (ALIGN - 1)) & -ALIGN

    counts, places, begins = [], [], []
    begin = jnp.int32(0)
    source = [jnp.int32(0)] * pieces
    for label in range(labels):
        begins.append(begin)
        counts.append([])
        places.append([])
        for index in range(pieces):
            free = space - source[index]
            count = counts_ref[index, label] * LANES + counts_ref[index, LOW + label]
            count = jnp.clip(count, 0, free)
            counts[label].append(count)
            places[label].append((source[index], begin))
            src, dst = source[index], begin

            def move(step, carry, ref=piece_refs[index], src=src, dst=dst):
                rows = pl.ds(pl.multiple_of(src + step * STEP, ALIGN), STEP)
                to = pl.ds(pl.multiple_of(dst + step * STEP, ALIGN), STEP)
                rows_ref[to, :] = ref[rows, :]
                return carry

            move(0, 0)
            lax.fori_loop(1, (count + STEP - 1) // STEP, move, 0)
            source[index] = source[index] + aligned(count)
            begin = begin + aligned(count)

    for label in range(labels):
        first = begins[label]
        own_end = places[label][tiles][1]
        end = begins[label + 1] if label + 1 < labels else begin

        def window(row, column, label=label):
            left = rows_ref[pl.ds(pl.multiple_of(row, ALIGN), LEFT), :]
            right = rows_ref[pl.ds(pl.multiple_of(column, ALIGN), RIGHT), :]
            scores = lax.dot_general(
                left, right, (((1,), (1,)), ((), ())), preferred_element_type=jnp.float32
            )
            at = iota((1, RIGHT), 1) + column
            valid = at < 0
            for index in range(pieces):
                low = places[label][index][1]
                valid = valid | ((at >= low) & (at < low + counts[label][index]))
            at = jnp.where(valid, at, -1)
            itself = iota((LEFT, RIGHT), 0) + row
            counted = (at >= 0) & (at != itself)
            terms = jnp.where(counted, jnp.exp(sharpness * scores), 0.0)
            return jnp.sum(terms, axis=1, keepdims=True)

        def strip(row, first=first, end=end, window=window):
            sums = window(row, first)
            sums = lax.fori_loop(
                1,
                (end - first + RIGHT - 1) // RIGHT,
                lambda step, sums: sums + window(row, first + step * RIGHT),
                sums,
            )
            total_ref[pl.ds(pl.multiple_of(row, ALIGN), LEFT), :] = jnp.broadcast_to(
                sums, (LEFT, LANES)
            )

        def more(step, carry, first=first, strip=strip):
            strip(first + step * LEFT)
            return carry

        strip(first)
        lax.fori_loop(1, (own_end - first + LEFT - 1) // LEFT, more, 0)

    for index in range(tiles):
        for label in range(labels):
            src, dst = places[label][index][1], places[label][index][0]

            def back(step, carry, index=index, src=src, dst=dst):
                rows = pl.ds(pl.multiple_of(src + step * STEP, ALIGN), STEP)
                to = pl.ds(pl.multiple_of(dst + step * STEP, ALIGN), STEP)
                back_ref[index, to, :] = total_ref[rows, :]
                return carry

            back(0, 0)
            lax.fori_loop(1, (counts[label][index] + STEP - 1) // STEP, back, 0)

    lanes = out_ref.shape[1]
    row = iota((space, LANES), 0)
    chip, tile = lax.axis_index("chip"), lax.axis_index("tile")
    for shift in range(tiles):
        for side in range(across):
            home = (chip ^ side) * tiles + ((tile - shift) & (tiles - 1))
            for start in range(0, lanes, LANES):
                place = place_refs[shift][side : side + 1, start : start + LANES]
                value = jnp.sum(
                    jnp.where(row == place, back_ref[shift, 0:space, :], 0.0),
                    axis=0,
                    keepdims=True,
                )
                if start + LANES == lanes:
                    value = jnp.where(lane == FLAG, flag.astype(jnp.float32), value)
                out_ref[pl.ds(home, 1), start : start + LANES] = value


def unpack_kernel(chips, ret_ref, ids_ref, rank_ref, out_ref, flag_ref):
    rows = ids_ref.shape[1]
    lanes = ret_ref.shape[1]
    values = ret_ref[...]
    flag = jnp.max(values[:, lanes - 1 :], axis=0, keepdims=True)
    flag_ref[...] = jnp.broadcast_to(flag, flag_ref.shape).astype(jnp.int32)
    chip = ids_ref[...] & (chips - 1)
    rank = rank_ref[...].astype(jnp.int32)
    at_rank = jnp.where(iota((lanes, rows), 0) == rank, 1.0, 0.0)
    found = exact_dot(values, at_rank)
    total = jnp.sum(jnp.where(iota((chips, rows), 0) == chip, found, 0.0), axis=0, keepdims=True)
    out_ref[...] = jnp.log(1.0 + total)


def call(kernel, name, out_shape, inputs, **options):
    vmem = pl.BlockSpec(memory_space=pltpu.VMEM)
    return pl.pallas_call(
        kernel,
        out_shape=out_shape,
        in_specs=[vmem] * len(inputs),
        out_specs=jax.tree.map(lambda _: vmem, out_shape),
        compiler_params=pltpu.CompilerParams(vmem_limit_bytes=VMEM_BYTES),
        name=name,
        **options,
    )(*inputs)


def body(embeddings, cluster_ids):
    rows, width = embeddings.shape
    across, tiles = lax.axis_size("chip"), lax.axis_size("tile")
    chips = across * tiles
    labels = KG * across * lax.axis_size("core") // chips
    cap = up(room(rows, chips, 5.0) + 1, 8)
    pool = up(room(rows, tiles, 4.25) + across, ALIGN)
    space = up(room(rows, tiles, 4.75) + labels * (ALIGN - 4), ALIGN)
    order = sorted(range(1, tiles), key=lambda shift: (-min(shift, tiles - shift), shift))
    size = dict(
        chips=chips, across=across, tiles=tiles, labels=labels, cap=cap, pool=pool, space=space,
        first=order[0],
    )
    lanes = up(cap + 1, LANES)
    shape = jax.ShapeDtypeStruct

    ids_row = cluster_ids.reshape(1, rows)
    first, aug, slots, rank = call(
        functools.partial(plan_kernel, size),
        "plan",
        [
            shape((pool, width), jnp.bfloat16),
            shape((rows + LANES, width), jnp.bfloat16),
            shape((1, rows + LANES), jnp.int32),
            shape((1, rows), jnp.float32),
        ],
        [embeddings, ids_row],
    )

    def pack(shift, count, step):
        return call(
            functools.partial(
                pack_kernel, [shift * PLACES + index * step for index in range(count)]
            ),
            "pack",
            [shape((step, width), jnp.bfloat16)] * count,
            [aug, slots],
        )

    def along(shift):
        return [(z, (z + shift) % tiles) for z in range(tiles)]

    def over(side):
        return [(a, a ^ side) for a in range(across)]

    def after(value, *others):
        return lax.optimization_barrier((value, others))[0]

    def send_across(blocks):
        return [blocks[0]] + [
            lax.ppermute(blocks[side], "chip", over(side)) for side in range(1, across)
        ]

    def send_far(blocks, shift, side):
        route = [(a * tiles + z, b * tiles + y) for a, b in over(side) for z, y in along(shift)]
        return lax.ppermute(blocks[side], ("chip", "tile"), route)

    swap = [(0, 1), (1, 0)]
    own, other, places = {}, {}, {}

    def finish(shift, arrived):
        own[shift], places[shift] = call(
            functools.partial(sort_kernel, size),
            "sort",
            [
                shape((space + STEP, width), jnp.bfloat16),
                shape((across, lanes), jnp.int32),
            ],
            arrived,
            scratch_shapes=[pltpu.VMEM((across * up(cap, ALIGN), width), jnp.bfloat16)],
        )
        other[shift] = lax.ppermute(own[shift], "core", swap)

    pooled = lax.ppermute(first, "tile", along(order[0]))
    before = []
    for shift in order[1:-1]:
        blocks = pack(shift, across, cap)
        arrived = [send_far(blocks, shift, side) for side in range(across)]
        finish(shift, arrived)
        before += arrived
    near = send_across(pack(0, across, cap))
    finish(0, near)
    before += near
    arrived = []
    if len(order) > 1:
        blocks = after(pack(order[-1], across, cap), *near)
        arrived = [send_far(blocks, order[-1], 0)]
        blocks = after(blocks, pooled, *arrived)
    regrouped = call(
        functools.partial(regroup_kernel, size),
        "regroup",
        [shape((cap, width), jnp.bfloat16)] * across,
        [after(pooled, *before, *arrived)],
    )
    finish(order[0], send_across(regrouped))
    if len(order) > 1:
        arrived += [send_far(blocks, order[-1], side) for side in range(1, across)]
        finish(order[-1], arrived)
    own, other, places = (
        [found[shift] for shift in range(tiles)] for found in (own, other, places)
    )
    room_all = 2 * tiles * space + RIGHT
    totals = call(
        functools.partial(score_kernel, size),
        "score",
        shape((chips, lanes), jnp.float32),
        [*own, *other, *places],
        scratch_shapes=[
            pltpu.VMEM((room_all, width), jnp.bfloat16),
            pltpu.VMEM((room_all, LANES), jnp.float32),
            pltpu.VMEM((tiles, space + STEP, LANES), jnp.float32),
            pltpu.VMEM((2 * tiles, LANES), jnp.int32),
            pltpu.SMEM((2 * tiles, LANES), jnp.int32),
            pltpu.SemaphoreType.DMA,
        ],
    )
    returned = lax.all_to_all(totals, ("chip", "tile"), split_axis=0, concat_axis=0, tiled=True)
    result, flag = call(
        functools.partial(unpack_kernel, chips),
        "unpack",
        [shape((1, rows), jnp.float32), shape((8, LANES), jnp.int32)],
        [returned, ids_row, rank],
    )
    return lax.cond(
        flag[0, 0] > 0,
        lambda: general_plan(embeddings, cluster_ids),
        lambda: result.reshape(rows),
    )


def solution(mesh):
    shards = mesh.shape["shard"]
    tiles = mesh.shape["tile"]
    split = Mesh(mesh.devices.reshape(shards // 2, 2, tiles), ("chip", "core", "tile"))
    rows = ("chip", "core", "tile")
    return jax.shard_map(
        body, mesh=split, in_specs=(P(rows, None), P(rows)), out_specs=P(rows), check_vma=False
    )
```

```python
import functools
import math

import jax
import jax.numpy as jnp
from jax import lax
from jax.experimental import pallas as pl
from jax.experimental.pallas import tpu as pltpu
from jax.sharding import Mesh
from jax.sharding import PartitionSpec as P

KG = 16


sharpness = 30.0
epsilon = 1e-06

VMEM_BYTES = 48 * 1024 * 1024
LANES = 128
FLAG = LANES - 1
LOW = LANES // 2
ALIGN = 16
STEP = 96
LEFT = 256
RIGHT = 512
PLACES = 1 << 16


def unit_rows(embeddings):
    energy = jnp.sum(embeddings * embeddings, axis=1, keepdims=True)
    return (embeddings * lax.rsqrt(energy + epsilon)).astype(jnp.bfloat16)


def row_sums(left, left_labels, right, right_labels, same_rows):
    count = left.shape[0]
    block = min(512, count)
    blocks = count // block

    def step(start, items):
        rows_block, labels_block = items
        scores = lax.dot_general(
            rows_block, right, (((1,), (1,)), ((), ())), preferred_element_type=jnp.float32
        )
        same = (labels_block[:, None] == right_labels[None, :]) & (labels_block[:, None] >= 0)
        itself = (start + jnp.arange(block))[:, None] == jnp.arange(count)[None, :]
        same = same & ~(itself & same_rows)
        terms = jnp.where(same, jnp.exp(sharpness * scores), 0.0)
        return (start + block, jnp.sum(terms, axis=1))

    _, totals = lax.scan(
        step,
        jnp.int32(0),
        (left.reshape(blocks, block, left.shape[1]), left_labels.reshape(blocks, block)),
    )
    return totals.reshape(count)


def general_plan(embeddings, cluster_ids):
    shard_axes = ("chip", "core")
    local_rows = embeddings.shape[0]
    shards = lax.axis_size("chip") * lax.axis_size("core")
    tiles = lax.axis_size("tile")
    capacity = 2 * local_rows // shards
    slot_count = shards * capacity
    unit = unit_rows(embeddings)
    owner = cluster_ids // KG
    onehot = (owner[:, None] == jnp.arange(shards, dtype=jnp.int32)[None, :]).astype(jnp.int32)
    ranks = jnp.sum((jnp.cumsum(onehot, axis=0) - 1) * onehot, axis=1)
    slots = owner * capacity + ranks
    outgoing = jnp.zeros((slot_count, unit.shape[1]), jnp.bfloat16).at[slots].set(unit)
    outgoing_labels = jnp.full((slot_count,), -1, jnp.int32).at[slots].set(cluster_ids)
    owned = lax.all_to_all(outgoing, shard_axes, split_axis=0, concat_axis=0, tiled=True)
    owned_labels = lax.all_to_all(
        outgoing_labels, shard_axes, split_axis=0, concat_axis=0, tiled=True
    )
    around = [(tile, (tile + 1) % tiles) for tile in range(tiles)]

    def visit(step, state):
        totals, rows, labels = state
        totals = totals + row_sums(owned, owned_labels, rows, labels, step == 0)
        return (totals, lax.ppermute(rows, "tile", around), lax.ppermute(labels, "tile", around))

    totals, _, _ = lax.fori_loop(
        0, tiles, visit, (jnp.zeros((slot_count,), jnp.float32), owned, owned_labels)
    )
    returned = lax.all_to_all(totals, shard_axes, split_axis=0, concat_axis=0, tiled=True)
    return jnp.log(1.0 + returned[slots])


def up(value, multiple):
    return -(-value // multiple) * multiple


def room(count, parts, sigmas):
    mean = count / parts
    return math.ceil(mean + sigmas * (mean * (1 - 1 / parts)) ** 0.5)


def iota(shape, axis):
    return lax.broadcasted_iota(jnp.int32, shape, axis)


def exact_dot(left, right):
    return jnp.dot(
        left, right, precision=lax.Precision.HIGHEST, preferred_element_type=jnp.float32
    )


def pick_rows(places, start, count, rows):
    pick = jnp.where(iota((count, places.shape[1]), 0) + start == places, 1.0, 0.0)
    return jnp.dot(pick.astype(jnp.bfloat16), rows, preferred_element_type=jnp.float32).astype(
        jnp.bfloat16
    )


def plan_kernel(size, emb_ref, ids_ref, pool_ref, aug_ref, place_ref, rank_ref):
    rows, width = emb_ref.shape
    chips, labels, cap, pool = size["chips"], size["labels"], size["cap"], size["pool"]
    across, tiles = size["across"], size["tiles"]
    chunk = 256
    for start in range(0, rows, chunk):
        x = emb_ref[start : start + chunk, :]
        energy = jnp.sum(x * x, axis=1, keepdims=True)
        aug_ref[start : start + chunk, :] = (x * lax.rsqrt(energy + epsilon)).astype(jnp.bfloat16)

    ids = ids_ref[...]
    label = ids >> (chips.bit_length() - 1)
    shift = ((ids & (tiles - 1)) - lax.axis_index("tile")) & (tiles - 1)
    side = ((ids & (chips - 1)) >> (tiles.bit_length() - 1)) ^ lax.axis_index("chip")
    block = shift * across + side
    key = ((block * labels + label) * rows + iota((1, rows), 1)).astype(jnp.float32)
    base = (block * (labels * rows)).astype(jnp.float32)
    base_shift = (shift * (across * labels * rows)).astype(jnp.float32)
    key_t = jnp.broadcast_to(key, (LANES, rows)).T
    ranks, pooled = [], []
    for start in range(0, rows, LANES):
        here = slice(start, start + LANES)
        smaller = key_t < key[:, here]
        in_block = jnp.where(smaller & (key_t >= base[:, here]), 1.0, 0.0)
        in_shift = jnp.where(smaller & (key_t >= base_shift[:, here]), 1.0, 0.0)
        ranks.append(jnp.sum(in_block, axis=0, keepdims=True))
        pooled.append(jnp.sum(in_shift, axis=0, keepdims=True))
    rank = jnp.concatenate(ranks, axis=1)
    rank_ref[...] = rank
    pooled = jnp.concatenate(pooled, axis=1)

    def apart(shift):
        return shift != size["first"]

    full = (rank >= cap - 1) | (~apart(shift) & (pooled >= pool - across))
    over = jnp.max(jnp.where(full, 1.0, 0.0), axis=1, keepdims=True)
    place = jnp.where(apart(shift), side * cap + rank.astype(jnp.int32), pooled.astype(jnp.int32))
    place = jnp.where(full, -1, place)

    in_block = jnp.where(iota((LANES, rows), 0) == block, 1.0, 0.0).astype(jnp.bfloat16)
    in_label = jnp.where(iota((LANES, rows), 0) == label, 1.0, 0.0).astype(jnp.bfloat16)
    counts = lax.dot_general(
        in_block, in_label, (((1,), (1,)), ((), ())), preferred_element_type=jnp.float32
    )
    counts = jnp.where(iota((LANES, LANES), 1) == FLAG, over, counts)
    aug_ref[rows:, :] = jnp.zeros((LANES, width), jnp.bfloat16)
    aug_ref[rows:, 0:LANES] = counts.astype(jnp.bfloat16)
    lane = iota((1, LANES), 1)
    head_shift = jnp.where(lane < chips, lane >> (across.bit_length() - 1), -1)
    head_side = lane & (across - 1)
    head = jnp.where(
        apart(head_shift), head_side * cap + cap - 1, pool - across + head_side
    )
    shift = jnp.concatenate([shift, head_shift], axis=1)
    place = jnp.concatenate([place, head], axis=1)
    place = jnp.where(place >= 0, shift * PLACES + place, -1)
    place_ref[...] = place
    pool_ref[...] = pick_rows(place, size["first"] * PLACES, pool, aug_ref[...])


def pack_kernel(starts, aug_ref, place_ref, *out_refs):
    aug = aug_ref[...]
    place = place_ref[...]
    for start, out_ref in zip(starts, out_refs):
        out_ref[...] = pick_rows(place, start, out_ref.shape[0], aug)


def regroup_kernel(size, pool_ref, *out_refs):
    across, cap, pool, labels = size["across"], size["cap"], size["pool"], size["labels"]
    rows = pool_ref[...]
    heads = rows[pool - 16 :, 0:LANES].astype(jnp.float32)
    heads = jnp.where(iota((16, LANES), 1) < labels, heads, 0.0)
    counts = jnp.sum(heads, axis=1, keepdims=True).astype(jnp.int32)
    spot = iota((1, pool), 1)
    place = jnp.full((1, pool), -1, jnp.int32)
    begin = jnp.zeros((1, 1), jnp.int32)
    for side in range(across):
        end = begin + counts[16 - across + side : 17 - across + side, :]
        place = jnp.where((spot >= begin) & (spot < end), spot - begin + side * cap, place)
        begin = end
    place = jnp.where(spot >= pool - across, (spot - (pool - across) + 1) * cap - 1, place)
    for side, out_ref in enumerate(out_refs):
        out_ref[...] = pick_rows(place, side * cap, cap, rows)


def sort_kernel(size, *refs):
    across, labels, cap, space = size["across"], size["labels"], size["cap"], size["space"]
    block_refs, (out_ref, place_ref, rows_ref) = refs[:across], refs[across:]
    held = up(cap, ALIGN)
    total = across * held
    for index, ref in enumerate(block_refs):
        if held > cap:
            start = (index + 1) * held - ALIGN
            rows_ref[start : start + ALIGN, :] = jnp.zeros((ALIGN, ref.shape[1]), jnp.bfloat16)
        rows_ref[index * held : index * held + cap, :] = ref[...]
    rows = rows_ref[...]
    spot = iota((LANES, total), 1)
    block = iota((LANES, total), 0)
    head = jnp.where(spot == block * held + cap - 1, 1.0, 0.0).astype(jnp.bfloat16)
    counts = jnp.dot(head, rows[:, 0:LANES], preferred_element_type=jnp.float32)
    flag = jnp.max(counts[:, FLAG:], axis=0, keepdims=True)

    counts_t = counts.T
    lower = jnp.where(iota((LANES, LANES), 0) < iota((LANES, LANES), 1), 1.0, 0.0)
    ahead = exact_dot(counts_t, lower)
    in_block = jnp.zeros((1, LANES), jnp.float32)
    found = jnp.zeros((1, LANES), jnp.float32)
    begin = jnp.zeros((1, 1), jnp.float32)
    lane = iota((1, LANES), 1)
    table = []
    for label in range(labels):
        own = counts_t[label : label + 1, :]
        table.append(begin + ahead[label : label + 1, :] - in_block)
        in_block = in_block + own
        table.append(in_block)
        count = jnp.sum(own, axis=1, keepdims=True)
        high = jnp.floor(count * (1.0 / LANES))
        found = jnp.where(lane == label, high, found)
        found = jnp.where(lane == LOW + label, count - high * LANES, found)
        begin = begin + jnp.floor((count + (ALIGN - 1)) * (1.0 / ALIGN)) * ALIGN
    flag = jnp.maximum(flag, jnp.where(begin > space, 1.0, 0.0))
    found = jnp.where(lane == FLAG, flag, found)
    table.append((lane * held).astype(jnp.float32))
    table.extend([jnp.zeros((1, LANES), jnp.float32)] * (up(len(table), 8) - len(table)))
    table = jnp.concatenate(table, axis=0)

    def places(expand, rank_row):
        where = exact_dot(table, expand)
        rank = rank_row(where)
        place = jnp.full(rank.shape, -1.0, jnp.float32)
        for label in reversed(range(labels)):
            inside = rank < where[2 * label + 1 : 2 * label + 2, :]
            place = jnp.where(inside, where[2 * label : 2 * label + 1, :] + rank, place)
        return place.astype(jnp.int32)

    spot_block = jnp.where((spot >= block * held) & (spot < block * held + cap), 1.0, 0.0)
    spot_row = iota((1, total), 1).astype(jnp.float32)
    place = places(spot_block, lambda where: spot_row - where[2 * labels : 2 * labels + 1, :])
    lanes = place_ref.shape[1]
    rank_row = iota((1, lanes), 1).astype(jnp.float32)
    for index in range(across):
        only = jnp.where(iota((LANES, lanes), 0) == index, 1.0, 0.0)
        place_ref[index : index + 1, :] = places(only, lambda where: rank_row)

    out_ref[space:, :] = jnp.zeros((STEP, out_ref.shape[1]), jnp.bfloat16)
    out_ref[space : space + ALIGN, 0:LANES] = jnp.broadcast_to(found, (ALIGN, LANES)).astype(
        jnp.bfloat16
    )
    for start in range(0, space, ALIGN * 9):
        count = min(ALIGN * 9, space - start)
        out_ref[start : start + count, :] = pick_rows(place, start, count, rows)


def score_kernel(size, *refs):
    across, tiles, labels, space = size["across"], size["tiles"], size["labels"], size["space"]
    pieces = 2 * tiles
    piece_refs, place_refs = refs[:pieces], refs[pieces : pieces + tiles]
    out_ref, rows_ref, total_ref, back_ref, heads_ref, counts_ref, sem = refs[pieces + tiles :]
    lane = iota((1, LANES), 1)
    heads = [ref[space : space + ALIGN, 0:LANES].astype(jnp.float32)[0:1, :] for ref in piece_refs]
    heads_ref[...] = jnp.concatenate(heads, axis=0).astype(jnp.int32)
    copy = pltpu.make_async_copy(heads_ref, counts_ref, sem)
    copy.start()
    copy.wait()
    flag = jnp.int32(0)
    for index in range(pieces):
        flag = jnp.maximum(flag, counts_ref[index, FLAG])

    def aligned(count):
        return (count + (ALIGN - 1)) & -ALIGN

    runs, ends = [], []
    begin = jnp.int32(0)
    source = [jnp.int32(0)] * pieces
    many = jnp.bool_(False)
    for label in range(labels):
        runs.append([])
        for index in range(pieces):
            count = counts_ref[index, label] * LANES + counts_ref[index, LOW + label]
            count = jnp.clip(count, 0, space - source[index])
            runs[label].append((source[index], begin, count))
            many = many | (count > STEP)
            source[index] = source[index] + aligned(count)
            begin = begin + aligned(count)
        ends.append(begin)

    def span(start, step, size):
        return pl.ds(pl.multiple_of(start + step * size, ALIGN), size)

    def gather(index, src, dst, step):
        rows_ref[span(dst, step, STEP), :] = piece_refs[index][span(src, step, STEP), :]

    def repeat(first, end, act):
        def once(step, carry):
            act(step)
            return carry

        lax.fori_loop(first, end, once, 0)

    def cover(count, size):
        return (count + size - 1) // size

    for label in range(labels):
        for index, (src, dst, count) in enumerate(runs[label]):
            gather(index, src, dst, 0)

    @pl.when(many)
    def _():
        for label in range(labels):
            for index, (src, dst, count) in enumerate(runs[label]):
                repeat(0, cover(count, STEP), functools.partial(gather, index, src, dst))

    def window(label, row, column):
        left = rows_ref[span(row, 0, LEFT), :]
        right = rows_ref[span(column, 0, RIGHT), :]
        scores = lax.dot_general(
            left, right, (((1,), (1,)), ((), ())), preferred_element_type=jnp.float32
        )
        at = iota((1, RIGHT), 1) + column
        valid = at < 0
        for _, low, count in runs[label]:
            valid = valid | ((at >= low) & (at < low + count))
        at = jnp.where(valid, at, -1)
        itself = iota((LEFT, RIGHT), 0) + row
        counted = (at >= 0) & (at != itself)
        terms = jnp.where(counted, jnp.exp(sharpness * scores), 0.0)
        sums = jnp.sum(terms, axis=1, keepdims=True)
        return jnp.broadcast_to(sums, (LEFT, LANES))

    wide = jnp.bool_(False)
    for label in range(labels):
        first, own_end = runs[label][0][1], runs[label][tiles][1]
        total_ref[label, 0:LEFT, :] = window(label, first, first)
        wide = wide | (own_end - first > LEFT) | (ends[label] - first > RIGHT)

    @pl.when(wide)
    def _():
        for label in range(labels):
            first, own_end = runs[label][0][1], runs[label][tiles][1]
            across_steps = cover(ends[label] - first, RIGHT)

            def add(strip, step, label=label, first=first):
                row, column = first + strip * LEFT, first + step * RIGHT
                total_ref[label, span(0, strip, LEFT), :] += window(label, row, column)

            def strips(strip, label=label, add=add, across_steps=across_steps):
                total_ref[label, span(0, strip, LEFT), :] = jnp.zeros((LEFT, LANES), jnp.float32)
                repeat(0, across_steps, functools.partial(add, strip))

            repeat(1, across_steps, functools.partial(add, 0))
            repeat(1, cover(own_end - first, LEFT), strips)

    def scatter(label, index, step):
        src, dst, _ = runs[label][index]
        back_ref[index, span(src, step, STEP), :] = total_ref[
            label, span(dst - runs[label][0][1], step, STEP), :
        ]

    for index in range(tiles):
        for label in range(labels):
            scatter(label, index, 0)

    @pl.when(many)
    def _():
        for index in range(tiles):
            for label in range(labels):
                count = runs[label][index][2]
                repeat(0, cover(count, STEP), functools.partial(scatter, label, index))

    lanes = out_ref.shape[1]
    row = iota((space, LANES), 0)
    chip, tile = lax.axis_index("chip"), lax.axis_index("tile")
    for shift in range(tiles):
        for side in range(across):
            home = (chip ^ side) * tiles + ((tile - shift) & (tiles - 1))
            for start in range(0, lanes, LANES):
                place = place_refs[shift][side : side + 1, start : start + LANES]
                value = jnp.sum(
                    jnp.where(row == place, back_ref[shift, 0:space, :], 0.0),
                    axis=0,
                    keepdims=True,
                )
                if start + LANES == lanes:
                    value = jnp.where(lane == FLAG, flag.astype(jnp.float32), value)
                out_ref[pl.ds(home, 1), start : start + LANES] = value


def unpack_kernel(chips, ret_ref, ids_ref, rank_ref, out_ref, flag_ref):
    rows = ids_ref.shape[1]
    lanes = ret_ref.shape[1]
    values = ret_ref[...]
    flag = jnp.max(values[:, lanes - 1 :], axis=0, keepdims=True)
    flag_ref[...] = jnp.broadcast_to(flag, flag_ref.shape).astype(jnp.int32)
    chip = ids_ref[...] & (chips - 1)
    rank = rank_ref[...].astype(jnp.int32)
    at_rank = jnp.where(iota((lanes, rows), 0) == rank, 1.0, 0.0)
    found = exact_dot(values, at_rank)
    total = jnp.sum(jnp.where(iota((chips, rows), 0) == chip, found, 0.0), axis=0, keepdims=True)
    out_ref[...] = jnp.log(1.0 + total)


def call(kernel, name, out_shape, inputs, **options):
    vmem = pl.BlockSpec(memory_space=pltpu.VMEM)
    return pl.pallas_call(
        kernel,
        out_shape=out_shape,
        in_specs=[vmem] * len(inputs),
        out_specs=jax.tree.map(lambda _: vmem, out_shape),
        compiler_params=pltpu.CompilerParams(vmem_limit_bytes=VMEM_BYTES),
        name=name,
        **options,
    )(*inputs)


def body(embeddings, cluster_ids):
    rows, width = embeddings.shape
    across, tiles = lax.axis_size("chip"), lax.axis_size("tile")
    chips = across * tiles
    labels = KG * across * lax.axis_size("core") // chips
    cap = up(room(rows, chips, 5.0) + 1, 8)
    pool = up(room(rows, tiles, 4.25) + across, ALIGN)
    space = up(room(rows, tiles, 4.75) + labels * (ALIGN - 4), ALIGN)
    order = sorted(range(1, tiles), key=lambda shift: (-min(shift, tiles - shift), shift))
    size = dict(
        chips=chips, across=across, tiles=tiles, labels=labels, cap=cap, pool=pool, space=space,
        first=order[0],
    )
    lanes = up(cap + 1, LANES)
    shape = jax.ShapeDtypeStruct

    ids_row = cluster_ids.reshape(1, rows)
    pool_rows, aug, slots, rank = call(
        functools.partial(plan_kernel, size),
        "plan",
        [
            shape((pool, width), jnp.bfloat16),
            shape((rows + LANES, width), jnp.bfloat16),
            shape((1, rows + LANES), jnp.int32),
            shape((1, rows), jnp.float32),
        ],
        [embeddings, ids_row],
    )

    def pack(shift, count, step):
        return call(
            functools.partial(
                pack_kernel, [shift * PLACES + index * step for index in range(count)]
            ),
            "pack",
            [shape((step, width), jnp.bfloat16)] * count,
            [aug, slots],
        )

    def along(shift):
        return [(z, (z + shift) % tiles) for z in range(tiles)]

    def over(side):
        return [(a, a ^ side) for a in range(across)]

    def after(value, *others):
        return lax.optimization_barrier((value, others))[0]

    def send_across(blocks):
        return [blocks[0]] + [
            lax.ppermute(blocks[side], "chip", over(side)) for side in range(1, across)
        ]

    def send_far(blocks, shift, side):
        route = [(a * tiles + z, b * tiles + y) for a, b in over(side) for z, y in along(shift)]
        return lax.ppermute(blocks[side], ("chip", "tile"), route)

    swap = [(0, 1), (1, 0)]
    own, other, places = {}, {}, {}

    def finish(shift, arrived):
        own[shift], places[shift] = call(
            functools.partial(sort_kernel, size),
            "sort",
            [
                shape((space + STEP, width), jnp.bfloat16),
                shape((across, lanes), jnp.int32),
            ],
            arrived,
            scratch_shapes=[pltpu.VMEM((across * up(cap, ALIGN), width), jnp.bfloat16)],
        )
        other[shift] = lax.ppermute(own[shift], "core", swap)

    pooled = lax.ppermute(pool_rows, "tile", along(order[0]))
    near = send_across(pack(0, across, cap))
    finish(0, near)
    packed = {shift: pack(shift, across, cap) for shift in order[1:]}
    ready = [block for shift in order[1:] for block in packed[shift]]
    regrouped = call(
        functools.partial(regroup_kernel, size),
        "regroup",
        [shape((cap, width), jnp.bfloat16)] * across,
        [after(pooled, *near, *ready)],
    )
    passed = send_across(regrouped)
    finish(order[0], passed)
    for shift in order[1:]:
        blocks = after(packed[shift], pooled)
        finish(shift, [send_far(blocks, shift, side) for side in range(across)])
    own, other, places = (
        [found[shift] for shift in range(tiles)] for found in (own, other, places)
    )
    room_own = tiles * space + LEFT + STEP
    totals = call(
        functools.partial(score_kernel, size),
        "score",
        shape((chips, lanes), jnp.float32),
        [*own, *other, *places],
        scratch_shapes=[
            pltpu.VMEM((2 * tiles * space + LEFT + RIGHT, width), jnp.bfloat16),
            pltpu.VMEM((labels, room_own, LANES), jnp.float32),
            pltpu.VMEM((tiles, space + STEP, LANES), jnp.float32),
            pltpu.VMEM((2 * tiles, LANES), jnp.int32),
            pltpu.SMEM((2 * tiles, LANES), jnp.int32),
            pltpu.SemaphoreType.DMA,
        ],
    )
    returned = lax.all_to_all(totals, ("chip", "tile"), split_axis=0, concat_axis=0, tiled=True)
    result, flag = call(
        functools.partial(unpack_kernel, chips),
        "unpack",
        [shape((1, rows), jnp.float32), shape((8, LANES), jnp.int32)],
        [returned, ids_row, rank],
    )
    return lax.cond(
        flag[0, 0] > 0,
        lambda: general_plan(embeddings, cluster_ids),
        lambda: result.reshape(rows),
    )


def solution(mesh):
    shards = mesh.shape["shard"]
    tiles = mesh.shape["tile"]
    split = Mesh(mesh.devices.reshape(shards // 2, 2, tiles), ("chip", "core", "tile"))
    rows = ("chip", "core", "tile")
    return jax.shard_map(
        body, mesh=split, in_specs=(P(rows, None), P(rows)), out_specs=P(rows), check_vma=False
    )
```

```python
import functools
import math

import jax
import jax.numpy as jnp
from jax import lax
from jax.experimental import pallas as pl
from jax.experimental.pallas import tpu as pltpu
from jax.sharding import Mesh
from jax.sharding import PartitionSpec as P

KG = 16


sharpness = 30.0
epsilon = 1e-06

MIB = 1024 * 1024
LANES = 128
FLAG = LANES - 1
LOW = LANES // 2
ALIGN = 16
STEP = 96
LEFT = 256
RIGHT = 512
PLACES = 1 << 16


def unit_rows(embeddings):
    energy = jnp.sum(embeddings * embeddings, axis=1, keepdims=True)
    return (embeddings * lax.rsqrt(energy + epsilon)).astype(jnp.bfloat16)


def row_sums(left, left_labels, right, right_labels, same_rows):
    count = left.shape[0]
    block = min(512, count)
    blocks = count // block

    def step(start, items):
        rows_block, labels_block = items
        scores = lax.dot_general(
            rows_block, right, (((1,), (1,)), ((), ())), preferred_element_type=jnp.float32
        )
        same = (labels_block[:, None] == right_labels[None, :]) & (labels_block[:, None] >= 0)
        itself = (start + jnp.arange(block))[:, None] == jnp.arange(count)[None, :]
        same = same & ~(itself & same_rows)
        terms = jnp.where(same, jnp.exp(sharpness * scores), 0.0)
        return (start + block, jnp.sum(terms, axis=1))

    _, totals = lax.scan(
        step,
        jnp.int32(0),
        (left.reshape(blocks, block, left.shape[1]), left_labels.reshape(blocks, block)),
    )
    return totals.reshape(count)


def general_plan(embeddings, cluster_ids):
    shard_axes = ("chip", "core")
    local_rows = embeddings.shape[0]
    shards = lax.axis_size("chip") * lax.axis_size("core")
    tiles = lax.axis_size("tile")
    capacity = 2 * local_rows // shards
    slot_count = shards * capacity
    unit = unit_rows(embeddings)
    owner = cluster_ids // KG
    onehot = (owner[:, None] == jnp.arange(shards, dtype=jnp.int32)[None, :]).astype(jnp.int32)
    ranks = jnp.sum((jnp.cumsum(onehot, axis=0) - 1) * onehot, axis=1)
    slots = owner * capacity + ranks
    outgoing = jnp.zeros((slot_count, unit.shape[1]), jnp.bfloat16).at[slots].set(unit)
    outgoing_labels = jnp.full((slot_count,), -1, jnp.int32).at[slots].set(cluster_ids)
    owned = lax.all_to_all(outgoing, shard_axes, split_axis=0, concat_axis=0, tiled=True)
    owned_labels = lax.all_to_all(
        outgoing_labels, shard_axes, split_axis=0, concat_axis=0, tiled=True
    )
    around = [(tile, (tile + 1) % tiles) for tile in range(tiles)]

    def visit(step, state):
        totals, rows, labels = state
        totals = totals + row_sums(owned, owned_labels, rows, labels, step == 0)
        return (totals, lax.ppermute(rows, "tile", around), lax.ppermute(labels, "tile", around))

    totals, _, _ = lax.fori_loop(
        0, tiles, visit, (jnp.zeros((slot_count,), jnp.float32), owned, owned_labels)
    )
    returned = lax.all_to_all(totals, shard_axes, split_axis=0, concat_axis=0, tiled=True)
    return jnp.log(1.0 + returned[slots])


def up(value, multiple):
    return -(-value // multiple) * multiple


def room(count, parts, sigmas):
    mean = count / parts
    return math.ceil(mean + sigmas * (mean * (1 - 1 / parts)) ** 0.5)


def iota(shape, axis):
    return lax.broadcasted_iota(jnp.int32, shape, axis)


def exact_dot(left, right):
    return jnp.dot(
        left, right, precision=lax.Precision.HIGHEST, preferred_element_type=jnp.float32
    )


def pick_rows(places, start, count, rows):
    pick = jnp.where(iota((count, places.shape[1]), 0) + start == places, 1.0, 0.0)
    return jnp.dot(pick.astype(jnp.bfloat16), rows, preferred_element_type=jnp.float32).astype(
        jnp.bfloat16
    )


def plan_kernel(size, emb_ref, ids_ref, pool_ref, aug_ref, place_ref, rank_ref):
    rows, width = emb_ref.shape
    chips, labels, cap, pool = size["chips"], size["labels"], size["cap"], size["pool"]
    across, tiles = size["across"], size["tiles"]
    chunk = 256
    for start in range(0, rows, chunk):
        x = emb_ref[start : start + chunk, :]
        energy = jnp.sum(x * x, axis=1, keepdims=True)
        aug_ref[start : start + chunk, :] = (x * lax.rsqrt(energy + epsilon)).astype(jnp.bfloat16)

    ids = ids_ref[...]
    label = ids >> (chips.bit_length() - 1)
    shift = ((ids & (tiles - 1)) - lax.axis_index("tile")) & (tiles - 1)
    side = ((ids & (chips - 1)) >> (tiles.bit_length() - 1)) ^ lax.axis_index("chip")
    block = shift * across + side
    key = ((block * labels + label) * rows + iota((1, rows), 1)).astype(jnp.float32)
    base = (block * (labels * rows)).astype(jnp.float32)
    base_shift = (shift * (across * labels * rows)).astype(jnp.float32)
    key_t = jnp.broadcast_to(key, (LANES, rows)).T
    ranks, pooled = [], []
    for start in range(0, rows, LANES):
        here = slice(start, start + LANES)
        smaller = key_t < key[:, here]
        in_block = jnp.where(smaller & (key_t >= base[:, here]), 1.0, 0.0)
        in_shift = jnp.where(smaller & (key_t >= base_shift[:, here]), 1.0, 0.0)
        ranks.append(jnp.sum(in_block, axis=0, keepdims=True))
        pooled.append(jnp.sum(in_shift, axis=0, keepdims=True))
    rank = jnp.concatenate(ranks, axis=1)
    rank_ref[...] = rank
    pooled = jnp.concatenate(pooled, axis=1)

    def apart(shift):
        return shift != size["first"]

    full = (rank >= cap - 1) | (~apart(shift) & (pooled >= pool - across))
    over = jnp.max(jnp.where(full, 1.0, 0.0), axis=1, keepdims=True)
    place = jnp.where(apart(shift), side * cap + rank.astype(jnp.int32), pooled.astype(jnp.int32))
    place = jnp.where(full, -1, place)

    in_block = jnp.where(iota((LANES, rows), 0) == block, 1.0, 0.0).astype(jnp.bfloat16)
    in_label = jnp.where(iota((LANES, rows), 0) == label, 1.0, 0.0).astype(jnp.bfloat16)
    counts = lax.dot_general(
        in_block, in_label, (((1,), (1,)), ((), ())), preferred_element_type=jnp.float32
    )
    counts = jnp.where(iota((LANES, LANES), 1) == FLAG, over, counts)
    aug_ref[rows:, :] = jnp.zeros((LANES, width), jnp.bfloat16)
    aug_ref[rows:, 0:LANES] = counts.astype(jnp.bfloat16)
    lane = iota((1, LANES), 1)
    head_shift = jnp.where(lane < chips, lane >> (across.bit_length() - 1), -1)
    head_side = lane & (across - 1)
    head = jnp.where(
        apart(head_shift), head_side * cap + cap - 1, pool - across + head_side
    )
    shift = jnp.concatenate([shift, head_shift], axis=1)
    place = jnp.concatenate([place, head], axis=1)
    place = jnp.where(place >= 0, shift * PLACES + place, -1)
    place_ref[...] = place
    pool_ref[...] = pick_rows(place, size["first"] * PLACES, pool, aug_ref[...])


def pack_kernel(starts, aug_ref, place_ref, *out_refs):
    aug = aug_ref[...]
    place = place_ref[...]
    for start, out_ref in zip(starts, out_refs):
        out_ref[...] = pick_rows(place, start, out_ref.shape[0], aug)


def regroup_kernel(size, pool_ref, *out_refs):
    across, cap, pool, labels = size["across"], size["cap"], size["pool"], size["labels"]
    rows = pool_ref[...]
    heads = rows[pool - 16 :, 0:LANES].astype(jnp.float32)
    heads = jnp.where(iota((16, LANES), 1) < labels, heads, 0.0)
    counts = jnp.sum(heads, axis=1, keepdims=True).astype(jnp.int32)
    spot = iota((1, pool), 1)
    place = jnp.full((1, pool), -1, jnp.int32)
    begin = jnp.zeros((1, 1), jnp.int32)
    for side in range(across):
        end = begin + counts[16 - across + side : 17 - across + side, :]
        place = jnp.where((spot >= begin) & (spot < end), spot - begin + side * cap, place)
        begin = end
    place = jnp.where(spot >= pool - across, (spot - (pool - across) + 1) * cap - 1, place)
    for side, out_ref in enumerate(out_refs):
        out_ref[...] = pick_rows(place, side * cap, cap, rows)


def sort_kernel(size, *refs):
    across, labels, cap, space = size["across"], size["labels"], size["cap"], size["space"]
    block_refs, (out_ref, place_ref, rows_ref) = refs[:across], refs[across:]
    held = up(cap, ALIGN)
    total = across * held
    for index, ref in enumerate(block_refs):
        if held > cap:
            start = (index + 1) * held - ALIGN
            rows_ref[start : start + ALIGN, :] = jnp.zeros((ALIGN, ref.shape[1]), jnp.bfloat16)
        rows_ref[index * held : index * held + cap, :] = ref[...]
    rows = rows_ref[...]
    spot = iota((LANES, total), 1)
    block = iota((LANES, total), 0)
    head = jnp.where(spot == block * held + cap - 1, 1.0, 0.0).astype(jnp.bfloat16)
    counts = jnp.dot(head, rows[:, 0:LANES], preferred_element_type=jnp.float32)
    flag = jnp.max(counts[:, FLAG:], axis=0, keepdims=True)

    counts_t = counts.T
    lower = jnp.where(iota((LANES, LANES), 0) < iota((LANES, LANES), 1), 1.0, 0.0)
    ahead = exact_dot(counts_t, lower)
    in_block = jnp.zeros((1, LANES), jnp.float32)
    found = jnp.zeros((1, LANES), jnp.float32)
    begin = jnp.zeros((1, 1), jnp.float32)
    lane = iota((1, LANES), 1)
    table = []
    for label in range(labels):
        own = counts_t[label : label + 1, :]
        table.append(begin + ahead[label : label + 1, :] - in_block)
        in_block = in_block + own
        table.append(in_block)
        count = jnp.sum(own, axis=1, keepdims=True)
        high = jnp.floor(count * (1.0 / LANES))
        found = jnp.where(lane == label, high, found)
        found = jnp.where(lane == LOW + label, count - high * LANES, found)
        begin = begin + jnp.floor((count + (ALIGN - 1)) * (1.0 / ALIGN)) * ALIGN
    flag = jnp.maximum(flag, jnp.where(begin > space, 1.0, 0.0))
    found = jnp.where(lane == FLAG, flag, found)
    table.append((lane * held).astype(jnp.float32))
    table.extend([jnp.zeros((1, LANES), jnp.float32)] * (up(len(table), 8) - len(table)))
    table = jnp.concatenate(table, axis=0)

    def places(expand, rank_row):
        where = exact_dot(table, expand)
        rank = rank_row(where)
        place = jnp.full(rank.shape, -1.0, jnp.float32)
        for label in reversed(range(labels)):
            inside = rank < where[2 * label + 1 : 2 * label + 2, :]
            place = jnp.where(inside, where[2 * label : 2 * label + 1, :] + rank, place)
        return place.astype(jnp.int32)

    spot_block = jnp.where((spot >= block * held) & (spot < block * held + cap), 1.0, 0.0)
    spot_row = iota((1, total), 1).astype(jnp.float32)
    place = places(spot_block, lambda where: spot_row - where[2 * labels : 2 * labels + 1, :])
    lanes = place_ref.shape[1]
    rank_row = iota((1, lanes), 1).astype(jnp.float32)
    for index in range(across):
        only = jnp.where(iota((LANES, lanes), 0) == index, 1.0, 0.0)
        place_ref[index : index + 1, :] = places(only, lambda where: rank_row)

    out_ref[space:, :] = jnp.zeros((STEP, out_ref.shape[1]), jnp.bfloat16)
    out_ref[space : space + ALIGN, 0:LANES] = jnp.broadcast_to(found, (ALIGN, LANES)).astype(
        jnp.bfloat16
    )
    for start in range(0, space, ALIGN * 9):
        count = min(ALIGN * 9, space - start)
        out_ref[start : start + count, :] = pick_rows(place, start, count, rows)


def score_kernel(size, *refs):
    across, tiles, labels, space = size["across"], size["tiles"], size["labels"], size["space"]
    pieces = 2 * tiles
    piece_refs, place_refs = refs[:pieces], refs[pieces : pieces + tiles]
    out_ref, rows_ref, total_ref, back_ref, heads_ref, counts_ref, sem = refs[pieces + tiles :]
    lane = iota((1, LANES), 1)
    heads = [ref[space : space + ALIGN, 0:LANES].astype(jnp.float32)[0:1, :] for ref in piece_refs]
    heads_ref[...] = jnp.concatenate(heads, axis=0).astype(jnp.int32)
    copy = pltpu.make_async_copy(heads_ref, counts_ref, sem)
    copy.start()
    copy.wait()
    flag = jnp.int32(0)
    for index in range(pieces):
        flag = jnp.maximum(flag, counts_ref[index, FLAG])

    def aligned(count):
        return (count + (ALIGN - 1)) & -ALIGN

    runs, ends = [], []
    begin = jnp.int32(0)
    source = [jnp.int32(0)] * pieces
    many = jnp.bool_(False)
    for label in range(labels):
        runs.append([])
        for index in range(pieces):
            count = counts_ref[index, label] * LANES + counts_ref[index, LOW + label]
            count = jnp.clip(count, 0, space - source[index])
            runs[label].append((source[index], begin, count))
            many = many | (count > STEP)
            source[index] = source[index] + aligned(count)
            begin = begin + aligned(count)
        ends.append(begin)

    def span(start, step, size):
        return pl.ds(pl.multiple_of(start + step * size, ALIGN), size)

    def gather(index, src, dst, step):
        rows_ref[span(dst, step, STEP), :] = piece_refs[index][span(src, step, STEP), :]

    def repeat(first, end, act):
        def once(step, carry):
            act(step)
            return carry

        lax.fori_loop(first, end, once, 0)

    def cover(count, size):
        return (count + size - 1) // size

    for label in range(labels):
        for index, (src, dst, count) in enumerate(runs[label]):
            gather(index, src, dst, 0)

    @pl.when(many)
    def _():
        for label in range(labels):
            for index, (src, dst, count) in enumerate(runs[label]):
                repeat(0, cover(count, STEP), functools.partial(gather, index, src, dst))

    def window(label, row, column):
        left = rows_ref[span(row, 0, LEFT), :]
        right = rows_ref[span(column, 0, RIGHT), :]
        scores = lax.dot_general(
            left, right, (((1,), (1,)), ((), ())), preferred_element_type=jnp.float32
        )
        at = iota((1, RIGHT), 1) + column
        valid = at < 0
        for _, low, count in runs[label]:
            valid = valid | ((at >= low) & (at < low + count))
        at = jnp.where(valid, at, -1)
        itself = iota((LEFT, RIGHT), 0) + row
        counted = (at >= 0) & (at != itself)
        terms = jnp.where(counted, jnp.exp(sharpness * scores), 0.0)
        sums = jnp.sum(terms, axis=1, keepdims=True)
        return jnp.broadcast_to(sums, (LEFT, LANES))

    wide = jnp.bool_(False)
    for label in range(labels):
        first, own_end = runs[label][0][1], runs[label][tiles][1]
        total_ref[label, 0:LEFT, :] = window(label, first, first)
        wide = wide | (own_end - first > LEFT) | (ends[label] - first > RIGHT)

    @pl.when(wide)
    def _():
        for label in range(labels):
            first, own_end = runs[label][0][1], runs[label][tiles][1]
            across_steps = cover(ends[label] - first, RIGHT)

            def add(strip, step, label=label, first=first):
                row, column = first + strip * LEFT, first + step * RIGHT
                total_ref[label, span(0, strip, LEFT), :] += window(label, row, column)

            def strips(strip, label=label, add=add, across_steps=across_steps):
                total_ref[label, span(0, strip, LEFT), :] = jnp.zeros((LEFT, LANES), jnp.float32)
                repeat(0, across_steps, functools.partial(add, strip))

            repeat(1, across_steps, functools.partial(add, 0))
            repeat(1, cover(own_end - first, LEFT), strips)

    def scatter(label, index, step):
        src, dst, _ = runs[label][index]
        back_ref[index, span(src, step, STEP), :] = total_ref[
            label, span(dst - runs[label][0][1], step, STEP), :
        ]

    for index in range(tiles):
        for label in range(labels):
            scatter(label, index, 0)

    @pl.when(many)
    def _():
        for index in range(tiles):
            for label in range(labels):
                count = runs[label][index][2]
                repeat(0, cover(count, STEP), functools.partial(scatter, label, index))

    lanes = out_ref.shape[1]
    row = iota((space, LANES), 0)
    chip, tile = lax.axis_index("chip"), lax.axis_index("tile")
    for shift in range(tiles):
        for side in range(across):
            home = (chip ^ side) * tiles + ((tile - shift) & (tiles - 1))
            for start in range(0, lanes, LANES):
                place = place_refs[shift][side : side + 1, start : start + LANES]
                value = jnp.sum(
                    jnp.where(row == place, back_ref[shift, 0:space, :], 0.0),
                    axis=0,
                    keepdims=True,
                )
                if start + LANES == lanes:
                    value = jnp.where(lane == FLAG, flag.astype(jnp.float32), value)
                out_ref[pl.ds(home, 1), start : start + LANES] = value


def unpack_kernel(chips, ret_ref, ids_ref, rank_ref, out_ref, flag_ref):
    rows = ids_ref.shape[1]
    lanes = ret_ref.shape[1]
    values = ret_ref[...]
    flag = jnp.max(values[:, lanes - 1 :], axis=0, keepdims=True)
    flag_ref[0, 0] = jnp.sum(flag).astype(jnp.int32)
    chip = ids_ref[...] & (chips - 1)
    rank = rank_ref[...].astype(jnp.int32)
    at_rank = jnp.where(iota((lanes, rows), 0) == rank, 1.0, 0.0)
    found = exact_dot(values, at_rank)
    total = jnp.sum(jnp.where(iota((chips, rows), 0) == chip, found, 0.0), axis=0, keepdims=True)
    out_ref[...] = jnp.log(1.0 + total)


def call(kernel, name, out_shape, inputs, vmem_mib=12, **options):
    vmem = pl.BlockSpec(memory_space=pltpu.VMEM)
    return pl.pallas_call(
        kernel,
        out_shape=out_shape,
        in_specs=[vmem] * len(inputs),
        out_specs=options.pop("out_specs", jax.tree.map(lambda _: vmem, out_shape)),
        compiler_params=pltpu.CompilerParams(vmem_limit_bytes=vmem_mib * MIB),
        name=name,
        **options,
    )(*inputs)


def body(embeddings, cluster_ids):
    rows, width = embeddings.shape
    across, tiles = lax.axis_size("chip"), lax.axis_size("tile")
    chips = across * tiles
    labels = KG * across * lax.axis_size("core") // chips
    cap = up(room(rows, chips, 5.0) + 1, 8)
    pool = up(room(rows, tiles, 4.25) + across, ALIGN)
    space = up(room(rows, tiles, 4.75) + labels * (ALIGN - 4), ALIGN)
    order = sorted(range(1, tiles), key=lambda shift: (-min(shift, tiles - shift), shift))
    size = dict(
        chips=chips, across=across, tiles=tiles, labels=labels, cap=cap, pool=pool, space=space,
        first=order[0],
    )
    lanes = up(cap + 1, LANES)
    shape = jax.ShapeDtypeStruct

    ids_row = cluster_ids.reshape(1, rows)
    pool_rows, aug, slots, rank = call(
        functools.partial(plan_kernel, size),
        "plan",
        [
            shape((pool, width), jnp.bfloat16),
            shape((rows + LANES, width), jnp.bfloat16),
            shape((1, rows + LANES), jnp.int32),
            shape((1, rows), jnp.float32),
        ],
        [embeddings, ids_row],
    )

    near_and_far = [0, *order[1:]]
    blocks = call(
        functools.partial(
            pack_kernel,
            [shift * PLACES + side * cap for shift in near_and_far for side in range(across)],
        ),
        "pack",
        [shape((cap, width), jnp.bfloat16)] * (across * len(near_and_far)),
        [aug, slots],
    )
    packed = {
        shift: blocks[place * across : (place + 1) * across]
        for place, shift in enumerate(near_and_far)
    }

    def along(shift):
        return [(z, (z + shift) % tiles) for z in range(tiles)]

    def over(side):
        return [(a, a ^ side) for a in range(across)]

    def after(value, *others):
        return lax.optimization_barrier((value, others))[0]

    def send_across(blocks):
        return [blocks[0]] + [
            lax.ppermute(blocks[side], "chip", over(side)) for side in range(1, across)
        ]

    def send_far(blocks, shift, side):
        route = [(a * tiles + z, b * tiles + y) for a, b in over(side) for z, y in along(shift)]
        return lax.ppermute(blocks[side], ("chip", "tile"), route)

    swap = [(0, 1), (1, 0)]
    own, other, places = {}, {}, {}

    def finish(shift, arrived):
        own[shift], places[shift] = call(
            functools.partial(sort_kernel, size),
            "sort",
            [
                shape((space + STEP, width), jnp.bfloat16),
                shape((across, lanes), jnp.int32),
            ],
            arrived,
            scratch_shapes=[pltpu.VMEM((across * up(cap, ALIGN), width), jnp.bfloat16)],
        )
        other[shift] = lax.ppermute(own[shift], "core", swap)

    pooled = lax.ppermute(pool_rows, "tile", along(order[0]))
    near = send_across(packed[0])
    finish(0, near)
    regrouped = call(
        functools.partial(regroup_kernel, size),
        "regroup",
        [shape((cap, width), jnp.bfloat16)] * across,
        [after(pooled, *near)],
    )
    passed = send_across(regrouped)
    finish(order[0], passed)
    for shift in order[1:]:
        blocks = after(packed[shift], pooled)
        finish(shift, [send_far(blocks, shift, side) for side in range(across)])
    own, other, places = (
        [found[shift] for shift in range(tiles)] for found in (own, other, places)
    )
    room_own = tiles * space + LEFT + STEP
    totals = call(
        functools.partial(score_kernel, size),
        "score",
        shape((chips, lanes), jnp.float32),
        [*own, *other, *places],
        vmem_mib=26,
        scratch_shapes=[
            pltpu.VMEM((2 * tiles * space + LEFT + RIGHT, width), jnp.bfloat16),
            pltpu.VMEM((labels, room_own, LANES), jnp.float32),
            pltpu.VMEM((tiles, space + STEP, LANES), jnp.float32),
            pltpu.VMEM((2 * tiles, LANES), jnp.int32),
            pltpu.SMEM((2 * tiles, LANES), jnp.int32),
            pltpu.SemaphoreType.DMA,
        ],
    )
    returned = lax.all_to_all(totals, ("chip", "tile"), split_axis=0, concat_axis=0, tiled=True)
    result, flag = call(
        functools.partial(unpack_kernel, chips),
        "unpack",
        [shape((1, rows), jnp.float32), shape((1, 1), jnp.int32)],
        [returned, ids_row, rank],
        out_specs=[
            pl.BlockSpec(memory_space=pltpu.VMEM),
            pl.BlockSpec(memory_space=pltpu.SMEM),
        ],
    )
    return lax.cond(
        flag.reshape(()) > 0,
        lambda: general_plan(embeddings, cluster_ids),
        lambda: result.reshape(rows),
    )


def solution(mesh):
    shards = mesh.shape["shard"]
    tiles = mesh.shape["tile"]
    split = Mesh(mesh.devices.reshape(shards // 2, 2, tiles), ("chip", "core", "tile"))
    rows = ("chip", "core", "tile")
    return jax.shard_map(
        body, mesh=split, in_specs=(P(rows, None), P(rows)), out_specs=P(rows), check_vma=False
    )
```

```python
import functools
import math

import jax
import jax.numpy as jnp
from jax import lax
from jax.experimental import pallas as pl
from jax.experimental.pallas import tpu as pltpu
from jax.sharding import Mesh
from jax.sharding import PartitionSpec as P

KG = 16


sharpness = 30.0
epsilon = 1e-06

MIB = 1024 * 1024
LANES = 128
FLAG = LANES - 1
LOW = LANES // 2
ALIGN = 16
STEP = 96
LEFT = 256
RIGHT = 512
PLACES = 1 << 16


def unit_rows(embeddings):
    energy = jnp.sum(embeddings * embeddings, axis=1, keepdims=True)
    return (embeddings * lax.rsqrt(energy + epsilon)).astype(jnp.bfloat16)


def row_sums(left, left_labels, right, right_labels, same_rows):
    count = left.shape[0]
    block = min(512, count)
    blocks = count // block

    def step(start, items):
        rows_block, labels_block = items
        scores = lax.dot_general(
            rows_block, right, (((1,), (1,)), ((), ())), preferred_element_type=jnp.float32
        )
        same = (labels_block[:, None] == right_labels[None, :]) & (labels_block[:, None] >= 0)
        itself = (start + jnp.arange(block))[:, None] == jnp.arange(count)[None, :]
        same = same & ~(itself & same_rows)
        terms = jnp.where(same, jnp.exp(sharpness * scores), 0.0)
        return (start + block, jnp.sum(terms, axis=1))

    _, totals = lax.scan(
        step,
        jnp.int32(0),
        (left.reshape(blocks, block, left.shape[1]), left_labels.reshape(blocks, block)),
    )
    return totals.reshape(count)


def general_plan(embeddings, cluster_ids):
    shard_axes = ("chip", "core")
    local_rows = embeddings.shape[0]
    shards = lax.axis_size("chip") * lax.axis_size("core")
    tiles = lax.axis_size("tile")
    capacity = 2 * local_rows // shards
    slot_count = shards * capacity
    unit = unit_rows(embeddings)
    owner = cluster_ids // KG
    onehot = (owner[:, None] == jnp.arange(shards, dtype=jnp.int32)[None, :]).astype(jnp.int32)
    ranks = jnp.sum((jnp.cumsum(onehot, axis=0) - 1) * onehot, axis=1)
    slots = owner * capacity + ranks
    outgoing = jnp.zeros((slot_count, unit.shape[1]), jnp.bfloat16).at[slots].set(unit)
    outgoing_labels = jnp.full((slot_count,), -1, jnp.int32).at[slots].set(cluster_ids)
    owned = lax.all_to_all(outgoing, shard_axes, split_axis=0, concat_axis=0, tiled=True)
    owned_labels = lax.all_to_all(
        outgoing_labels, shard_axes, split_axis=0, concat_axis=0, tiled=True
    )
    around = [(tile, (tile + 1) % tiles) for tile in range(tiles)]

    def visit(step, state):
        totals, rows, labels = state
        totals = totals + row_sums(owned, owned_labels, rows, labels, step == 0)
        return (totals, lax.ppermute(rows, "tile", around), lax.ppermute(labels, "tile", around))

    totals, _, _ = lax.fori_loop(
        0, tiles, visit, (jnp.zeros((slot_count,), jnp.float32), owned, owned_labels)
    )
    returned = lax.all_to_all(totals, shard_axes, split_axis=0, concat_axis=0, tiled=True)
    return jnp.log(1.0 + returned[slots])


def up(value, multiple):
    return -(-value // multiple) * multiple


def room(count, parts, sigmas):
    mean = count / parts
    return math.ceil(mean + sigmas * (mean * (1 - 1 / parts)) ** 0.5)


def iota(shape, axis):
    return lax.broadcasted_iota(jnp.int32, shape, axis)


def exact_dot(left, right):
    return jnp.dot(
        left, right, precision=lax.Precision.HIGHEST, preferred_element_type=jnp.float32
    )


def pick_rows(places, start, count, rows):
    pick = jnp.where(iota((count, places.shape[1]), 0) + start == places, 1.0, 0.0)
    return jnp.dot(pick.astype(jnp.bfloat16), rows, preferred_element_type=jnp.float32).astype(
        jnp.bfloat16
    )


def plan_kernel(size, emb_ref, ids_ref, pool_ref, aug_ref, place_ref, rank_ref):
    rows, width = emb_ref.shape
    chips, labels, cap, pool = size["chips"], size["labels"], size["cap"], size["pool"]
    across, tiles = size["across"], size["tiles"]
    chunk = 256
    for start in range(0, rows, chunk):
        x = emb_ref[start : start + chunk, :]
        energy = jnp.sum(x * x, axis=1, keepdims=True)
        aug_ref[start : start + chunk, :] = (x * lax.rsqrt(energy + epsilon)).astype(jnp.bfloat16)

    ids = ids_ref[...]
    label = ids >> (chips.bit_length() - 1)
    shift = ((ids & (tiles - 1)) - lax.axis_index("tile")) & (tiles - 1)
    side = ((ids & (chips - 1)) >> (tiles.bit_length() - 1)) ^ lax.axis_index("chip")
    block = shift * across + side
    key = ((block * labels + label) * rows + iota((1, rows), 1)).astype(jnp.float32)
    base = (block * (labels * rows)).astype(jnp.float32)
    base_shift = (shift * (across * labels * rows)).astype(jnp.float32)
    key_t = jnp.broadcast_to(key, (LANES, rows)).T
    ranks, pooled = [], []
    for start in range(0, rows, LANES):
        here = slice(start, start + LANES)
        smaller = key_t < key[:, here]
        in_block = jnp.where(smaller & (key_t >= base[:, here]), 1.0, 0.0)
        in_shift = jnp.where(smaller & (key_t >= base_shift[:, here]), 1.0, 0.0)
        ranks.append(jnp.sum(in_block, axis=0, keepdims=True))
        pooled.append(jnp.sum(in_shift, axis=0, keepdims=True))
    rank = jnp.concatenate(ranks, axis=1)
    rank_ref[...] = rank
    pooled = jnp.concatenate(pooled, axis=1)

    def apart(shift):
        return shift != size["first"]

    full = (rank >= cap - 1) | (~apart(shift) & (pooled >= pool - across))
    over = jnp.max(jnp.where(full, 1.0, 0.0), axis=1, keepdims=True)
    place = jnp.where(apart(shift), side * cap + rank.astype(jnp.int32), pooled.astype(jnp.int32))
    place = jnp.where(full, -1, place)

    in_block = jnp.where(iota((LANES, rows), 0) == block, 1.0, 0.0).astype(jnp.bfloat16)
    in_label = jnp.where(iota((LANES, rows), 0) == label, 1.0, 0.0).astype(jnp.bfloat16)
    counts = lax.dot_general(
        in_block, in_label, (((1,), (1,)), ((), ())), preferred_element_type=jnp.float32
    )
    counts = jnp.where(iota((LANES, LANES), 1) == FLAG, over, counts)
    aug_ref[rows:, :] = jnp.zeros((LANES, width), jnp.bfloat16)
    aug_ref[rows:, 0:LANES] = counts.astype(jnp.bfloat16)
    lane = iota((1, LANES), 1)
    head_shift = jnp.where(lane < chips, lane >> (across.bit_length() - 1), -1)
    head_side = lane & (across - 1)
    head = jnp.where(
        apart(head_shift), head_side * cap + cap - 1, pool - across + head_side
    )
    shift = jnp.concatenate([shift, head_shift], axis=1)
    place = jnp.concatenate([place, head], axis=1)
    place = jnp.where(place >= 0, shift * PLACES + place, -1)
    place_ref[...] = place
    pool_ref[...] = pick_rows(place, size["first"] * PLACES, pool, aug_ref[...])


def pack_kernel(starts, aug_ref, place_ref, *out_refs):
    aug = aug_ref[...]
    place = place_ref[...]
    for start, out_ref in zip(starts, out_refs):
        out_ref[...] = pick_rows(place, start, out_ref.shape[0], aug)


def regroup_kernel(size, pool_ref, *out_refs):
    across, cap, pool, labels = size["across"], size["cap"], size["pool"], size["labels"]
    rows = pool_ref[...]
    heads = rows[pool - 16 :, 0:LANES].astype(jnp.float32)
    heads = jnp.where(iota((16, LANES), 1) < labels, heads, 0.0)
    counts = jnp.sum(heads, axis=1, keepdims=True).astype(jnp.int32)
    spot = iota((1, pool), 1)
    place = jnp.full((1, pool), -1, jnp.int32)
    begin = jnp.zeros((1, 1), jnp.int32)
    for side in range(across):
        end = begin + counts[16 - across + side : 17 - across + side, :]
        place = jnp.where((spot >= begin) & (spot < end), spot - begin + side * cap, place)
        begin = end
    place = jnp.where(spot >= pool - across, (spot - (pool - across) + 1) * cap - 1, place)
    for side, out_ref in enumerate(out_refs):
        out_ref[...] = pick_rows(place, side * cap, cap, rows)


def sort_kernel(size, *refs):
    across, labels, cap, space = size["across"], size["labels"], size["cap"], size["space"]
    block_refs, (out_ref, place_ref, rows_ref) = refs[:across], refs[across:]
    held = up(cap, ALIGN)
    total = across * held
    for index, ref in enumerate(block_refs):
        if held > cap:
            start = (index + 1) * held - ALIGN
            rows_ref[start : start + ALIGN, :] = jnp.zeros((ALIGN, ref.shape[1]), jnp.bfloat16)
        rows_ref[index * held : index * held + cap, :] = ref[...]
    rows = rows_ref[...]
    spot = iota((LANES, total), 1)
    block = iota((LANES, total), 0)
    head = jnp.where(spot == block * held + cap - 1, 1.0, 0.0).astype(jnp.bfloat16)
    counts = jnp.dot(head, rows[:, 0:LANES], preferred_element_type=jnp.float32)
    flag = jnp.max(counts[:, FLAG:], axis=0, keepdims=True)

    counts_t = counts.T
    lower = jnp.where(iota((LANES, LANES), 0) < iota((LANES, LANES), 1), 1.0, 0.0)
    ahead = exact_dot(counts_t, lower)
    in_block = jnp.zeros((1, LANES), jnp.float32)
    found = jnp.zeros((1, LANES), jnp.float32)
    begin = jnp.zeros((1, 1), jnp.float32)
    lane = iota((1, LANES), 1)
    table = []
    for label in range(labels):
        own = counts_t[label : label + 1, :]
        table.append(begin + ahead[label : label + 1, :] - in_block)
        in_block = in_block + own
        table.append(in_block)
        count = jnp.sum(own, axis=1, keepdims=True)
        high = jnp.floor(count * (1.0 / LANES))
        found = jnp.where(lane == label, high, found)
        found = jnp.where(lane == LOW + label, count - high * LANES, found)
        begin = begin + jnp.floor((count + (ALIGN - 1)) * (1.0 / ALIGN)) * ALIGN
    flag = jnp.maximum(flag, jnp.where(begin > space, 1.0, 0.0))
    found = jnp.where(lane == FLAG, flag, found)
    table.append((lane * held).astype(jnp.float32))
    table.extend([jnp.zeros((1, LANES), jnp.float32)] * (up(len(table), 8) - len(table)))
    table = jnp.concatenate(table, axis=0)

    def places(expand, rank_row):
        where = exact_dot(table, expand)
        rank = rank_row(where)
        place = jnp.full(rank.shape, -1.0, jnp.float32)
        for label in reversed(range(labels)):
            inside = rank < where[2 * label + 1 : 2 * label + 2, :]
            place = jnp.where(inside, where[2 * label : 2 * label + 1, :] + rank, place)
        return place.astype(jnp.int32)

    spot_block = jnp.where((spot >= block * held) & (spot < block * held + cap), 1.0, 0.0)
    spot_row = iota((1, total), 1).astype(jnp.float32)
    place = places(spot_block, lambda where: spot_row - where[2 * labels : 2 * labels + 1, :])
    lanes = place_ref.shape[1]
    rank_row = iota((1, lanes), 1).astype(jnp.float32)
    for index in range(across):
        only = jnp.where(iota((LANES, lanes), 0) == index, 1.0, 0.0)
        place_ref[index : index + 1, :] = places(only, lambda where: rank_row)

    out_ref[space:, :] = jnp.zeros((STEP, out_ref.shape[1]), jnp.bfloat16)
    out_ref[space : space + ALIGN, 0:LANES] = jnp.broadcast_to(found, (ALIGN, LANES)).astype(
        jnp.bfloat16
    )
    for start in range(0, space, ALIGN * 9):
        count = min(ALIGN * 9, space - start)
        out_ref[start : start + count, :] = pick_rows(place, start, count, rows)


def score_kernel(size, *refs):
    across, tiles, labels, space = size["across"], size["tiles"], size["labels"], size["space"]
    pieces = 2 * tiles
    piece_refs, place_refs = refs[:pieces], refs[pieces : pieces + tiles]
    out_ref, rows_ref, total_ref, back_ref, heads_ref, counts_ref, sem = refs[pieces + tiles :]
    lane = iota((1, LANES), 1)
    heads = [ref[space : space + ALIGN, 0:LANES].astype(jnp.float32)[0:1, :] for ref in piece_refs]
    heads_ref[...] = jnp.concatenate(heads, axis=0).astype(jnp.int32)
    copy = pltpu.make_async_copy(heads_ref, counts_ref, sem)
    copy.start()
    copy.wait()
    flag = jnp.int32(0)
    for index in range(pieces):
        flag = jnp.maximum(flag, counts_ref[index, FLAG])

    def aligned(count):
        return (count + (ALIGN - 1)) & -ALIGN

    runs, ends = [], []
    begin = jnp.int32(0)
    source = [jnp.int32(0)] * pieces
    many = jnp.bool_(False)
    for label in range(labels):
        runs.append([])
        for index in range(pieces):
            count = counts_ref[index, label] * LANES + counts_ref[index, LOW + label]
            count = jnp.clip(count, 0, space - source[index])
            runs[label].append((source[index], begin, count))
            many = many | (count > STEP)
            source[index] = source[index] + aligned(count)
            begin = begin + aligned(count)
        ends.append(begin)

    def span(start, step, size):
        return pl.ds(pl.multiple_of(start + step * size, ALIGN), size)

    def gather(index, src, dst, step):
        rows_ref[span(dst, step, STEP), :] = piece_refs[index][span(src, step, STEP), :]

    def repeat(first, end, act):
        def once(step, carry):
            act(step)
            return carry

        lax.fori_loop(first, end, once, 0)

    def cover(count, size):
        return (count + size - 1) // size

    for label in range(labels):
        for index, (src, dst, count) in enumerate(runs[label]):
            gather(index, src, dst, 0)

    @pl.when(many)
    def _():
        for label in range(labels):
            for index, (src, dst, count) in enumerate(runs[label]):
                repeat(0, cover(count, STEP), functools.partial(gather, index, src, dst))

    def window(label, row, column):
        left = rows_ref[span(row, 0, LEFT), :]
        right = rows_ref[span(column, 0, RIGHT), :]
        scores = lax.dot_general(
            left, right, (((1,), (1,)), ((), ())), preferred_element_type=jnp.float32
        )
        at = iota((1, RIGHT), 1) + column
        valid = at < 0
        for _, low, count in runs[label]:
            valid = valid | ((at >= low) & (at < low + count))
        at = jnp.where(valid, at, -1)
        itself = iota((LEFT, RIGHT), 0) + row
        counted = (at >= 0) & (at != itself)
        terms = jnp.where(counted, jnp.exp(sharpness * scores), 0.0)
        sums = jnp.sum(terms, axis=1, keepdims=True)
        return jnp.broadcast_to(sums, (LEFT, LANES))

    wide = jnp.bool_(False)
    for label in range(labels):
        first, own_end = runs[label][0][1], runs[label][tiles][1]
        total_ref[label, 0:LEFT, :] = window(label, first, first)
        wide = wide | (own_end - first > LEFT) | (ends[label] - first > RIGHT)

    @pl.when(wide)
    def _():
        for label in range(labels):
            first, own_end = runs[label][0][1], runs[label][tiles][1]
            across_steps = cover(ends[label] - first, RIGHT)

            def add(strip, step, label=label, first=first):
                row, column = first + strip * LEFT, first + step * RIGHT
                total_ref[label, span(0, strip, LEFT), :] += window(label, row, column)

            def strips(strip, label=label, add=add, across_steps=across_steps):
                total_ref[label, span(0, strip, LEFT), :] = jnp.zeros((LEFT, LANES), jnp.float32)
                repeat(0, across_steps, functools.partial(add, strip))

            repeat(1, across_steps, functools.partial(add, 0))
            repeat(1, cover(own_end - first, LEFT), strips)

    def scatter(label, index, step):
        src, dst, _ = runs[label][index]
        back_ref[index, span(src, step, STEP), :] = total_ref[
            label, span(dst - runs[label][0][1], step, STEP), :
        ]

    for index in range(tiles):
        for label in range(labels):
            scatter(label, index, 0)

    @pl.when(many)
    def _():
        for index in range(tiles):
            for label in range(labels):
                count = runs[label][index][2]
                repeat(0, cover(count, STEP), functools.partial(scatter, label, index))

    lanes = out_ref.shape[1]
    row = iota((space, LANES), 0)
    chip, tile = lax.axis_index("chip"), lax.axis_index("tile")
    for shift in range(tiles):
        for side in range(across):
            home = (chip ^ side) * tiles + ((tile - shift) & (tiles - 1))
            for start in range(0, lanes, LANES):
                place = place_refs[shift][side : side + 1, start : start + LANES]
                value = jnp.sum(
                    jnp.where(row == place, back_ref[shift, 0:space, :], 0.0),
                    axis=0,
                    keepdims=True,
                )
                if start + LANES == lanes:
                    value = jnp.where(lane == FLAG, flag.astype(jnp.float32), value)
                out_ref[pl.ds(home, 1), start : start + LANES] = value


def unpack_kernel(chips, ret_ref, ids_ref, rank_ref, out_ref, flag_ref):
    rows = ids_ref.shape[1]
    lanes = ret_ref.shape[1]
    values = ret_ref[...]
    flag = jnp.max(values[:, lanes - 1 :], axis=0, keepdims=True)
    flag_ref[0, 0] = jnp.sum(flag).astype(jnp.int32)
    chip = ids_ref[...] & (chips - 1)
    rank = rank_ref[...].astype(jnp.int32)
    at_rank = jnp.where(iota((lanes, rows), 0) == rank, 1.0, 0.0)
    found = exact_dot(values, at_rank)
    total = jnp.sum(jnp.where(iota((chips, rows), 0) == chip, found, 0.0), axis=0, keepdims=True)
    out_ref[...] = jnp.log(1.0 + total)


def call(kernel, name, out_shape, inputs, vmem_mib=12, **options):
    vmem = pl.BlockSpec(memory_space=pltpu.VMEM)
    return pl.pallas_call(
        kernel,
        out_shape=out_shape,
        in_specs=[vmem] * len(inputs),
        out_specs=options.pop("out_specs", jax.tree.map(lambda _: vmem, out_shape)),
        compiler_params=pltpu.CompilerParams(vmem_limit_bytes=vmem_mib * MIB),
        name=name,
        **options,
    )(*inputs)


def body(embeddings, cluster_ids):
    rows, width = embeddings.shape
    across, tiles = lax.axis_size("chip"), lax.axis_size("tile")
    chips = across * tiles
    labels = KG * across * lax.axis_size("core") // chips
    cap = up(room(rows, chips, 5.0) + 1, 8)
    pool = up(room(rows, tiles, 4.25) + across, ALIGN)
    space = up(room(rows, tiles, 4.75) + labels * (ALIGN - 4), ALIGN)
    order = sorted(range(1, tiles), key=lambda shift: (-min(shift, tiles - shift), shift))
    size = dict(
        chips=chips, across=across, tiles=tiles, labels=labels, cap=cap, pool=pool, space=space,
        first=order[0],
    )
    lanes = up(cap + 1, LANES)
    shape = jax.ShapeDtypeStruct

    ids_row = cluster_ids.reshape(1, rows)
    pool_rows, aug, slots, rank = call(
        functools.partial(plan_kernel, size),
        "plan",
        [
            shape((pool, width), jnp.bfloat16),
            shape((rows + LANES, width), jnp.bfloat16),
            shape((1, rows + LANES), jnp.int32),
            shape((1, rows), jnp.float32),
        ],
        [embeddings, ids_row],
    )

    near_and_far = [0, *order[1:]]
    blocks = call(
        functools.partial(
            pack_kernel,
            [shift * PLACES + side * cap for shift in near_and_far for side in range(across)],
        ),
        "pack",
        [shape((cap, width), jnp.bfloat16)] * (across * len(near_and_far)),
        [aug, slots],
    )
    packed = {
        shift: blocks[place * across : (place + 1) * across]
        for place, shift in enumerate(near_and_far)
    }

    def along(shift):
        return [(z, (z + shift) % tiles) for z in range(tiles)]

    def over(side):
        return [(a, a ^ side) for a in range(across)]

    def after(value, *others):
        return lax.optimization_barrier((value, others))[0]

    def send_across(blocks):
        return [blocks[0]] + [
            lax.ppermute(blocks[side], "chip", over(side)) for side in range(1, across)
        ]

    def send_far(blocks, shift, side):
        route = [(a * tiles + z, b * tiles + y) for a, b in over(side) for z, y in along(shift)]
        return lax.ppermute(blocks[side], ("chip", "tile"), route)

    swap = [(0, 1), (1, 0)]
    own, other, places = {}, {}, {}

    def finish(shift, arrived):
        own[shift], places[shift] = call(
            functools.partial(sort_kernel, size),
            "sort",
            [
                shape((space + STEP, width), jnp.bfloat16),
                shape((across, lanes), jnp.int32),
            ],
            arrived,
            scratch_shapes=[pltpu.VMEM((across * up(cap, ALIGN), width), jnp.bfloat16)],
        )
        other[shift] = lax.ppermute(own[shift], "core", swap)

    pooled = lax.ppermute(pool_rows, "tile", along(order[0]))
    near = send_across(packed[0])
    finish(0, near)
    blocks = [(shift, side) for shift in order[1:] for side in range(across)]
    beside = blocks[:1]
    arrived = {
        (shift, side): send_far(after(packed[shift], *near), shift, side) for shift, side in beside
    }
    regrouped = call(
        functools.partial(regroup_kernel, size),
        "regroup",
        [shape((cap, width), jnp.bfloat16)] * across,
        [after(pooled, *near, *arrived.values())],
    )
    passed = send_across(regrouped)
    finish(order[0], passed)
    for shift, side in blocks[len(beside) :]:
        arrived[shift, side] = send_far(after(packed[shift], pooled), shift, side)
    for shift in order[1:]:
        finish(shift, [arrived[shift, side] for side in range(across)])
    own, other, places = (
        [found[shift] for shift in range(tiles)] for found in (own, other, places)
    )
    room_own = tiles * space + LEFT + STEP
    totals = call(
        functools.partial(score_kernel, size),
        "score",
        shape((chips, lanes), jnp.float32),
        [*own, *other, *places],
        vmem_mib=26,
        scratch_shapes=[
            pltpu.VMEM((2 * tiles * space + LEFT + RIGHT, width), jnp.bfloat16),
            pltpu.VMEM((labels, room_own, LANES), jnp.float32),
            pltpu.VMEM((tiles, space + STEP, LANES), jnp.float32),
            pltpu.VMEM((2 * tiles, LANES), jnp.int32),
            pltpu.SMEM((2 * tiles, LANES), jnp.int32),
            pltpu.SemaphoreType.DMA,
        ],
    )
    returned = lax.all_to_all(totals, ("chip", "tile"), split_axis=0, concat_axis=0, tiled=True)
    result, flag = call(
        functools.partial(unpack_kernel, chips),
        "unpack",
        [shape((1, rows), jnp.float32), shape((1, 1), jnp.int32)],
        [returned, ids_row, rank],
        out_specs=[
            pl.BlockSpec(memory_space=pltpu.VMEM),
            pl.BlockSpec(memory_space=pltpu.SMEM),
        ],
    )
    return lax.cond(
        flag.reshape(()) > 0,
        lambda: general_plan(embeddings, cluster_ids),
        lambda: result.reshape(rows),
    )


def solution(mesh):
    shards = mesh.shape["shard"]
    tiles = mesh.shape["tile"]
    split = Mesh(mesh.devices.reshape(shards // 2, 2, tiles), ("chip", "core", "tile"))
    rows = ("chip", "core", "tile")
    return jax.shard_map(
        body, mesh=split, in_specs=(P(rows, None), P(rows)), out_specs=P(rows), check_vma=False
    )
```

```python
import functools
import math

import jax
import jax.numpy as jnp
from jax import lax
from jax.experimental import pallas as pl
from jax.experimental.pallas import tpu as pltpu
from jax.sharding import Mesh
from jax.sharding import PartitionSpec as P

KG = 16


sharpness = 30.0
epsilon = 1e-06

MIB = 1024 * 1024
LANES = 128
FLAG = LANES - 1
LOW = LANES // 2
ALIGN = 16
STEP = 96
LEFT = 256
RIGHT = 512
PLACES = 1 << 16


def unit_rows(embeddings):
    energy = jnp.sum(embeddings * embeddings, axis=1, keepdims=True)
    return (embeddings * lax.rsqrt(energy + epsilon)).astype(jnp.bfloat16)


def row_sums(left, left_labels, right, right_labels, same_rows):
    count = left.shape[0]
    block = min(512, count)
    blocks = count // block

    def step(start, items):
        rows_block, labels_block = items
        scores = lax.dot_general(
            rows_block, right, (((1,), (1,)), ((), ())), preferred_element_type=jnp.float32
        )
        same = (labels_block[:, None] == right_labels[None, :]) & (labels_block[:, None] >= 0)
        itself = (start + jnp.arange(block))[:, None] == jnp.arange(count)[None, :]
        same = same & ~(itself & same_rows)
        terms = jnp.where(same, jnp.exp(sharpness * scores), 0.0)
        return (start + block, jnp.sum(terms, axis=1))

    _, totals = lax.scan(
        step,
        jnp.int32(0),
        (left.reshape(blocks, block, left.shape[1]), left_labels.reshape(blocks, block)),
    )
    return totals.reshape(count)


def general_plan(embeddings, cluster_ids):
    shard_axes = ("chip", "core")
    local_rows = embeddings.shape[0]
    shards = lax.axis_size("chip") * lax.axis_size("core")
    tiles = lax.axis_size("tile")
    capacity = 2 * local_rows // shards
    slot_count = shards * capacity
    unit = unit_rows(embeddings)
    owner = cluster_ids // KG
    onehot = (owner[:, None] == jnp.arange(shards, dtype=jnp.int32)[None, :]).astype(jnp.int32)
    ranks = jnp.sum((jnp.cumsum(onehot, axis=0) - 1) * onehot, axis=1)
    slots = owner * capacity + ranks
    outgoing = jnp.zeros((slot_count, unit.shape[1]), jnp.bfloat16).at[slots].set(unit)
    outgoing_labels = jnp.full((slot_count,), -1, jnp.int32).at[slots].set(cluster_ids)
    owned = lax.all_to_all(outgoing, shard_axes, split_axis=0, concat_axis=0, tiled=True)
    owned_labels = lax.all_to_all(
        outgoing_labels, shard_axes, split_axis=0, concat_axis=0, tiled=True
    )
    around = [(tile, (tile + 1) % tiles) for tile in range(tiles)]

    def visit(step, state):
        totals, rows, labels = state
        totals = totals + row_sums(owned, owned_labels, rows, labels, step == 0)
        return (totals, lax.ppermute(rows, "tile", around), lax.ppermute(labels, "tile", around))

    totals, _, _ = lax.fori_loop(
        0, tiles, visit, (jnp.zeros((slot_count,), jnp.float32), owned, owned_labels)
    )
    returned = lax.all_to_all(totals, shard_axes, split_axis=0, concat_axis=0, tiled=True)
    return jnp.log(1.0 + returned[slots])


def up(value, multiple):
    return -(-value // multiple) * multiple


def room(count, parts, sigmas):
    mean = count / parts
    return math.ceil(mean + sigmas * (mean * (1 - 1 / parts)) ** 0.5)


def iota(shape, axis):
    return lax.broadcasted_iota(jnp.int32, shape, axis)


def exact_dot(left, right):
    return jnp.dot(
        left, right, precision=lax.Precision.HIGHEST, preferred_element_type=jnp.float32
    )


def pick_rows(places, start, count, rows):
    pick = jnp.where(iota((count, places.shape[1]), 0) + start == places, 1.0, 0.0)
    return jnp.dot(pick.astype(jnp.bfloat16), rows, preferred_element_type=jnp.float32).astype(
        jnp.bfloat16
    )


def plan_kernel(size, emb_ref, ids_ref, pool_ref, aug_ref, place_ref, rank_ref):
    rows, width = emb_ref.shape
    chips, labels, cap, pool = size["chips"], size["labels"], size["cap"], size["pool"]
    across, tiles = size["across"], size["tiles"]
    chunk = 256
    for start in range(0, rows, chunk):
        x = emb_ref[start : start + chunk, :]
        energy = jnp.sum(x * x, axis=1, keepdims=True)
        aug_ref[start : start + chunk, :] = (x * lax.rsqrt(energy + epsilon)).astype(jnp.bfloat16)

    ids = ids_ref[...]
    label = ids >> (chips.bit_length() - 1)
    shift = ((ids & (tiles - 1)) - lax.axis_index("tile")) & (tiles - 1)
    side = ((ids & (chips - 1)) >> (tiles.bit_length() - 1)) ^ lax.axis_index("chip")
    block = shift * across + side
    in_block = jnp.where(iota((LANES, rows), 0) == block, 1.0, 0.0).astype(jnp.bfloat16)
    in_label = jnp.where(iota((LANES, rows), 0) == label, 1.0, 0.0).astype(jnp.bfloat16)
    counts = lax.dot_general(
        in_block, in_label, (((1,), (1,)), ((), ())), preferred_element_type=jnp.float32
    )
    of_block = jnp.broadcast_to(jnp.sum(counts, axis=1, keepdims=True), (LANES, LANES))
    lower = jnp.where(iota((LANES, LANES), 1) < iota((LANES, LANES), 0), 1.0, 0.0)
    starts = exact_dot(lower, of_block)[0:chips, 0:1]

    def start_of(block):
        mine = iota((chips, rows), 0) == block
        return jnp.sum(jnp.where(mine, starts, 0.0), axis=0, keepdims=True)

    key = ((block * labels + label) * rows + iota((1, rows), 1)).astype(jnp.float32)
    key_t = jnp.broadcast_to(key, (LANES, rows)).T
    order = []
    for start in range(0, rows, LANES):
        smaller = jnp.where(key_t < key[:, start : start + LANES], 1.0, 0.0)
        order.append(jnp.sum(smaller, axis=0, keepdims=True))
    order = jnp.concatenate(order, axis=1)
    rank = order - start_of(block)
    pooled = order - start_of(shift * across)
    rank_ref[...] = rank

    def apart(shift):
        return shift != size["first"]

    full = (rank >= cap - 1) | (~apart(shift) & (pooled >= pool - across))
    over = jnp.max(jnp.where(full, 1.0, 0.0), axis=1, keepdims=True)
    place = jnp.where(apart(shift), side * cap + rank.astype(jnp.int32), pooled.astype(jnp.int32))
    place = jnp.where(full, -1, place)

    counts = jnp.where(iota((LANES, LANES), 1) == FLAG, over, counts)
    aug_ref[rows:, :] = jnp.zeros((LANES, width), jnp.bfloat16)
    aug_ref[rows:, 0:LANES] = counts.astype(jnp.bfloat16)
    lane = iota((1, LANES), 1)
    head_shift = jnp.where(lane < chips, lane >> (across.bit_length() - 1), -1)
    head_side = lane & (across - 1)
    head = jnp.where(
        apart(head_shift), head_side * cap + cap - 1, pool - across + head_side
    )
    shift = jnp.concatenate([shift, head_shift], axis=1)
    place = jnp.concatenate([place, head], axis=1)
    place = jnp.where(place >= 0, shift * PLACES + place, -1)
    place_ref[...] = place
    pool_ref[...] = pick_rows(place, size["first"] * PLACES, pool, aug_ref[...])


def pack_kernel(starts, aug_ref, place_ref, *out_refs):
    aug = aug_ref[...]
    place = place_ref[...]
    for start, out_ref in zip(starts, out_refs):
        out_ref[...] = pick_rows(place, start, out_ref.shape[0], aug)


def regroup_kernel(size, pool_ref, *out_refs):
    across, cap, pool, labels = size["across"], size["cap"], size["pool"], size["labels"]
    rows = pool_ref[...]
    heads = rows[pool - 16 :, 0:LANES].astype(jnp.float32)
    heads = jnp.where(iota((16, LANES), 1) < labels, heads, 0.0)
    counts = jnp.sum(heads, axis=1, keepdims=True).astype(jnp.int32)
    spot = iota((1, pool), 1)
    place = jnp.full((1, pool), -1, jnp.int32)
    begin = jnp.zeros((1, 1), jnp.int32)
    for side in range(across):
        end = begin + counts[16 - across + side : 17 - across + side, :]
        place = jnp.where((spot >= begin) & (spot < end), spot - begin + side * cap, place)
        begin = end
    place = jnp.where(spot >= pool - across, (spot - (pool - across) + 1) * cap - 1, place)
    for side, out_ref in enumerate(out_refs):
        out_ref[...] = pick_rows(place, side * cap, cap, rows)


def sort_kernel(size, *refs):
    across, labels, cap, space = size["across"], size["labels"], size["cap"], size["space"]
    block_refs, (out_ref, place_ref, rows_ref) = refs[:across], refs[across:]
    held = up(cap, ALIGN)
    total = across * held
    for index, ref in enumerate(block_refs):
        if held > cap:
            start = (index + 1) * held - ALIGN
            rows_ref[start : start + ALIGN, :] = jnp.zeros((ALIGN, ref.shape[1]), jnp.bfloat16)
        rows_ref[index * held : index * held + cap, :] = ref[...]
    rows = rows_ref[...]
    spot = iota((LANES, total), 1)
    block = iota((LANES, total), 0)
    head = jnp.where(spot == block * held + cap - 1, 1.0, 0.0).astype(jnp.bfloat16)
    counts = jnp.dot(head, rows[:, 0:LANES], preferred_element_type=jnp.float32)
    flag = jnp.max(counts[:, FLAG:], axis=0, keepdims=True)

    counts_t = counts.T
    lower = jnp.where(iota((LANES, LANES), 0) < iota((LANES, LANES), 1), 1.0, 0.0)
    ahead = exact_dot(counts_t, lower)
    in_block = jnp.zeros((1, LANES), jnp.float32)
    found = jnp.zeros((1, LANES), jnp.float32)
    begin = jnp.zeros((1, 1), jnp.float32)
    lane = iota((1, LANES), 1)
    table = []
    for label in range(labels):
        own = counts_t[label : label + 1, :]
        table.append(begin + ahead[label : label + 1, :] - in_block)
        in_block = in_block + own
        table.append(in_block)
        count = jnp.sum(own, axis=1, keepdims=True)
        high = jnp.floor(count * (1.0 / LANES))
        found = jnp.where(lane == label, high, found)
        found = jnp.where(lane == LOW + label, count - high * LANES, found)
        begin = begin + jnp.floor((count + (ALIGN - 1)) * (1.0 / ALIGN)) * ALIGN
    flag = jnp.maximum(flag, jnp.where(begin > space, 1.0, 0.0))
    found = jnp.where(lane == FLAG, flag, found)
    table.append((lane * held).astype(jnp.float32))
    table.extend([jnp.zeros((1, LANES), jnp.float32)] * (up(len(table), 8) - len(table)))
    table = jnp.concatenate(table, axis=0)

    def places(expand, rank_row):
        where = exact_dot(table, expand)
        rank = rank_row(where)
        place = jnp.full(rank.shape, -1.0, jnp.float32)
        for label in reversed(range(labels)):
            inside = rank < where[2 * label + 1 : 2 * label + 2, :]
            place = jnp.where(inside, where[2 * label : 2 * label + 1, :] + rank, place)
        return place.astype(jnp.int32)

    spot_block = jnp.where((spot >= block * held) & (spot < block * held + cap), 1.0, 0.0)
    spot_row = iota((1, total), 1).astype(jnp.float32)
    place = places(spot_block, lambda where: spot_row - where[2 * labels : 2 * labels + 1, :])
    lanes = place_ref.shape[1]
    rank_row = iota((1, lanes), 1).astype(jnp.float32)
    for index in range(across):
        only = jnp.where(iota((LANES, lanes), 0) == index, 1.0, 0.0)
        place_ref[index : index + 1, :] = places(only, lambda where: rank_row)

    out_ref[space:, :] = jnp.zeros((STEP, out_ref.shape[1]), jnp.bfloat16)
    out_ref[space : space + ALIGN, 0:LANES] = jnp.broadcast_to(found, (ALIGN, LANES)).astype(
        jnp.bfloat16
    )
    for start in range(0, space, ALIGN * 9):
        count = min(ALIGN * 9, space - start)
        out_ref[start : start + count, :] = pick_rows(place, start, count, rows)


def score_kernel(size, *refs):
    across, tiles, labels, space = size["across"], size["tiles"], size["labels"], size["space"]
    pieces = 2 * tiles
    piece_refs, place_refs = refs[:pieces], refs[pieces : pieces + tiles]
    out_ref, rows_ref, total_ref, back_ref, heads_ref, counts_ref, sem = refs[pieces + tiles :]
    lane = iota((1, LANES), 1)
    heads = [ref[space : space + ALIGN, 0:LANES].astype(jnp.float32)[0:1, :] for ref in piece_refs]
    heads_ref[...] = jnp.concatenate(heads, axis=0).astype(jnp.int32)
    copy = pltpu.make_async_copy(heads_ref, counts_ref, sem)
    copy.start()
    copy.wait()
    flag = jnp.int32(0)
    for index in range(pieces):
        flag = jnp.maximum(flag, counts_ref[index, FLAG])

    def aligned(count):
        return (count + (ALIGN - 1)) & -ALIGN

    runs, ends = [], []
    begin = jnp.int32(0)
    source = [jnp.int32(0)] * pieces
    many = jnp.bool_(False)
    for label in range(labels):
        runs.append([])
        for index in range(pieces):
            count = counts_ref[index, label] * LANES + counts_ref[index, LOW + label]
            count = jnp.clip(count, 0, space - source[index])
            runs[label].append((source[index], begin, count))
            many = many | (count > STEP)
            source[index] = source[index] + aligned(count)
            begin = begin + aligned(count)
        ends.append(begin)

    def span(start, step, size):
        return pl.ds(pl.multiple_of(start + step * size, ALIGN), size)

    def gather(index, src, dst, step):
        rows_ref[span(dst, step, STEP), :] = piece_refs[index][span(src, step, STEP), :]

    def repeat(first, end, act):
        def once(step, carry):
            act(step)
            return carry

        lax.fori_loop(first, end, once, 0)

    def cover(count, size):
        return (count + size - 1) // size

    for label in range(labels):
        for index, (src, dst, count) in enumerate(runs[label]):
            gather(index, src, dst, 0)

    @pl.when(many)
    def _():
        for label in range(labels):
            for index, (src, dst, count) in enumerate(runs[label]):
                repeat(0, cover(count, STEP), functools.partial(gather, index, src, dst))

    def window(label, row, column):
        left = rows_ref[span(row, 0, LEFT), :]
        right = rows_ref[span(column, 0, RIGHT), :]
        scores = lax.dot_general(
            left, right, (((1,), (1,)), ((), ())), preferred_element_type=jnp.float32
        )
        at = iota((1, RIGHT), 1) + column
        valid = at < 0
        for _, low, count in runs[label]:
            valid = valid | ((at >= low) & (at < low + count))
        at = jnp.where(valid, at, -1)
        itself = iota((LEFT, RIGHT), 0) + row
        counted = (at >= 0) & (at != itself)
        terms = jnp.where(counted, jnp.exp(sharpness * scores), 0.0)
        sums = jnp.sum(terms, axis=1, keepdims=True)
        return jnp.broadcast_to(sums, (LEFT, LANES))

    wide = jnp.bool_(False)
    for label in range(labels):
        first, own_end = runs[label][0][1], runs[label][tiles][1]
        total_ref[label, 0:LEFT, :] = window(label, first, first)
        wide = wide | (own_end - first > LEFT) | (ends[label] - first > RIGHT)

    @pl.when(wide)
    def _():
        for label in range(labels):
            first, own_end = runs[label][0][1], runs[label][tiles][1]
            across_steps = cover(ends[label] - first, RIGHT)

            def add(strip, step, label=label, first=first):
                row, column = first + strip * LEFT, first + step * RIGHT
                total_ref[label, span(0, strip, LEFT), :] += window(label, row, column)

            def strips(strip, label=label, add=add, across_steps=across_steps):
                total_ref[label, span(0, strip, LEFT), :] = jnp.zeros((LEFT, LANES), jnp.float32)
                repeat(0, across_steps, functools.partial(add, strip))

            repeat(1, across_steps, functools.partial(add, 0))
            repeat(1, cover(own_end - first, LEFT), strips)

    def scatter(label, index, step):
        src, dst, _ = runs[label][index]
        back_ref[index, span(src, step, STEP), :] = total_ref[
            label, span(dst - runs[label][0][1], step, STEP), :
        ]

    for index in range(tiles):
        for label in range(labels):
            scatter(label, index, 0)

    @pl.when(many)
    def _():
        for index in range(tiles):
            for label in range(labels):
                count = runs[label][index][2]
                repeat(0, cover(count, STEP), functools.partial(scatter, label, index))

    lanes = out_ref.shape[1]
    row = iota((space, LANES), 0)
    chip, tile = lax.axis_index("chip"), lax.axis_index("tile")
    for shift in range(tiles):
        for side in range(across):
            home = (chip ^ side) * tiles + ((tile - shift) & (tiles - 1))
            for start in range(0, lanes, LANES):
                place = place_refs[shift][side : side + 1, start : start + LANES]
                value = jnp.sum(
                    jnp.where(row == place, back_ref[shift, 0:space, :], 0.0),
                    axis=0,
                    keepdims=True,
                )
                if start + LANES == lanes:
                    value = jnp.where(lane == FLAG, flag.astype(jnp.float32), value)
                out_ref[pl.ds(home, 1), start : start + LANES] = value


def unpack_kernel(chips, ret_ref, ids_ref, rank_ref, out_ref, flag_ref):
    rows = ids_ref.shape[1]
    lanes = ret_ref.shape[1]
    values = ret_ref[...]
    flag = jnp.max(values[:, lanes - 1 :], axis=0, keepdims=True)
    flag_ref[0, 0] = jnp.sum(flag).astype(jnp.int32)
    chip = ids_ref[...] & (chips - 1)
    rank = rank_ref[...].astype(jnp.int32)
    at_rank = jnp.where(iota((lanes, rows), 0) == rank, 1.0, 0.0)
    found = exact_dot(values, at_rank)
    total = jnp.sum(jnp.where(iota((chips, rows), 0) == chip, found, 0.0), axis=0, keepdims=True)
    out_ref[...] = jnp.log(1.0 + total)


def call(kernel, name, out_shape, inputs, vmem_mib=12, **options):
    vmem = pl.BlockSpec(memory_space=pltpu.VMEM)
    return pl.pallas_call(
        kernel,
        out_shape=out_shape,
        in_specs=[vmem] * len(inputs),
        out_specs=options.pop("out_specs", jax.tree.map(lambda _: vmem, out_shape)),
        compiler_params=pltpu.CompilerParams(vmem_limit_bytes=vmem_mib * MIB),
        name=name,
        **options,
    )(*inputs)


def body(embeddings, cluster_ids):
    rows, width = embeddings.shape
    across, tiles = lax.axis_size("chip"), lax.axis_size("tile")
    chips = across * tiles
    labels = KG * across * lax.axis_size("core") // chips
    cap = up(room(rows, chips, 5.0) + 1, 8)
    pool = up(room(rows, tiles, 4.25) + across, ALIGN)
    space = up(room(rows, tiles, 4.75) + labels * (ALIGN - 4), ALIGN)
    order = sorted(range(1, tiles), key=lambda shift: (-min(shift, tiles - shift), shift))
    size = dict(
        chips=chips, across=across, tiles=tiles, labels=labels, cap=cap, pool=pool, space=space,
        first=order[0],
    )
    lanes = up(cap + 1, LANES)
    shape = jax.ShapeDtypeStruct

    ids_row = cluster_ids.reshape(1, rows)
    pool_rows, aug, slots, rank = call(
        functools.partial(plan_kernel, size),
        "plan",
        [
            shape((pool, width), jnp.bfloat16),
            shape((rows + LANES, width), jnp.bfloat16),
            shape((1, rows + LANES), jnp.int32),
            shape((1, rows), jnp.float32),
        ],
        [embeddings, ids_row],
    )

    near_and_far = [0, *order[1:]]
    blocks = call(
        functools.partial(
            pack_kernel,
            [shift * PLACES + side * cap for shift in near_and_far for side in range(across)],
        ),
        "pack",
        [shape((cap, width), jnp.bfloat16)] * (across * len(near_and_far)),
        [aug, slots],
    )
    packed = {
        shift: blocks[place * across : (place + 1) * across]
        for place, shift in enumerate(near_and_far)
    }

    def along(shift):
        return [(z, (z + shift) % tiles) for z in range(tiles)]

    def over(side):
        return [(a, a ^ side) for a in range(across)]

    def after(value, *others):
        return lax.optimization_barrier((value, others))[0]

    def send_across(blocks):
        return [blocks[0]] + [
            lax.ppermute(blocks[side], "chip", over(side)) for side in range(1, across)
        ]

    def send_far(blocks, shift, side):
        route = [(a * tiles + z, b * tiles + y) for a, b in over(side) for z, y in along(shift)]
        return lax.ppermute(blocks[side], ("chip", "tile"), route)

    swap = [(0, 1), (1, 0)]
    own, other, places = {}, {}, {}

    def finish(shift, arrived):
        own[shift], places[shift] = call(
            functools.partial(sort_kernel, size),
            "sort",
            [
                shape((space + STEP, width), jnp.bfloat16),
                shape((across, lanes), jnp.int32),
            ],
            arrived,
            scratch_shapes=[pltpu.VMEM((across * up(cap, ALIGN), width), jnp.bfloat16)],
        )
        other[shift] = lax.ppermute(own[shift], "core", swap)

    pooled = lax.ppermute(pool_rows, "tile", along(order[0]))
    near = send_across(packed[0])
    finish(0, near)
    blocks = [(shift, side) for shift in order[1:] for side in range(across)]
    beside = [(shift, across - 1) for shift in order[1:2]]
    arrived = {
        (shift, side): send_far(after(packed[shift], *near), shift, side) for shift, side in beside
    }
    regrouped = call(
        functools.partial(regroup_kernel, size),
        "regroup",
        [shape((cap, width), jnp.bfloat16)] * across,
        [after(pooled, *near, *arrived.values())],
    )
    passed = send_across(regrouped)
    finish(order[0], passed)
    for shift, side in sorted(set(blocks) - set(beside), key=lambda block: (block[1] > 0, block)):
        ready = after(packed[shift], pooled if side == 0 else pooled)
        arrived[shift, side] = send_far(ready, shift, side)
    for shift in order[1:]:
        finish(shift, [arrived[shift, side] for side in range(across)])
    own, other, places = (
        [found[shift] for shift in range(tiles)] for found in (own, other, places)
    )
    room_own = tiles * space + LEFT + STEP
    totals = call(
        functools.partial(score_kernel, size),
        "score",
        shape((chips, lanes), jnp.float32),
        [*own, *other, *places],
        vmem_mib=26,
        scratch_shapes=[
            pltpu.VMEM((2 * tiles * space + LEFT + RIGHT, width), jnp.bfloat16),
            pltpu.VMEM((labels, room_own, LANES), jnp.float32),
            pltpu.VMEM((tiles, space + STEP, LANES), jnp.float32),
            pltpu.VMEM((2 * tiles, LANES), jnp.int32),
            pltpu.SMEM((2 * tiles, LANES), jnp.int32),
            pltpu.SemaphoreType.DMA,
        ],
    )
    returned = lax.all_to_all(totals, ("chip", "tile"), split_axis=0, concat_axis=0, tiled=True)
    result, flag = call(
        functools.partial(unpack_kernel, chips),
        "unpack",
        [shape((1, rows), jnp.float32), shape((1, 1), jnp.int32)],
        [returned, ids_row, rank],
        out_specs=[
            pl.BlockSpec(memory_space=pltpu.VMEM),
            pl.BlockSpec(memory_space=pltpu.SMEM),
        ],
    )
    return lax.cond(
        flag.reshape(()) > 0,
        lambda: general_plan(embeddings, cluster_ids),
        lambda: result.reshape(rows),
    )


def solution(mesh):
    shards = mesh.shape["shard"]
    tiles = mesh.shape["tile"]
    split = Mesh(mesh.devices.reshape(shards // 2, 2, tiles), ("chip", "core", "tile"))
    rows = ("chip", "core", "tile")
    return jax.shard_map(
        body, mesh=split, in_specs=(P(rows, None), P(rows)), out_specs=P(rows), check_vma=False
    )
```

```python
import functools
import math

import jax
import jax.numpy as jnp
from jax import lax
from jax.experimental import pallas as pl
from jax.experimental.pallas import tpu as pltpu
from jax.sharding import Mesh
from jax.sharding import PartitionSpec as P

KG = 16


sharpness = 30.0
epsilon = 1e-06

MIB = 1024 * 1024
LANES = 128
FLAG = LANES - 1
LOW = LANES // 2
ALIGN = 16
STEP = 96
LEFT = 256
RIGHT = 512
PLACES = 1 << 16


def unit_rows(embeddings):
    energy = jnp.sum(embeddings * embeddings, axis=1, keepdims=True)
    return (embeddings * lax.rsqrt(energy + epsilon)).astype(jnp.bfloat16)


def row_sums(left, left_labels, right, right_labels, same_rows):
    count = left.shape[0]
    block = min(512, count)
    blocks = count // block

    def step(start, items):
        rows_block, labels_block = items
        scores = lax.dot_general(
            rows_block, right, (((1,), (1,)), ((), ())), preferred_element_type=jnp.float32
        )
        same = (labels_block[:, None] == right_labels[None, :]) & (labels_block[:, None] >= 0)
        itself = (start + jnp.arange(block))[:, None] == jnp.arange(count)[None, :]
        same = same & ~(itself & same_rows)
        terms = jnp.where(same, jnp.exp(sharpness * scores), 0.0)
        return (start + block, jnp.sum(terms, axis=1))

    _, totals = lax.scan(
        step,
        jnp.int32(0),
        (left.reshape(blocks, block, left.shape[1]), left_labels.reshape(blocks, block)),
    )
    return totals.reshape(count)


def general_plan(embeddings, cluster_ids):
    shard_axes = ("chip", "core")
    local_rows = embeddings.shape[0]
    shards = lax.axis_size("chip") * lax.axis_size("core")
    tiles = lax.axis_size("tile")
    capacity = 2 * local_rows // shards
    slot_count = shards * capacity
    unit = unit_rows(embeddings)
    owner = cluster_ids // KG
    onehot = (owner[:, None] == jnp.arange(shards, dtype=jnp.int32)[None, :]).astype(jnp.int32)
    ranks = jnp.sum((jnp.cumsum(onehot, axis=0) - 1) * onehot, axis=1)
    slots = owner * capacity + ranks
    outgoing = jnp.zeros((slot_count, unit.shape[1]), jnp.bfloat16).at[slots].set(unit)
    outgoing_labels = jnp.full((slot_count,), -1, jnp.int32).at[slots].set(cluster_ids)
    owned = lax.all_to_all(outgoing, shard_axes, split_axis=0, concat_axis=0, tiled=True)
    owned_labels = lax.all_to_all(
        outgoing_labels, shard_axes, split_axis=0, concat_axis=0, tiled=True
    )
    around = [(tile, (tile + 1) % tiles) for tile in range(tiles)]

    def visit(step, state):
        totals, rows, labels = state
        totals = totals + row_sums(owned, owned_labels, rows, labels, step == 0)
        return (totals, lax.ppermute(rows, "tile", around), lax.ppermute(labels, "tile", around))

    totals, _, _ = lax.fori_loop(
        0, tiles, visit, (jnp.zeros((slot_count,), jnp.float32), owned, owned_labels)
    )
    returned = lax.all_to_all(totals, shard_axes, split_axis=0, concat_axis=0, tiled=True)
    return jnp.log(1.0 + returned[slots])


def up(value, multiple):
    return -(-value // multiple) * multiple


def room(count, parts, sigmas):
    mean = count / parts
    return math.ceil(mean + sigmas * (mean * (1 - 1 / parts)) ** 0.5)


def iota(shape, axis):
    return lax.broadcasted_iota(jnp.int32, shape, axis)


def exact_dot(left, right):
    return jnp.dot(
        left, right, precision=lax.Precision.HIGHEST, preferred_element_type=jnp.float32
    )


def pick_rows(places, start, count, rows):
    pick = jnp.where(iota((count, places.shape[1]), 0) + start == places, 1.0, 0.0)
    return jnp.dot(pick.astype(jnp.bfloat16), rows, preferred_element_type=jnp.float32).astype(
        jnp.bfloat16
    )


def plan_kernel(size, emb_ref, ids_ref, pool_ref, aug_ref, place_ref, rank_ref):
    rows, width = emb_ref.shape
    chips, labels, cap, pool = size["chips"], size["labels"], size["cap"], size["pool"]
    across, tiles = size["across"], size["tiles"]
    chunk = 256
    for start in range(0, rows, chunk):
        x = emb_ref[start : start + chunk, :]
        energy = jnp.sum(x * x, axis=1, keepdims=True)
        aug_ref[start : start + chunk, :] = (x * lax.rsqrt(energy + epsilon)).astype(jnp.bfloat16)

    ids = ids_ref[...]
    label = ids >> (chips.bit_length() - 1)
    shift = ((ids & (tiles - 1)) - lax.axis_index("tile")) & (tiles - 1)
    side = ((ids & (chips - 1)) >> (tiles.bit_length() - 1)) ^ lax.axis_index("chip")
    block = shift * across + side
    in_block = jnp.where(iota((LANES, rows), 0) == block, 1.0, 0.0).astype(jnp.bfloat16)
    in_label = jnp.where(iota((LANES, rows), 0) == label, 1.0, 0.0).astype(jnp.bfloat16)
    counts = lax.dot_general(
        in_block, in_label, (((1,), (1,)), ((), ())), preferred_element_type=jnp.float32
    )
    of_block = jnp.broadcast_to(jnp.sum(counts, axis=1, keepdims=True), (LANES, LANES))
    lower = jnp.where(iota((LANES, LANES), 1) < iota((LANES, LANES), 0), 1.0, 0.0)
    starts = exact_dot(lower, of_block)[0:chips, 0:1]

    def start_of(block):
        mine = iota((chips, rows), 0) == block
        return jnp.sum(jnp.where(mine, starts, 0.0), axis=0, keepdims=True)

    key = ((block * labels + label) * rows + iota((1, rows), 1)).astype(jnp.float32)
    key_t = jnp.broadcast_to(key, (LANES, rows)).T
    order = []
    for start in range(0, rows, LANES):
        smaller = jnp.where(key_t < key[:, start : start + LANES], 1.0, 0.0)
        order.append(jnp.sum(smaller, axis=0, keepdims=True))
    order = jnp.concatenate(order, axis=1)
    rank = order - start_of(block)
    pooled = order - start_of(shift * across)
    rank_ref[...] = rank

    def apart(shift):
        return shift != size["first"]

    full = (rank >= cap - 1) | (~apart(shift) & (pooled >= pool - across))
    over = jnp.max(jnp.where(full, 1.0, 0.0), axis=1, keepdims=True)
    place = jnp.where(apart(shift), side * cap + rank.astype(jnp.int32), pooled.astype(jnp.int32))
    place = jnp.where(full, -1, place)

    counts = jnp.where(iota((LANES, LANES), 1) == FLAG, over, counts)
    aug_ref[rows:, :] = jnp.zeros((LANES, width), jnp.bfloat16)
    aug_ref[rows:, 0:LANES] = counts.astype(jnp.bfloat16)
    lane = iota((1, LANES), 1)
    head_shift = jnp.where(lane < chips, lane >> (across.bit_length() - 1), -1)
    head_side = lane & (across - 1)
    head = jnp.where(
        apart(head_shift), head_side * cap + cap - 1, pool - across + head_side
    )
    shift = jnp.concatenate([shift, head_shift], axis=1)
    place = jnp.concatenate([place, head], axis=1)
    place = jnp.where(place >= 0, shift * PLACES + place, -1)
    place_ref[...] = place
    pool_ref[...] = pick_rows(place, size["first"] * PLACES, pool, aug_ref[...])


def pack_kernel(starts, aug_ref, place_ref, *out_refs):
    aug = aug_ref[...]
    place = place_ref[...]
    for start, out_ref in zip(starts, out_refs):
        out_ref[...] = pick_rows(place, start, out_ref.shape[0], aug)


def regroup_kernel(size, pool_ref, *out_refs):
    across, cap, pool, labels = size["across"], size["cap"], size["pool"], size["labels"]
    rows = pool_ref[...]
    heads = rows[pool - 16 :, 0:LANES].astype(jnp.float32)
    heads = jnp.where(iota((16, LANES), 1) < labels, heads, 0.0)
    counts = jnp.sum(heads, axis=1, keepdims=True).astype(jnp.int32)
    spot = iota((1, pool), 1)
    place = jnp.full((1, pool), -1, jnp.int32)
    begin = jnp.zeros((1, 1), jnp.int32)
    for side in range(across):
        end = begin + counts[16 - across + side : 17 - across + side, :]
        place = jnp.where((spot >= begin) & (spot < end), spot - begin + side * cap, place)
        begin = end
    place = jnp.where(spot >= pool - across, (spot - (pool - across) + 1) * cap - 1, place)
    for side, out_ref in enumerate(out_refs):
        out_ref[...] = pick_rows(place, side * cap, cap, rows)


def sort_kernel(size, *refs):
    across, labels, cap, space = size["across"], size["labels"], size["cap"], size["space"]
    block_refs, (out_ref, place_ref, rows_ref) = refs[:across], refs[across:]
    held = up(cap, ALIGN)
    total = across * held
    for index, ref in enumerate(block_refs):
        if held > cap:
            start = (index + 1) * held - ALIGN
            rows_ref[start : start + ALIGN, :] = jnp.zeros((ALIGN, ref.shape[1]), jnp.bfloat16)
        rows_ref[index * held : index * held + cap, :] = ref[...]
    rows = rows_ref[...]
    spot = iota((LANES, total), 1)
    block = iota((LANES, total), 0)
    head = jnp.where(spot == block * held + cap - 1, 1.0, 0.0).astype(jnp.bfloat16)
    counts = jnp.dot(head, rows[:, 0:LANES], preferred_element_type=jnp.float32)
    flag = jnp.max(counts[:, FLAG:], axis=0, keepdims=True)

    counts_t = counts.T
    lower = jnp.where(iota((LANES, LANES), 0) < iota((LANES, LANES), 1), 1.0, 0.0)
    ahead = exact_dot(counts_t, lower)
    in_block = jnp.zeros((1, LANES), jnp.float32)
    found = jnp.zeros((1, LANES), jnp.float32)
    begin = jnp.zeros((1, 1), jnp.float32)
    lane = iota((1, LANES), 1)
    table = []
    for label in range(labels):
        own = counts_t[label : label + 1, :]
        table.append(begin + ahead[label : label + 1, :] - in_block)
        in_block = in_block + own
        table.append(in_block)
        count = jnp.sum(own, axis=1, keepdims=True)
        high = jnp.floor(count * (1.0 / LANES))
        found = jnp.where(lane == label, high, found)
        found = jnp.where(lane == LOW + label, count - high * LANES, found)
        begin = begin + jnp.floor((count + (ALIGN - 1)) * (1.0 / ALIGN)) * ALIGN
    flag = jnp.maximum(flag, jnp.where(begin > space, 1.0, 0.0))
    found = jnp.where(lane == FLAG, flag, found)
    table.append((lane * held).astype(jnp.float32))
    table.extend([jnp.zeros((1, LANES), jnp.float32)] * (up(len(table), 8) - len(table)))
    table = jnp.concatenate(table, axis=0)

    def places(expand, rank_row):
        where = exact_dot(table, expand)
        rank = rank_row(where)
        place = jnp.full(rank.shape, -1.0, jnp.float32)
        for label in reversed(range(labels)):
            inside = rank < where[2 * label + 1 : 2 * label + 2, :]
            place = jnp.where(inside, where[2 * label : 2 * label + 1, :] + rank, place)
        return place.astype(jnp.int32)

    spot_block = jnp.where((spot >= block * held) & (spot < block * held + cap), 1.0, 0.0)
    spot_row = iota((1, total), 1).astype(jnp.float32)
    place = places(spot_block, lambda where: spot_row - where[2 * labels : 2 * labels + 1, :])
    lanes = place_ref.shape[1]
    rank_row = iota((1, lanes), 1).astype(jnp.float32)
    for index in range(across):
        only = jnp.where(iota((LANES, lanes), 0) == index, 1.0, 0.0)
        place_ref[index : index + 1, :] = places(only, lambda where: rank_row)

    out_ref[space:, :] = jnp.zeros((STEP, out_ref.shape[1]), jnp.bfloat16)
    out_ref[space : space + ALIGN, 0:LANES] = jnp.broadcast_to(found, (ALIGN, LANES)).astype(
        jnp.bfloat16
    )
    for start in range(0, space, ALIGN * 9):
        count = min(ALIGN * 9, space - start)
        out_ref[start : start + count, :] = pick_rows(place, start, count, rows)


def score_kernel(size, *refs):
    across, tiles, labels, space = size["across"], size["tiles"], size["labels"], size["space"]
    pieces = 2 * tiles
    piece_refs, place_refs = refs[:pieces], refs[pieces : pieces + tiles]
    out_ref, rows_ref, total_ref, back_ref, heads_ref, counts_ref, sem = refs[pieces + tiles :]
    lane = iota((1, LANES), 1)
    heads = [ref[space : space + ALIGN, 0:LANES].astype(jnp.float32)[0:1, :] for ref in piece_refs]
    heads_ref[...] = jnp.concatenate(heads, axis=0).astype(jnp.int32)
    copy = pltpu.make_async_copy(heads_ref, counts_ref, sem)
    copy.start()
    copy.wait()
    flag = jnp.int32(0)
    for index in range(pieces):
        flag = jnp.maximum(flag, counts_ref[index, FLAG])

    def aligned(count):
        return (count + (ALIGN - 1)) & -ALIGN

    runs, ends = [], []
    begin = jnp.int32(0)
    source = [jnp.int32(0)] * pieces
    many = jnp.bool_(False)
    for label in range(labels):
        runs.append([])
        for index in range(pieces):
            count = counts_ref[index, label] * LANES + counts_ref[index, LOW + label]
            count = jnp.clip(count, 0, space - source[index])
            runs[label].append((source[index], begin, count))
            many = many | (count > STEP)
            source[index] = source[index] + aligned(count)
            begin = begin + aligned(count)
        ends.append(begin)

    def span(start, step, size):
        return pl.ds(pl.multiple_of(start + step * size, ALIGN), size)

    def gather(index, src, dst, step):
        rows_ref[span(dst, step, STEP), :] = piece_refs[index][span(src, step, STEP), :]

    def repeat(first, end, act):
        def once(step, carry):
            act(step)
            return carry

        lax.fori_loop(first, end, once, 0)

    def cover(count, size):
        return (count + size - 1) // size

    for label in range(labels):
        for index, (src, dst, count) in enumerate(runs[label]):
            gather(index, src, dst, 0)

    @pl.when(many)
    def _():
        for label in range(labels):
            for index, (src, dst, count) in enumerate(runs[label]):
                repeat(0, cover(count, STEP), functools.partial(gather, index, src, dst))

    def window(label, row, column):
        left = rows_ref[span(row, 0, LEFT), :]
        right = rows_ref[span(column, 0, RIGHT), :]
        scores = lax.dot_general(
            left, right, (((1,), (1,)), ((), ())), preferred_element_type=jnp.float32
        )
        at = iota((1, RIGHT), 1) + column
        valid = at < 0
        for _, low, count in runs[label]:
            valid = valid | ((at >= low) & (at < low + count))
        at = jnp.where(valid, at, -1)
        itself = iota((LEFT, RIGHT), 0) + row
        counted = (at >= 0) & (at != itself)
        terms = jnp.where(counted, jnp.exp(sharpness * scores), 0.0)
        sums = jnp.sum(terms, axis=1, keepdims=True)
        return jnp.broadcast_to(sums, (LEFT, LANES))

    wide = jnp.bool_(False)
    for label in range(labels):
        first, own_end = runs[label][0][1], runs[label][tiles][1]
        total_ref[label, 0:LEFT, :] = window(label, first, first)
        wide = wide | (own_end - first > LEFT) | (ends[label] - first > RIGHT)

    @pl.when(wide)
    def _():
        for label in range(labels):
            first, own_end = runs[label][0][1], runs[label][tiles][1]
            across_steps = cover(ends[label] - first, RIGHT)

            def add(strip, step, label=label, first=first):
                row, column = first + strip * LEFT, first + step * RIGHT
                total_ref[label, span(0, strip, LEFT), :] += window(label, row, column)

            def strips(strip, label=label, add=add, across_steps=across_steps):
                total_ref[label, span(0, strip, LEFT), :] = jnp.zeros((LEFT, LANES), jnp.float32)
                repeat(0, across_steps, functools.partial(add, strip))

            repeat(1, across_steps, functools.partial(add, 0))
            repeat(1, cover(own_end - first, LEFT), strips)

    def scatter(label, index, step):
        src, dst, _ = runs[label][index]
        back_ref[index, span(src, step, STEP), :] = total_ref[
            label, span(dst - runs[label][0][1], step, STEP), :
        ]

    for index in range(tiles):
        for label in range(labels):
            scatter(label, index, 0)

    @pl.when(many)
    def _():
        for index in range(tiles):
            for label in range(labels):
                count = runs[label][index][2]
                repeat(0, cover(count, STEP), functools.partial(scatter, label, index))

    lanes = out_ref.shape[1]
    row = iota((space, LANES), 0)
    chip, tile = lax.axis_index("chip"), lax.axis_index("tile")
    for shift in range(tiles):
        for side in range(across):
            home = (chip ^ side) * tiles + ((tile - shift) & (tiles - 1))
            for start in range(0, lanes, LANES):
                place = place_refs[shift][side : side + 1, start : start + LANES]
                value = jnp.sum(
                    jnp.where(row == place, back_ref[shift, 0:space, :], 0.0),
                    axis=0,
                    keepdims=True,
                )
                if start + LANES == lanes:
                    value = jnp.where(lane == FLAG, flag.astype(jnp.float32), value)
                out_ref[pl.ds(home, 1), start : start + LANES] = value


def unpack_kernel(chips, ret_ref, ids_ref, rank_ref, out_ref, flag_ref):
    rows = ids_ref.shape[1]
    lanes = ret_ref.shape[1]
    values = ret_ref[...]
    flag = jnp.max(values[:, lanes - 1 :], axis=0, keepdims=True)
    flag_ref[0, 0] = jnp.sum(flag).astype(jnp.int32)
    chip = ids_ref[...] & (chips - 1)
    rank = rank_ref[...].astype(jnp.int32)
    at_rank = jnp.where(iota((lanes, rows), 0) == rank, 1.0, 0.0)
    found = exact_dot(values, at_rank)
    total = jnp.sum(jnp.where(iota((chips, rows), 0) == chip, found, 0.0), axis=0, keepdims=True)
    out_ref[...] = jnp.log(1.0 + total)


def call(kernel, name, out_shape, inputs, vmem_mib=12, **options):
    vmem = pl.BlockSpec(memory_space=pltpu.VMEM)
    return pl.pallas_call(
        kernel,
        out_shape=out_shape,
        in_specs=[vmem] * len(inputs),
        out_specs=options.pop("out_specs", jax.tree.map(lambda _: vmem, out_shape)),
        compiler_params=pltpu.CompilerParams(vmem_limit_bytes=vmem_mib * MIB),
        name=name,
        **options,
    )(*inputs)


def body(embeddings, cluster_ids):
    rows, width = embeddings.shape
    across, tiles = lax.axis_size("chip"), lax.axis_size("tile")
    chips = across * tiles
    labels = KG * across * lax.axis_size("core") // chips
    cap = up(room(rows, chips, 5.0) + 1, 8)
    pool = up(room(rows, tiles, 4.25) + across, ALIGN)
    space = up(room(rows, tiles, 4.75) + labels * (ALIGN - 4), ALIGN)
    order = sorted(range(1, tiles), key=lambda shift: (-min(shift, tiles - shift), shift))
    size = dict(
        chips=chips, across=across, tiles=tiles, labels=labels, cap=cap, pool=pool, space=space,
        first=order[0],
    )
    lanes = up(cap + 1, LANES)
    shape = jax.ShapeDtypeStruct

    ids_row = cluster_ids.reshape(1, rows)
    pool_rows, aug, slots, rank = call(
        functools.partial(plan_kernel, size),
        "plan",
        [
            shape((pool, width), jnp.bfloat16),
            shape((rows + LANES, width), jnp.bfloat16),
            shape((1, rows + LANES), jnp.int32),
            shape((1, rows), jnp.float32),
        ],
        [embeddings, ids_row],
    )

    near_and_far = [0, *order[1:]]
    blocks = call(
        functools.partial(
            pack_kernel,
            [shift * PLACES + side * cap for shift in near_and_far for side in range(across)],
        ),
        "pack",
        [shape((cap, width), jnp.bfloat16)] * (across * len(near_and_far)),
        [aug, slots],
    )
    packed = {
        shift: blocks[place * across : (place + 1) * across]
        for place, shift in enumerate(near_and_far)
    }

    def along(shift):
        return [(z, (z + shift) % tiles) for z in range(tiles)]

    def over(side):
        return [(a, a ^ side) for a in range(across)]

    def after(value, *others):
        return lax.optimization_barrier((value, others))[0]

    def send_across(blocks):
        return [blocks[0]] + [
            lax.ppermute(blocks[side], "chip", over(side)) for side in range(1, across)
        ]

    def send_far(blocks, shift, side):
        route = [(a * tiles + z, b * tiles + y) for a, b in over(side) for z, y in along(shift)]
        return lax.ppermute(blocks[side], ("chip", "tile"), route)

    swap = [(0, 1), (1, 0)]
    own, other, places = {}, {}, {}

    def finish(shift, arrived):
        own[shift], places[shift] = call(
            functools.partial(sort_kernel, size),
            "sort",
            [
                shape((space + STEP, width), jnp.bfloat16),
                shape((across, lanes), jnp.int32),
            ],
            arrived,
            scratch_shapes=[pltpu.VMEM((across * up(cap, ALIGN), width), jnp.bfloat16)],
        )
        other[shift] = lax.ppermute(own[shift], "core", swap)

    pooled = lax.ppermute(pool_rows, "tile", along(order[0]))
    near = send_across(packed[0])
    finish(0, near)
    blocks = [(shift, side) for shift in order[1:] for side in range(across)]
    beside = [(shift, across - 1) for shift in order[1:2]]
    arrived = {
        (shift, side): send_far(packed[shift], shift, side) for shift, side in beside
    }
    regrouped = call(
        functools.partial(regroup_kernel, size),
        "regroup",
        [shape((cap, width), jnp.bfloat16)] * across,
        [after(pooled, *near, *arrived.values())],
    )
    passed = send_across(regrouped)
    finish(order[0], passed)
    for shift, side in sorted(set(blocks) - set(beside), key=lambda block: (block[1] > 0, block)):
        ready = after(packed[shift], pooled if side == 0 else pooled)
        arrived[shift, side] = send_far(ready, shift, side)
    for shift in order[1:]:
        finish(shift, [arrived[shift, side] for side in range(across)])
    own, other, places = (
        [found[shift] for shift in range(tiles)] for found in (own, other, places)
    )
    room_own = tiles * space + LEFT + STEP
    totals = call(
        functools.partial(score_kernel, size),
        "score",
        shape((chips, lanes), jnp.float32),
        [*own, *other, *places],
        vmem_mib=26,
        scratch_shapes=[
            pltpu.VMEM((2 * tiles * space + LEFT + RIGHT, width), jnp.bfloat16),
            pltpu.VMEM((labels, room_own, LANES), jnp.float32),
            pltpu.VMEM((tiles, space + STEP, LANES), jnp.float32),
            pltpu.VMEM((2 * tiles, LANES), jnp.int32),
            pltpu.SMEM((2 * tiles, LANES), jnp.int32),
            pltpu.SemaphoreType.DMA,
        ],
    )
    returned = lax.all_to_all(totals, ("chip", "tile"), split_axis=0, concat_axis=0, tiled=True)
    result, flag = call(
        functools.partial(unpack_kernel, chips),
        "unpack",
        [shape((1, rows), jnp.float32), shape((1, 1), jnp.int32)],
        [returned, ids_row, rank],
        out_specs=[
            pl.BlockSpec(memory_space=pltpu.VMEM),
            pl.BlockSpec(memory_space=pltpu.SMEM),
        ],
    )
    return lax.cond(
        flag.reshape(()) > 0,
        lambda: general_plan(embeddings, cluster_ids),
        lambda: result.reshape(rows),
    )


def solution(mesh):
    shards = mesh.shape["shard"]
    tiles = mesh.shape["tile"]
    split = Mesh(mesh.devices.reshape(shards // 2, 2, tiles), ("chip", "core", "tile"))
    rows = ("chip", "core", "tile")
    return jax.shard_map(
        body, mesh=split, in_specs=(P(rows, None), P(rows)), out_specs=P(rows), check_vma=False
    )
```

```python
import functools
import math

import jax
import jax.numpy as jnp
from jax import lax
from jax.experimental import pallas as pl
from jax.experimental.pallas import tpu as pltpu
from jax.sharding import Mesh
from jax.sharding import PartitionSpec as P

KG = 16


sharpness = 30.0
epsilon = 1e-06

MIB = 1024 * 1024
LANES = 128
FLAG = LANES - 1
LOW = LANES // 2
ALIGN = 16
STEP = 96
LEFT = 256
RIGHT = 512
PLACES = 1 << 16


def unit_rows(embeddings):
    energy = jnp.sum(embeddings * embeddings, axis=1, keepdims=True)
    return (embeddings * lax.rsqrt(energy + epsilon)).astype(jnp.bfloat16)


def row_sums(left, left_labels, right, right_labels, same_rows):
    count = left.shape[0]
    block = min(512, count)
    blocks = count // block

    def step(start, items):
        rows_block, labels_block = items
        scores = lax.dot_general(
            rows_block, right, (((1,), (1,)), ((), ())), preferred_element_type=jnp.float32
        )
        same = (labels_block[:, None] == right_labels[None, :]) & (labels_block[:, None] >= 0)
        itself = (start + jnp.arange(block))[:, None] == jnp.arange(count)[None, :]
        same = same & ~(itself & same_rows)
        terms = jnp.where(same, jnp.exp(sharpness * scores), 0.0)
        return (start + block, jnp.sum(terms, axis=1))

    _, totals = lax.scan(
        step,
        jnp.int32(0),
        (left.reshape(blocks, block, left.shape[1]), left_labels.reshape(blocks, block)),
    )
    return totals.reshape(count)


def general_plan(embeddings, cluster_ids):
    shard_axes = ("chip", "core")
    local_rows = embeddings.shape[0]
    shards = lax.axis_size("chip") * lax.axis_size("core")
    tiles = lax.axis_size("tile")
    capacity = 2 * local_rows // shards
    slot_count = shards * capacity
    unit = unit_rows(embeddings)
    owner = cluster_ids // KG
    onehot = (owner[:, None] == jnp.arange(shards, dtype=jnp.int32)[None, :]).astype(jnp.int32)
    ranks = jnp.sum((jnp.cumsum(onehot, axis=0) - 1) * onehot, axis=1)
    slots = owner * capacity + ranks
    outgoing = jnp.zeros((slot_count, unit.shape[1]), jnp.bfloat16).at[slots].set(unit)
    outgoing_labels = jnp.full((slot_count,), -1, jnp.int32).at[slots].set(cluster_ids)
    owned = lax.all_to_all(outgoing, shard_axes, split_axis=0, concat_axis=0, tiled=True)
    owned_labels = lax.all_to_all(
        outgoing_labels, shard_axes, split_axis=0, concat_axis=0, tiled=True
    )
    around = [(tile, (tile + 1) % tiles) for tile in range(tiles)]

    def visit(step, state):
        totals, rows, labels = state
        totals = totals + row_sums(owned, owned_labels, rows, labels, step == 0)
        return (totals, lax.ppermute(rows, "tile", around), lax.ppermute(labels, "tile", around))

    totals, _, _ = lax.fori_loop(
        0, tiles, visit, (jnp.zeros((slot_count,), jnp.float32), owned, owned_labels)
    )
    returned = lax.all_to_all(totals, shard_axes, split_axis=0, concat_axis=0, tiled=True)
    return jnp.log(1.0 + returned[slots])


def up(value, multiple):
    return -(-value // multiple) * multiple


def room(count, parts, sigmas):
    mean = count / parts
    return math.ceil(mean + sigmas * (mean * (1 - 1 / parts)) ** 0.5)


def iota(shape, axis):
    return lax.broadcasted_iota(jnp.int32, shape, axis)


def exact_dot(left, right):
    return jnp.dot(
        left, right, precision=lax.Precision.HIGHEST, preferred_element_type=jnp.float32
    )


def pick_rows(places, start, count, rows):
    pick = jnp.where(iota((count, places.shape[1]), 0) + start == places, 1.0, 0.0)
    return jnp.dot(pick.astype(jnp.bfloat16), rows, preferred_element_type=jnp.float32).astype(
        jnp.bfloat16
    )


def plan_kernel(size, emb_ref, ids_ref, pool_ref, aug_ref, place_ref, rank_ref):
    rows, width = emb_ref.shape
    chips, labels, cap, pool = size["chips"], size["labels"], size["cap"], size["pool"]
    across, tiles = size["across"], size["tiles"]
    chunk = 256
    for start in range(0, rows, chunk):
        x = emb_ref[start : start + chunk, :]
        energy = jnp.sum(x * x, axis=1, keepdims=True)
        aug_ref[start : start + chunk, :] = (x * lax.rsqrt(energy + epsilon)).astype(jnp.bfloat16)

    ids = ids_ref[...]
    label = ids >> (chips.bit_length() - 1)
    shift = ((ids & (tiles - 1)) - lax.axis_index("tile")) & (tiles - 1)
    side = ((ids & (chips - 1)) >> (tiles.bit_length() - 1)) ^ lax.axis_index("chip")
    block = shift * across + side
    in_block = jnp.where(iota((LANES, rows), 0) == block, 1.0, 0.0).astype(jnp.bfloat16)
    in_label = jnp.where(iota((LANES, rows), 0) == label, 1.0, 0.0).astype(jnp.bfloat16)
    counts = lax.dot_general(
        in_block, in_label, (((1,), (1,)), ((), ())), preferred_element_type=jnp.float32
    )
    of_block = jnp.broadcast_to(jnp.sum(counts, axis=1, keepdims=True), (LANES, LANES))
    lower = jnp.where(iota((LANES, LANES), 1) < iota((LANES, LANES), 0), 1.0, 0.0)
    starts = exact_dot(lower, of_block)[0:chips, 0:1]

    def start_of(block):
        mine = iota((chips, rows), 0) == block
        return jnp.sum(jnp.where(mine, starts, 0.0), axis=0, keepdims=True)

    key = ((block * labels + label) * rows + iota((1, rows), 1)).astype(jnp.float32)
    key_t = jnp.broadcast_to(key, (LANES, rows)).T
    order = []
    for start in range(0, rows, LANES):
        smaller = jnp.where(key_t < key[:, start : start + LANES], 1.0, 0.0)
        order.append(jnp.sum(smaller, axis=0, keepdims=True))
    order = jnp.concatenate(order, axis=1)
    rank = order - start_of(block)
    pooled = order - start_of(shift * across)
    rank_ref[...] = rank

    def apart(shift):
        return shift != size["first"]

    full = (rank >= cap - 1) | (~apart(shift) & (pooled >= pool - across))
    over = jnp.max(jnp.where(full, 1.0, 0.0), axis=1, keepdims=True)
    place = jnp.where(apart(shift), side * cap + rank.astype(jnp.int32), pooled.astype(jnp.int32))
    place = jnp.where(full, -1, place)

    counts = jnp.where(iota((LANES, LANES), 1) == FLAG, over, counts)
    aug_ref[rows:, :] = jnp.zeros((LANES, width), jnp.bfloat16)
    aug_ref[rows:, 0:LANES] = counts.astype(jnp.bfloat16)
    lane = iota((1, LANES), 1)
    head_shift = jnp.where(lane < chips, lane >> (across.bit_length() - 1), -1)
    head_side = lane & (across - 1)
    head = jnp.where(
        apart(head_shift), head_side * cap + cap - 1, pool - across + head_side
    )
    shift = jnp.concatenate([shift, head_shift], axis=1)
    place = jnp.concatenate([place, head], axis=1)
    place = jnp.where(place >= 0, shift * PLACES + place, -1)
    place_ref[...] = place
    pool_ref[...] = pick_rows(place, size["first"] * PLACES, pool, aug_ref[...])


def pack_kernel(starts, aug_ref, place_ref, *out_refs):
    aug = aug_ref[...]
    place = place_ref[...]
    for start, out_ref in zip(starts, out_refs):
        out_ref[...] = pick_rows(place, start, out_ref.shape[0], aug)


def regroup_kernel(size, pool_ref, *out_refs):
    across, cap, pool, labels = size["across"], size["cap"], size["pool"], size["labels"]
    rows = pool_ref[...]
    heads = rows[pool - 16 :, 0:LANES].astype(jnp.float32)
    heads = jnp.where(iota((16, LANES), 1) < labels, heads, 0.0)
    counts = jnp.sum(heads, axis=1, keepdims=True).astype(jnp.int32)
    spot = iota((1, pool), 1)
    place = jnp.full((1, pool), -1, jnp.int32)
    begin = jnp.zeros((1, 1), jnp.int32)
    for side in range(across):
        end = begin + counts[16 - across + side : 17 - across + side, :]
        place = jnp.where((spot >= begin) & (spot < end), spot - begin + side * cap, place)
        begin = end
    place = jnp.where(spot >= pool - across, (spot - (pool - across) + 1) * cap - 1, place)
    for side, out_ref in enumerate(out_refs):
        out_ref[...] = pick_rows(place, side * cap, cap, rows)


def sort_kernel(size, *refs):
    across, labels, cap, space = size["across"], size["labels"], size["cap"], size["space"]
    block_refs, (out_ref, place_ref, rows_ref) = refs[:across], refs[across:]
    held = up(cap, ALIGN)
    total = across * held
    for index, ref in enumerate(block_refs):
        if held > cap:
            start = (index + 1) * held - ALIGN
            rows_ref[start : start + ALIGN, :] = jnp.zeros((ALIGN, ref.shape[1]), jnp.bfloat16)
        rows_ref[index * held : index * held + cap, :] = ref[...]
    rows = rows_ref[...]
    spot = iota((LANES, total), 1)
    block = iota((LANES, total), 0)
    head = jnp.where(spot == block * held + cap - 1, 1.0, 0.0).astype(jnp.bfloat16)
    counts = jnp.dot(head, rows[:, 0:LANES], preferred_element_type=jnp.float32)
    flag = jnp.max(counts[:, FLAG:], axis=0, keepdims=True)

    counts_t = counts.T
    lower = jnp.where(iota((LANES, LANES), 0) < iota((LANES, LANES), 1), 1.0, 0.0)
    ahead = exact_dot(counts_t, lower)
    in_block = jnp.zeros((1, LANES), jnp.float32)
    found = jnp.zeros((1, LANES), jnp.float32)
    begin = jnp.zeros((1, 1), jnp.float32)
    lane = iota((1, LANES), 1)
    table = []
    for label in range(labels):
        own = counts_t[label : label + 1, :]
        table.append(begin + ahead[label : label + 1, :] - in_block)
        in_block = in_block + own
        table.append(in_block)
        count = jnp.sum(own, axis=1, keepdims=True)
        high = jnp.floor(count * (1.0 / LANES))
        found = jnp.where(lane == label, high, found)
        found = jnp.where(lane == LOW + label, count - high * LANES, found)
        begin = begin + jnp.floor((count + (ALIGN - 1)) * (1.0 / ALIGN)) * ALIGN
    flag = jnp.maximum(flag, jnp.where(begin > space, 1.0, 0.0))
    found = jnp.where(lane == FLAG, flag, found)
    table.append((lane * held).astype(jnp.float32))
    table.extend([jnp.zeros((1, LANES), jnp.float32)] * (up(len(table), 8) - len(table)))
    table = jnp.concatenate(table, axis=0)

    def places(where, rank):
        place = jnp.full(rank.shape, -1.0, jnp.float32)
        for label in reversed(range(labels)):
            inside = rank < where[2 * label + 1 : 2 * label + 2, :]
            place = jnp.where(inside, where[2 * label : 2 * label + 1, :] + rank, place)
        return place.astype(jnp.int32)

    spot_block = jnp.where((spot >= block * held) & (spot < block * held + cap), 1.0, 0.0)
    spot_row = iota((1, total), 1).astype(jnp.float32)
    where = exact_dot(table, spot_block)
    place = places(where, spot_row - where[2 * labels : 2 * labels + 1, :])
    lanes = place_ref.shape[1]
    rank_row = iota((1, lanes), 1).astype(jnp.float32)
    for index in range(across):
        place_ref[index : index + 1, :] = places(table[:, index : index + 1], rank_row)

    out_ref[space:, :] = jnp.zeros((STEP, out_ref.shape[1]), jnp.bfloat16)
    out_ref[space : space + ALIGN, 0:LANES] = jnp.broadcast_to(found, (ALIGN, LANES)).astype(
        jnp.bfloat16
    )
    for start in range(0, space, ALIGN * 9):
        count = min(ALIGN * 9, space - start)
        out_ref[start : start + count, :] = pick_rows(place, start, count, rows)


def score_kernel(size, *refs):
    across, tiles, labels, space = size["across"], size["tiles"], size["labels"], size["space"]
    pieces = 2 * tiles
    piece_refs, place_refs = refs[:pieces], refs[pieces : pieces + tiles]
    out_ref, rows_ref, total_ref, back_ref, heads_ref, counts_ref, sem = refs[pieces + tiles :]
    lane = iota((1, LANES), 1)
    heads = [ref[space : space + ALIGN, 0:LANES].astype(jnp.float32)[0:1, :] for ref in piece_refs]
    heads_ref[...] = jnp.concatenate(heads, axis=0).astype(jnp.int32)
    copy = pltpu.make_async_copy(heads_ref, counts_ref, sem)
    copy.start()
    copy.wait()
    flag = jnp.int32(0)
    for index in range(pieces):
        flag = jnp.maximum(flag, counts_ref[index, FLAG])

    def aligned(count):
        return (count + (ALIGN - 1)) & -ALIGN

    runs, ends = [], []
    begin = jnp.int32(0)
    source = [jnp.int32(0)] * pieces
    many = jnp.bool_(False)
    for label in range(labels):
        runs.append([])
        for index in range(pieces):
            count = counts_ref[index, label] * LANES + counts_ref[index, LOW + label]
            count = jnp.clip(count, 0, space - source[index])
            runs[label].append((source[index], begin, count))
            many = many | (count > STEP)
            source[index] = source[index] + aligned(count)
            begin = begin + aligned(count)
        ends.append(begin)

    def span(start, step, size):
        return pl.ds(pl.multiple_of(start + step * size, ALIGN), size)

    def gather(index, src, dst, step):
        rows_ref[span(dst, step, STEP), :] = piece_refs[index][span(src, step, STEP), :]

    def repeat(first, end, act):
        def once(step, carry):
            act(step)
            return carry

        lax.fori_loop(first, end, once, 0)

    def cover(count, size):
        return (count + size - 1) // size

    for label in range(labels):
        for index, (src, dst, count) in enumerate(runs[label]):
            gather(index, src, dst, 0)

    @pl.when(many)
    def _():
        for label in range(labels):
            for index, (src, dst, count) in enumerate(runs[label]):
                repeat(0, cover(count, STEP), functools.partial(gather, index, src, dst))

    def window(label, row, column):
        left = rows_ref[span(row, 0, LEFT), :]
        right = rows_ref[span(column, 0, RIGHT), :]
        scores = lax.dot_general(
            left, right, (((1,), (1,)), ((), ())), preferred_element_type=jnp.float32
        )
        at = iota((1, RIGHT), 1) + column
        valid = at < 0
        for _, low, count in runs[label]:
            valid = valid | ((at >= low) & (at < low + count))
        at = jnp.where(valid, at, -1)
        itself = iota((LEFT, RIGHT), 0) + row
        counted = (at >= 0) & (at != itself)
        terms = jnp.where(counted, jnp.exp(sharpness * scores), 0.0)
        sums = jnp.sum(terms, axis=1, keepdims=True)
        return jnp.broadcast_to(sums, (LEFT, LANES))

    wide = jnp.bool_(False)
    for label in range(labels):
        first, own_end = runs[label][0][1], runs[label][tiles][1]
        total_ref[label, 0:LEFT, :] = window(label, first, first)
        wide = wide | (own_end - first > LEFT) | (ends[label] - first > RIGHT)

    @pl.when(wide)
    def _():
        for label in range(labels):
            first, own_end = runs[label][0][1], runs[label][tiles][1]
            across_steps = cover(ends[label] - first, RIGHT)

            def add(strip, step, label=label, first=first):
                row, column = first + strip * LEFT, first + step * RIGHT
                total_ref[label, span(0, strip, LEFT), :] += window(label, row, column)

            def strips(strip, label=label, add=add, across_steps=across_steps):
                total_ref[label, span(0, strip, LEFT), :] = jnp.zeros((LEFT, LANES), jnp.float32)
                repeat(0, across_steps, functools.partial(add, strip))

            repeat(1, across_steps, functools.partial(add, 0))
            repeat(1, cover(own_end - first, LEFT), strips)

    def scatter(label, index, step):
        src, dst, _ = runs[label][index]
        back_ref[index, span(src, step, STEP), :] = total_ref[
            label, span(dst - runs[label][0][1], step, STEP), :
        ]

    for index in range(tiles):
        for label in range(labels):
            scatter(label, index, 0)

    @pl.when(many)
    def _():
        for index in range(tiles):
            for label in range(labels):
                count = runs[label][index][2]
                repeat(0, cover(count, STEP), functools.partial(scatter, label, index))

    lanes = out_ref.shape[1]
    row = iota((space, LANES), 0)
    chip, tile = lax.axis_index("chip"), lax.axis_index("tile")
    for shift in range(tiles):
        for side in range(across):
            home = (chip ^ side) * tiles + ((tile - shift) & (tiles - 1))
            for start in range(0, lanes, LANES):
                place = place_refs[shift][side : side + 1, start : start + LANES]
                value = jnp.sum(
                    jnp.where(row == place, back_ref[shift, 0:space, :], 0.0),
                    axis=0,
                    keepdims=True,
                )
                if start + LANES == lanes:
                    value = jnp.where(lane == FLAG, flag.astype(jnp.float32), value)
                out_ref[pl.ds(home, 1), start : start + LANES] = value


def unpack_kernel(chips, ret_ref, ids_ref, rank_ref, out_ref, flag_ref):
    rows = ids_ref.shape[1]
    lanes = ret_ref.shape[1]
    values = ret_ref[...]
    flag = jnp.max(values[:, lanes - 1 :], axis=0, keepdims=True)
    flag_ref[0, 0] = jnp.sum(flag).astype(jnp.int32)
    chip = ids_ref[...] & (chips - 1)
    rank = rank_ref[...].astype(jnp.int32)
    at_rank = jnp.where(iota((lanes, rows), 0) == rank, 1.0, 0.0)
    found = exact_dot(values, at_rank)
    total = jnp.sum(jnp.where(iota((chips, rows), 0) == chip, found, 0.0), axis=0, keepdims=True)
    out_ref[...] = jnp.log(1.0 + total)


def call(kernel, name, out_shape, inputs, vmem_mib=12, **options):
    vmem = pl.BlockSpec(memory_space=pltpu.VMEM)
    return pl.pallas_call(
        kernel,
        out_shape=out_shape,
        in_specs=[vmem] * len(inputs),
        out_specs=options.pop("out_specs", jax.tree.map(lambda _: vmem, out_shape)),
        compiler_params=pltpu.CompilerParams(vmem_limit_bytes=vmem_mib * MIB),
        name=name,
        **options,
    )(*inputs)


def body(embeddings, cluster_ids):
    rows, width = embeddings.shape
    across, tiles = lax.axis_size("chip"), lax.axis_size("tile")
    chips = across * tiles
    labels = KG * across * lax.axis_size("core") // chips
    cap = up(room(rows, chips, 5.0) + 1, 8)
    pool = up(room(rows, tiles, 4.25) + across, ALIGN)
    space = up(room(rows, tiles, 4.75) + labels * (ALIGN - 4), ALIGN)
    order = sorted(range(1, tiles), key=lambda shift: (-min(shift, tiles - shift), shift))
    size = dict(
        chips=chips, across=across, tiles=tiles, labels=labels, cap=cap, pool=pool, space=space,
        first=order[0],
    )
    lanes = up(cap + 1, LANES)
    shape = jax.ShapeDtypeStruct

    ids_row = cluster_ids.reshape(1, rows)
    pool_rows, aug, slots, rank = call(
        functools.partial(plan_kernel, size),
        "plan",
        [
            shape((pool, width), jnp.bfloat16),
            shape((rows + LANES, width), jnp.bfloat16),
            shape((1, rows + LANES), jnp.int32),
            shape((1, rows), jnp.float32),
        ],
        [embeddings, ids_row],
    )

    near_and_far = [0, *order[1:]]
    blocks = call(
        functools.partial(
            pack_kernel,
            [shift * PLACES + side * cap for shift in near_and_far for side in range(across)],
        ),
        "pack",
        [shape((cap, width), jnp.bfloat16)] * (across * len(near_and_far)),
        [aug, slots],
    )
    packed = {
        shift: blocks[place * across : (place + 1) * across]
        for place, shift in enumerate(near_and_far)
    }

    def along(shift):
        return [(z, (z + shift) % tiles) for z in range(tiles)]

    def over(side):
        return [(a, a ^ side) for a in range(across)]

    def after(value, *others):
        return lax.optimization_barrier((value, others))[0]

    def send_across(blocks):
        return [blocks[0]] + [
            lax.ppermute(blocks[side], "chip", over(side)) for side in range(1, across)
        ]

    def send_far(blocks, shift, side):
        route = [(a * tiles + z, b * tiles + y) for a, b in over(side) for z, y in along(shift)]
        return lax.ppermute(blocks[side], ("chip", "tile"), route)

    swap = [(0, 1), (1, 0)]
    own, other, places = {}, {}, {}

    def finish(shift, arrived):
        own[shift], places[shift] = call(
            functools.partial(sort_kernel, size),
            "sort",
            [
                shape((space + STEP, width), jnp.bfloat16),
                shape((across, lanes), jnp.int32),
            ],
            arrived,
            scratch_shapes=[pltpu.VMEM((across * up(cap, ALIGN), width), jnp.bfloat16)],
        )
        other[shift] = lax.ppermute(own[shift], "core", swap)

    pooled = lax.ppermute(pool_rows, "tile", along(order[0]))
    near = send_across(packed[0])
    finish(0, near)
    blocks = [(shift, side) for shift in order[1:] for side in range(across)]
    beside = [(shift, across - 1) for shift in order[1:2]]
    arrived = {
        (shift, side): send_far(packed[shift], shift, side) for shift, side in beside
    }
    regrouped = call(
        functools.partial(regroup_kernel, size),
        "regroup",
        [shape((cap, width), jnp.bfloat16)] * across,
        [after(pooled, *near, *arrived.values())],
    )
    passed = send_across(regrouped)
    finish(order[0], passed)
    for shift, side in sorted(set(blocks) - set(beside), key=lambda block: (block[1] > 0, block)):
        ready = after(packed[shift], pooled if side == 0 else pooled)
        arrived[shift, side] = send_far(ready, shift, side)
    for shift in order[1:]:
        finish(shift, [arrived[shift, side] for side in range(across)])
    own, other, places = (
        [found[shift] for shift in range(tiles)] for found in (own, other, places)
    )
    room_own = tiles * space + LEFT + STEP
    totals = call(
        functools.partial(score_kernel, size),
        "score",
        shape((chips, lanes), jnp.float32),
        [*own, *other, *places],
        vmem_mib=26,
        scratch_shapes=[
            pltpu.VMEM((2 * tiles * space + LEFT + RIGHT, width), jnp.bfloat16),
            pltpu.VMEM((labels, room_own, LANES), jnp.float32),
            pltpu.VMEM((tiles, space + STEP, LANES), jnp.float32),
            pltpu.VMEM((2 * tiles, LANES), jnp.int32),
            pltpu.SMEM((2 * tiles, LANES), jnp.int32),
            pltpu.SemaphoreType.DMA,
        ],
    )
    returned = lax.all_to_all(totals, ("chip", "tile"), split_axis=0, concat_axis=0, tiled=True)
    result, flag = call(
        functools.partial(unpack_kernel, chips),
        "unpack",
        [shape((1, rows), jnp.float32), shape((1, 1), jnp.int32)],
        [returned, ids_row, rank],
        out_specs=[
            pl.BlockSpec(memory_space=pltpu.VMEM),
            pl.BlockSpec(memory_space=pltpu.SMEM),
        ],
    )
    return lax.cond(
        flag.reshape(()) > 0,
        lambda: general_plan(embeddings, cluster_ids),
        lambda: result.reshape(rows),
    )


def solution(mesh):
    shards = mesh.shape["shard"]
    tiles = mesh.shape["tile"]
    split = Mesh(mesh.devices.reshape(shards // 2, 2, tiles), ("chip", "core", "tile"))
    rows = ("chip", "core", "tile")
    return jax.shard_map(
        body, mesh=split, in_specs=(P(rows, None), P(rows)), out_specs=P(rows), check_vma=False
    )
```
